32 devices in a mesh: dp: 8 (over z, x), section: 4 (over y, core).
Axes of the slice: x: 2, y: 2, z: 4, core: 2. Of those that a mesh axis runs over, the one named last changes fastest.
Arguments:
- inputs: bfloat16 [8192, 768], P(('dp', 'section')), may hold values from -6 to 6
- timesteps: int32 [32, 3], P(('dp', 'section')), may hold values from 0 to 999
- lengths: int32 [32, 3], P(('dp', 'section')), may hold values from 1 to 128, 256 in all within a row
- cotangent: bfloat16 [8192, 768], P(('dp', 'section')), may hold values from -6 to 6
- time_table: bfloat16 [1000, 768], replicated, may hold values from -6 to 6
- attn_norm_gain: bfloat16 [2, 768], replicated, may hold values from 0.5 to 1.5
- attn_norm_bias: bfloat16 [2, 768], replicated, may hold values from -3 to 3
- qkv_weight: bfloat16 [2, 768, 2304], replicated, may hold values from -0.3125 to 0.3125
- qv_bias: bfloat16 [2, 1536], replicated, may hold values from -3 to 3
- out_weight: bfloat16 [2, 768, 768], replicated, may hold values from -0.625 to 0.625
- out_bias: bfloat16 [2, 768], replicated, may hold values from -3 to 3
- mlp_norm_gain: bfloat16 [2, 768], replicated, may hold values from 0.5 to 1.5
- mlp_norm_bias: bfloat16 [2, 768], replicated, may hold values from -3 to 3
- up_weight: bfloat16 [2, 768, 3072], replicated, may hold values from -0.21875 to 0.21875
- up_bias: bfloat16 [2, 3072], replicated, may hold values from -3 to 3
- down_weight: bfloat16 [2, 3072, 768], replicated, may hold values from -0.15625 to 0.15625
- down_bias: bfloat16 [2, 768], replicated, may hold values from -3 to 3
Outputs:
- output: bfloat16 [8192, 768], P(('dp', 'section'))
- input_grad: bfloat16 [8192, 768], P(('dp', 'section'))
- time_table_grad: float32 [1000, 768], P(None, 'dp')
- attn_norm_gain_grad: float32 [2, 768], P(None, 'dp')
- attn_norm_bias_grad: float32 [2, 768], P(None, 'dp')
- qkv_weight_grad: float32 [2, 768, 2304], P(None, 'dp')
- qv_bias_grad: float32 [2, 1536], P(None, 'dp')
- out_weight_grad: float32 [2, 768, 768], P(None, 'dp')
- out_bias_grad: float32 [2, 768], P(None, 'dp')
- mlp_norm_gain_grad: float32 [2, 768], P(None, 'dp')
- mlp_norm_bias_grad: float32 [2, 768], P(None, 'dp')
- up_weight_grad: float32 [2, 768, 3072], P(None, 'dp')
- up_bias_grad: float32 [2, 3072], P(None, 'dp')
- down_weight_grad: float32 [2, 3072, 768], P(None, 'dp')
- down_bias_grad: float32 [2, 768], P(None, 'dp')
The draws below stay inside these ranges and needn't reach their ends.
Inputs may be any that keep to these rules, and one draw needn't show every extreme that they name: Each row's 3 lengths sum to 256, and the longest is 128.
All inputs are finite; a program needn't handle non-finite values.
Results may differ from the reference program's by a relative error of at most 0.018.
Values may be sent and summed in bfloat16 or wider, within the bound.
No kernel may reach another device: no remote copies, remote signals or barrier semaphores. Data moves between devices by JAX's collectives and lax.ppermute only.
A program may use at most 256 MiB of HBM per device.

```python
import math
import jax
import jax.numpy as jnp
import numpy as np
from jax import lax

D = 768
HEADS = 12
HDIM = 64
FF = 3072
NSTEPS = 1000
LAYERS = 2
ROWS = 256
MOST = 128
DOCS = 3
MICROS = 32
TOKENS = 8192


def place_ends(array, stream_key, smallest, largest):
    spot = [jax.random.randint(jax.random.fold_in(stream_key, axis), (), 0, length) for axis, length in enumerate(array.shape)]
    longest = array.shape.index(max(array.shape))
    neighbour = spot[:longest] + [(spot[longest] + 1) % array.shape[longest]] + spot[longest + 1:]
    return array.at[tuple(spot)].set(smallest).at[tuple(neighbour)].set(largest)


def steps_of(own_key, dims, cuts, smallest, high):
    def one(dim, blocks):
        steps = jax.random.uniform(jax.random.fold_in(jax.random.fold_in(own_key, 6), dim), (blocks,), jnp.float32, smallest / len(cuts), high / len(cuts))
        return jnp.repeat(jnp.exp(steps), dims[dim] // blocks).reshape((-1,) + (1,) * (len(dims) - dim - 1))

    loudness = one(*cuts[0])
    for cut in cuts[1:]:
        loudness = loudness * one(*cut)
    return loudness


def split_up(count, total, reach, slope):
    loads = [(1 << 20) // math.isqrt(rank ** slope) + 1 for rank in range(2, count + 1)]
    surplus, given = total - reach - (count - 1), [1] * (count - 1)
    while surplus > 0:
        candidates = [i for i in range(count - 1) if given[i] < reach]
        whole, remaining = sum([loads[i] for i in candidates]), surplus
        for i in candidates:
            more = min(reach - given[i], max(1, remaining * loads[i] // whole), surplus)
            given[i] = given[i] + more
            surplus = surplus - more
    return np.array([reach] + given)


def ragged(rng, amount, total, bound, lean):
    if amount == 2:
        one = jax.random.randint(rng, (), max(1, total - bound), min(bound, total - 1) + 1)
        return jnp.stack([one, total - one])
    sizes = jnp.asarray(split_up(amount, total, bound, lean), jnp.int32)
    pairs = (amount - 1) // 2
    source_of, taker = sizes[1:1 + 2 * pairs:2], sizes[2:2 + 2 * pairs:2]
    slack = jnp.minimum(source_of - 1, bound - taker)
    shifted = jax.random.randint(jax.random.fold_in(rng, 1), (pairs,), 0, 1 << 20) % (slack + 1)
    sizes = sizes.at[1:1 + 2 * pairs:2].set(source_of - shifted).at[2:2 + 2 * pairs:2].set(taker + shifted)
    return sizes[jax.random.permutation(jax.random.fold_in(rng, 2), amount)]


def noise(own_key, dims, deviation, reach, shards=(), held_as=jnp.bfloat16):
    values = jax.random.normal(own_key, dims, jnp.float32) * deviation
    if len(shards) > 0:
        values = steps_of(own_key, dims, shards, -0.22, 0.18) * values
    return jnp.clip(values, min=-reach, max=reach).astype(held_as)


def setup_inputs(seed: int = 0) -> dict:
    keys = jax.random.split(jax.random.key(seed), 18)
    return {
        "inputs": noise(keys[0], (TOKENS, D), 1.0, 6.0, ((0, 32),)),
        "timesteps": place_ends(jax.random.randint(keys[1], (MICROS, DOCS), 0, NSTEPS), jax.random.fold_in(keys[1], 1), 0, NSTEPS - 1).astype(jnp.int32),
        "lengths": jax.vmap(lambda own: ragged(own, DOCS, ROWS, MOST, 1))(jax.random.split(keys[2], MICROS)).reshape((MICROS, DOCS)).astype(jnp.int32),
        "cotangent": noise(keys[3], (TOKENS, D), 1.0, 6.0, ((0, 32),)),
        "time_table": noise(keys[4], (NSTEPS, D), 1.0, 6.0),
        "attn_norm_gain": jnp.clip(1.0 + 0.1 * jax.random.normal(keys[5], (LAYERS, D), jnp.float32), 0.5, 1.5).astype(jnp.bfloat16),
        "attn_norm_bias": noise(keys[6], (LAYERS, D), 0.3, 3.0),
        "qkv_weight": noise(keys[7], (LAYERS, D, 3 * D), (D // 2) ** -0.5, 0.3125),
        "qv_bias": noise(keys[8], (LAYERS, 2 * D), 0.3, 3.0),
        "out_weight": noise(keys[9], (LAYERS, D, D), (D // 8) ** -0.5, 0.625),
        "out_bias": noise(keys[10], (LAYERS, D), 0.3, 3.0),
        "mlp_norm_gain": jnp.clip(1.0 + 0.1 * jax.random.normal(keys[11], (LAYERS, D), jnp.float32), 0.5, 1.5).astype(jnp.bfloat16),
        "mlp_norm_bias": noise(keys[12], (LAYERS, D), 0.3, 3.0),
        "up_weight": noise(keys[13], (LAYERS, D, FF), D ** -0.5, 0.21875),
        "up_bias": noise(keys[14], (LAYERS, FF), 0.3, 3.0),
        "down_weight": noise(keys[15], (LAYERS, FF, D), (FF // 2) ** -0.5, 0.15625),
        "down_bias": noise(keys[16], (LAYERS, D), 0.3, 3.0),
    }


@jax.custom_vjp
def low(v):
    return lax.optimization_barrier(v.astype(jnp.bfloat16)).astype(jnp.float32)

@jax.custom_vjp
def low_back(v):
    return v

def low_keep(v):
    return (low(v), None)

def low_pass(kept, grad):
    return (grad,)

def back_keep(v):
    return (v, None)

def back_low(kept, grad):
    return (low(grad),)
low.defvjp(low_keep, low_pass)
low_back.defvjp(back_keep, back_low)
epsilon = 1e-05
masked_score = -1000000000.0
highest = lax.Precision.HIGHEST

def layer_norm(values, gain_row, shift_row):
    center = lax.optimization_barrier(jnp.mean(values, axis=-1, keepdims=True))
    centered = values - center
    variance = lax.optimization_barrier(jnp.mean(centered * centered, axis=-1, keepdims=True))
    return centered * lax.rsqrt(variance + epsilon) * gain_row + shift_row

def doc_index(doc_lengths, row_count):
    boundary = jnp.cumsum(doc_lengths, dtype=jnp.int32)
    position = jnp.arange(row_count, dtype=jnp.int32)
    return lax.optimization_barrier(jnp.sum((position[:, None] >= boundary[None, :]).astype(jnp.int32), axis=1))

def attention(hidden, segment, gain_row, shift_row, qkv_matrix, qv_shift, out_matrix, out_shift):
    row_count = hidden.shape[0]
    normed = low(layer_norm(hidden, gain_row, shift_row))
    mixed = jnp.dot(normed, qkv_matrix, precision=highest)
    query = low_back(low(mixed[:, :D] + qv_shift[:D])).reshape(row_count, HEADS, HDIM)
    keyset = low_back(low(mixed[:, D:2 * D])).reshape(row_count, HEADS, HDIM)
    valueset = low_back(low(mixed[:, 2 * D:] + qv_shift[D:])).reshape(row_count, HEADS, HDIM)
    scores = low_back(jnp.einsum('qhd,khd->hqk', query, keyset, precision=highest) * HDIM ** (-0.5))
    same_doc = segment[:, None] == segment[None, :]
    scores = jnp.where(same_doc[None], scores, masked_score)
    peak = lax.optimization_barrier(jnp.max(scores, axis=-1, keepdims=True))
    lifted = jnp.exp(scores - peak)
    weights = lifted / lax.optimization_barrier(jnp.sum(lifted, axis=-1, keepdims=True))
    weights_low = low(weights)
    context = jnp.einsum('hqk,khd->qhd', weights_low, valueset, precision=highest).reshape(row_count, D)
    context = low_back(low(context))
    return hidden + jnp.dot(context, out_matrix, precision=highest) + out_shift

def feed_forward(hidden, gain_row, shift_row, up_matrix, up_shift, down_matrix, down_shift):
    normed = low(layer_norm(hidden, gain_row, shift_row))
    inner = low_back(jnp.dot(normed, up_matrix, precision=highest) + up_shift)
    active = low(jax.nn.gelu(inner))
    return hidden + jnp.dot(active, down_matrix, precision=highest) + down_shift

def forward(start_rows, steps_row, segment, table, a_gain, a_shift, qkv_matrix, qv_shift, out_matrix, out_shift, m_gain, m_shift, up_matrix, up_shift, down_matrix, down_shift):
    embedded = jnp.take(table, jnp.take(steps_row, segment), axis=0)
    hidden = low_back(low(start_rows + embedded))
    for layer in range(LAYERS):
        hidden = low_back(low(attention(hidden, segment, a_gain[layer], a_shift[layer], qkv_matrix[layer], qv_shift[layer], out_matrix[layer], out_shift[layer])))
        hidden = low_back(low(feed_forward(hidden, m_gain[layer], m_shift[layer], up_matrix[layer], up_shift[layer], down_matrix[layer], down_shift[layer])))
    return hidden

def reference(inputs, timesteps, lengths, cotangent, time_table, attn_norm_gain, attn_norm_bias, qkv_weight, qv_bias, out_weight, out_bias, mlp_norm_gain, mlp_norm_bias, up_weight, up_bias, down_weight, down_bias):
    params = tuple((item.astype(jnp.float32) for item in (time_table, attn_norm_gain, attn_norm_bias, qkv_weight, qv_bias, out_weight, out_bias, mlp_norm_gain, mlp_norm_bias, up_weight, up_bias, down_weight, down_bias)))
    micro_inputs = inputs.reshape(MICROS, ROWS, D)
    micro_cot = cotangent.reshape(MICROS, ROWS, D)

    def one_row(carried, item):
        row_input, steps_row, length_row, row_cot = item
        segment = doc_index(length_row, ROWS)

        def run(start_rows, *weights):
            return forward(start_rows, steps_row, segment, *weights)
        result, pullback = jax.vjp(run, row_input.astype(jnp.float32), *params)
        grads = pullback(row_cot.astype(jnp.float32))
        carried = tuple((total + piece for total, piece in zip(carried, grads[1:])))
        return (carried, (result.astype(jnp.bfloat16), grads[0].astype(jnp.bfloat16)))
    initial = tuple((jnp.zeros(item.shape, jnp.float32) for item in params))
    totals, (results, starts) = lax.scan(one_row, initial, (micro_inputs, timesteps, lengths, micro_cot))
    return (results.reshape(TOKENS, D), starts.reshape(TOKENS, D), totals[0], totals[1], totals[2], totals[3], totals[4], totals[5], totals[6], totals[7], totals[8], totals[9], totals[10], totals[11], totals[12])
```

```python
import functools

import jax
import jax.numpy as jnp
from jax import lax
from jax.experimental import pallas as pl
from jax.experimental.pallas import tpu as pltpu
from jax.sharding import PartitionSpec as P

HDIM = 64
PAIR = 2 * HDIM
LAYERS = 2
BLOCK = 256
LIMIT = 60 * 1024 * 1024

epsilon = 1e-05
masked_score = -1000000000.0
scale = HDIM ** (-0.5)
f32 = jnp.float32
bf16 = jnp.bfloat16
ANY = pl.BlockSpec(memory_space=pl.ANY)
VMEM = pl.BlockSpec(memory_space=pltpu.VMEM)
SMEM = pl.BlockSpec(memory_space=pltpu.SMEM)


def mm(a, b):
    return lax.dot_general(a, b, (((1,), (0,)), ((), ())), preferred_element_type=f32)


def mm_nt(a, b):
    return lax.dot_general(a, b, (((1,), (1,)), ((), ())), preferred_element_type=f32)


def cols(n, size=BLOCK):
    return pl.ds(pl.multiple_of(n * size, 128), size)


def rows_of(n, size=BLOCK):
    return pl.ds(pl.multiple_of(n * size, 16), size)


def loop(count, body):
    lax.fori_loop(0, count, lambda n, none: (body(n), none)[1], 0)


class Copies:
    def __init__(self, sems):
        self.sems, self.used, self.pending = sems, 0, []

    def start(self, source, target):
        copy = pltpu.make_async_copy(source, target, self.sems.at[self.used])
        self.used += 1
        copy.start()
        return copy

    def send(self, source, target):
        self.pending.append(self.start(source, target))

    def finish(self):
        for copy in self.pending:
            copy.wait()


def norm_stats(hidden):
    full = hidden.astype(f32)
    centered = full - jnp.mean(full, axis=-1, keepdims=True)
    rstd = lax.rsqrt(jnp.mean(centered * centered, axis=-1, keepdims=True) + epsilon)
    return centered * rstd, rstd


def norm_forward(hidden, gain, shift):
    xhat, rstd = norm_stats(hidden)
    return (xhat * gain.astype(f32) + shift.astype(f32)).astype(bf16)


def gelu_pair(u):
    c, a = 0.7978845608028654, 0.044715
    square = u * u
    t = jnp.tanh(c * u * (1.0 + a * square))
    half = 0.5 * (1.0 + t)
    slope = half + 0.5 * u * (1.0 - t * t) * (c * (1.0 + 3.0 * a * square))
    return u * half, slope


def doc_mask(bounds, rows):
    one = lax.broadcasted_iota(jnp.int32, (rows, rows), 0)
    other = lax.broadcasted_iota(jnp.int32, (rows, rows), 1)
    left = sum((one >= b).astype(jnp.int32) for b in bounds)
    right = sum((other >= b).astype(jnp.int32) for b in bounds)
    return left == right


def bounds_of(len_ref):
    bounds, total = [], 0
    for k in range(len_ref.shape[1] - 1):
        total = total + len_ref[0, k]
        bounds.append(total)
    return bounds


def halves(x):
    low = lax.broadcasted_iota(jnp.int32, x.shape, 1) < HDIM
    zero = jnp.zeros_like(x)
    return jnp.where(low, x, zero), jnp.where(low, zero, x)


def soft_columns(key, query, same):
    s = jnp.where(same, mm_nt(key, query) * scale, masked_score)
    e = jnp.exp(s - jnp.max(s, axis=0, keepdims=True))
    return e * (1.0 / jnp.sum(e, axis=0, keepdims=True))


def qkv_forward(normed, weight, bias_ref, bias_row, target):
    width = normed.shape[1]
    per = width // BLOCK

    def part(base, bias_base):
        def body(n):
            at = cols(n + base * per)
            out = mm(normed, weight[:, at])
            if bias_base is not None:
                out = out + bias_ref[bias_row, cols(n + bias_base * per)].astype(f32)
            target[:, at] = out.astype(bf16)

        loop(per, body)

    part(0, 0)
    part(1, None)
    part(2, 1)


def attend_context(mixed, same_ref, target):
    width = mixed.shape[1] // 3
    count = width // PAIR

    def body(p):
        q = mixed[:, cols(p, PAIR)]
        k = mixed[:, cols(p + count, PAIR)]
        v = mixed[:, cols(p + 2 * count, PAIR)]
        same = same_ref[...] > 0.5
        total = None
        for key, value in zip(halves(k), halves(v)):
            probs = soft_columns(key, q, same).astype(bf16)
            piece = mm(value.T, probs)
            total = piece if total is None else total + piece
        target[:, cols(p, PAIR)] = total.T.astype(bf16)

    loop(count, body)


def attend_grad(mixed, same_ref, dcontext, target, context=None):
    width = mixed.shape[1] // 3
    count = width // PAIR

    def body(p):
        q = mixed[:, cols(p, PAIR)]
        k = mixed[:, cols(p + count, PAIR)]
        v = mixed[:, cols(p + 2 * count, PAIR)]
        d = dcontext[:, cols(p, PAIR)]
        same = same_ref[...] > 0.5
        dq = dk = dv = ctx = 0.0
        for key, value, query, dc in zip(halves(k), halves(v), halves(q), halves(d)):
            soft = soft_columns(key, q, same)
            probs = soft.astype(bf16)
            dsoft = mm_nt(value, d)
            inner = jnp.sum(soft * dsoft, axis=0, keepdims=True)
            dscores = (soft * (dsoft - inner)).astype(bf16)
            dv = dv + mm(probs, dc)
            dk = dk + mm(dscores, query)
            dq = dq + mm(key.T, dscores)
            if context is not None:
                ctx = ctx + mm(value.T, probs)
        target[:, cols(p, PAIR)] = (dq * scale).T.astype(bf16)
        target[:, cols(p + count, PAIR)] = (dk * scale).astype(bf16)
        target[:, cols(p + 2 * count, PAIR)] = dv.astype(bf16)
        if context is not None:
            context[:, cols(p, PAIR)] = ctx.T.astype(bf16)

    loop(count, body)


def forward_kernel(
    bits, lengths, h0, a_gain, a_shift, qv, out_b, m_gain, m_shift, up_b, down_b,
    qkv_w, out_w, up_w, down_w,
    x1, y1, hidden, last, na, mixed, ctx, nm, act, slope,
    v_qkv, v_out, v_up, v_down, v_h, v_na, v_mixed, v_ctx, v_nm, v_act, v_slope, v_x, same, sems,
):
    copies = Copies(sems)
    rows, width = h0.shape
    wide = up_w.shape[2]
    loads = []
    for l in range(LAYERS):
        loads.append(
            [
                copies.start(w.at[l], v.at[l])
                for w, v in ((qkv_w, v_qkv), (out_w, v_out), (up_w, v_up), (down_w, v_down))
            ]
        )
    bounds = bounds_of(lengths)
    same[...] = doc_mask(bounds, rows).astype(f32)
    v_h[0] = h0[...]
    tail = x1.shape[0] - rows
    which = lax.broadcasted_iota(jnp.int32, (tail, width), 0)
    note = jnp.zeros((tail, width), f32)
    for k, bound in enumerate(bounds):
        note = jnp.where(which == k, bound.astype(f32), note)
    v_x[...] = note.astype(bf16)
    copies.send(v_x, x1.at[pl.ds(rows, tail)])
    for l in range(LAYERS):
        h_in, h_mid = v_h.at[2 * l], v_h.at[2 * l + 1]
        h_out = v_h.at[2 * l + 2]
        v_na[l] = norm_forward(h_in[...], a_gain[l : l + 1, :], a_shift[l : l + 1, :])
        loads[l][0].wait()
        qkv_forward(v_na[l], v_qkv.at[l], qv, slice(l, l + 1), v_mixed.at[l])
        copies.send(v_na.at[l], na.at[l])
        copies.send(v_mixed.at[l], mixed.at[l])
        attend_context(v_mixed.at[l], same, v_ctx.at[l])
        copies.send(v_ctx.at[l], ctx.at[l])
        loads[l][1].wait()

        def project(n):
            at = cols(n)
            out = h_in[:, at].astype(f32) + mm(v_ctx[l], v_out[l, :, at])
            h_mid[:, at] = (out + out_b[l : l + 1, at].astype(f32)).astype(bf16)

        loop(width // BLOCK, project)
        v_nm[l] = norm_forward(h_mid[...], m_gain[l : l + 1, :], m_shift[l : l + 1, :])
        copies.send(v_nm.at[l], nm.at[l])
        loads[l][2].wait()

        def expand(n):
            at = cols(n)
            inner = mm(v_nm[l], v_up[l, :, at]) + up_b[l : l + 1, at].astype(f32)
            active, s = gelu_pair(inner)
            v_act[l, :, at] = active.astype(bf16)
            v_slope[l, :, at] = s.astype(bf16)

        loop(wide // BLOCK, expand)
        copies.send(v_act.at[l], act.at[l])
        copies.send(v_slope.at[l], slope.at[l])
        loads[l][3].wait()

        def contract(n):
            at = cols(n)
            out = h_mid[:, at].astype(f32) + mm(v_act[l], v_down[l, :, at])
            h_out[:, at] = (out + down_b[l : l + 1, at].astype(f32)).astype(bf16)

        loop(width // BLOCK, contract)
    for k in range(1, 2 * LAYERS):
        copies.send(v_h.at[k], hidden.at[k - 1])
    copies.send(v_h.at[2 * LAYERS], last)
    by_x = jnp.where(bits[0] == 0, 2, 0)
    by_y = jnp.where(bits[1] == 0, 3, 1)
    copies.send(v_h.at[by_x], x1.at[pl.ds(0, rows)])
    copies.send(v_h.at[by_y], y1)
    copies.finish()


def norm_backward(h, gain, dnormed, upstream, vec, at_gain, at_shift, target):
    width = h.shape[1]
    xhat, rstd = norm_stats(h[...])
    dn = dnormed[...]
    e = dn * gain.astype(f32)
    grad = (
        e - jnp.mean(e, axis=-1, keepdims=True) - xhat * jnp.mean(e * xhat, axis=-1, keepdims=True)
    ) * rstd
    target[...] = (upstream[...].astype(f32) + grad).astype(bf16)
    vec[:, at_gain : at_gain + width] = jnp.sum(dn * xhat, axis=0, keepdims=True)
    vec[:, at_shift : at_shift + width] = jnp.sum(dn, axis=0, keepdims=True)


def colsum(x):
    return jnp.sum(x.astype(f32), axis=0, keepdims=True)


def backward_kernel(layer, *refs):
    refs = list(refs)
    take = lambda n: [refs.pop(0) for _ in range(n)]
    bits, lengths, g, a_gain, m_gain = take(5)
    h_a, h_m, mixed, slope, qkv_w, out_w, up_w, down_w = take(8)
    if layer == 0:
        take(2)
        g_upper, g_other = take(2)
    dinner, dmixed, g_mid, vec, send, own, extra = take(7)
    v_qkv, v_out, v_up, v_down, v_ha, v_hm, v_mixed, v_slope = take(8)
    v_dinner, v_dctx, v_dmixed, v_dn, v_gmid, v_gout, v_far, same, sems = take(9)
    copies = Copies(sems)
    rows, width = g.shape
    wide = up_w.shape[2]
    q = wide // 4
    l_slope = copies.start(slope.at[layer], v_slope)
    l_down = [
        copies.start(down_w.at[layer, pl.ds(k * q, q)], v_down.at[pl.ds(k * q, q)]) for k in range(4)
    ]
    l_up = copies.start(up_w.at[layer], v_up)
    l_hm = copies.start(h_m if layer == 0 else h_m, v_hm)
    l_out = copies.start(out_w.at[layer], v_out)
    l_mixed = copies.start(mixed.at[layer], v_mixed)
    l_qkv = copies.start(qkv_w.at[layer], v_qkv)
    l_ha = copies.start(h_a, v_ha)
    if layer == 0:
        l_far = copies.start(g_upper, v_far)
    same[...] = doc_mask(bounds_of(lengths), rows).astype(f32)
    vec[:, 2 * width : 3 * width] = jnp.zeros((1, width), f32)
    at_qv, at_mshift, at_downb, at_upb = 4 * width, 6 * width, 7 * width, 8 * width
    vec[:, at_downb : at_downb + width] = colsum(g[...])
    l_slope.wait()
    per = q // BLOCK
    for k in range(4):
        l_down[k].wait()

        def body(n):
            n = n + k * per
            at = cols(n)
            dact = mm_nt(g[...], v_down[rows_of(n), :])
            di = (dact * v_slope[:, at].astype(f32)).astype(bf16)
            v_dinner[:, at] = di
            vec[:, pl.ds(pl.multiple_of(at_upb + n * BLOCK, 128), BLOCK)] = colsum(di)

        loop(per, body)
    copies.send(v_dinner, dinner.at[layer])
    l_up.wait()

    def back_up(n):
        v_dn[:, cols(n)] = mm_nt(v_dinner[...], v_up[rows_of(n), :])

    loop(width // BLOCK, back_up)
    l_hm.wait()
    norm_backward(v_hm, m_gain[layer : layer + 1, :], v_dn, g, vec, 3 * width, at_mshift, v_gmid)
    copies.send(v_gmid, g_mid)
    vec[:, 2 * width : 3 * width] = colsum(v_gmid[...])
    l_out.wait()

    def back_out(n):
        v_dctx[:, cols(n)] = mm_nt(v_gmid[...], v_out[rows_of(n), :]).astype(bf16)

    loop(width // BLOCK, back_out)
    l_mixed.wait()
    attend_grad(v_mixed, same, v_dctx, v_dmixed)
    copies.send(v_dmixed, dmixed.at[layer])
    vec[:, at_qv : at_qv + width] = colsum(v_dmixed[:, :width])
    vec[:, at_qv + width : at_qv + 2 * width] = colsum(v_dmixed[:, 2 * width :])
    l_qkv.wait()

    def back_qkv(n):
        v_dn[:, cols(n)] = mm_nt(v_dmixed[...], v_qkv[rows_of(n), :])

    loop(width // BLOCK, back_qkv)
    l_ha.wait()
    norm_backward(v_ha, a_gain[layer : layer + 1, :], v_dn, v_gmid, vec, 0, width, v_gout)
    if layer == LAYERS - 1:
        copies.send(v_gout, extra)
        first = bits[1] == 0
        v_far[...] = g[...]
        a, b = v_far, v_gout
    else:
        l_far.wait()
        first = bits[0] == 0
        a, b = v_far, v_gmid
        count = lengths.shape[1]
        doc = lax.broadcasted_iota(jnp.int32, (16, rows), 0)
        token = lax.broadcasted_iota(jnp.int32, (16, rows), 1)
        index = sum((token >= bound).astype(jnp.int32) for bound in bounds_of(lengths))
        onehot = ((index == doc) & (doc < count)).astype(f32).astype(bf16)
        extra[...] = mm(onehot, v_gout[...])
        copies.send(v_gout, g_other)

    @pl.when(first)
    def _():
        pltpu.sync_copy(a, send)
        pltpu.sync_copy(b, own)

    @pl.when(jnp.logical_not(first))
    def _():
        pltpu.sync_copy(b, send)
        pltpu.sync_copy(a, own)

    copies.finish()


def feed_weight_kernel(
    bits, h, g, own_nm, own_dinner, gain, shift, up_b, up_w, down_w,
    send, keep, act,
    v_up, v_down, v_own, v_nm, v_left, v_dinner, v_own_dinner, v_act, v_send, v_keep, sems,
):
    copies = Copies(sems)
    rows, width = h.shape
    wide = up_w.shape[2]
    half = wide // 2
    layer, core = bits[1], bits[2]
    l_nm = copies.start(own_nm.at[layer], v_own)
    loads = []
    for k in range(2):
        part = jnp.where(k == 0, 1 - core, core)
        at = pl.ds(pl.multiple_of(part * half, 128), half)
        down_at = pl.ds(pl.multiple_of(part * half, 16), half)
        loads.append(
            [
                copies.start(up_w.at[layer, :, at], v_up.at[k]),
                copies.start(down_w.at[layer, down_at], v_down.at[k]),
                copies.start(own_dinner.at[layer, :, at], v_own_dinner.at[k]),
            ]
        )
    pick = lambda ref: jnp.where(layer == 0, ref[0:1, :].astype(f32), ref[1:2, :].astype(f32))
    normed = norm_forward(h[...], pick(gain), pick(shift))
    v_nm[...] = normed
    v_left[:, rows:] = normed.T
    l_nm.wait()
    v_left[:, :rows] = v_own[...].T
    for k in range(2):
        part = jnp.where(k == 0, 1 - core, core)
        for load in loads[k]:
            load.wait()
        target = v_send if k == 0 else v_keep

        def body(n):
            at = cols(n)
            far = pl.ds(pl.multiple_of(part * half + n * BLOCK, 128), BLOCK)
            bias = jnp.where(layer == 0, up_b[0:1, far].astype(f32), up_b[1:2, far].astype(f32))
            inner = mm(v_nm[...], v_up[k, :, at]) + bias
            active, slope = gelu_pair(inner)
            v_act[:, far] = active.astype(bf16)
            dact = mm_nt(g[...], v_down[k, rows_of(n), :])
            v_dinner[:rows] = v_own_dinner[k, :, at]
            v_dinner[rows:] = (dact * slope).astype(bf16)
            target[:, at] = mm(v_left[...], v_dinner[...]).astype(bf16)

        loop(half // BLOCK, body)
        copies.send(target, send if k == 0 else keep)
    copies.send(v_act, act)
    copies.finish()


def down_weight_kernel(
    bits, g, own_g, notes, act, own_act,
    send, keep,
    v_left, v_act, v_own, v_send, v_keep, sems,
):
    copies = Copies(sems)
    rows, width = g.shape
    wide = act.shape[1]
    half = width // 2
    layer, core = bits[1], bits[2]
    l_own = copies.start(own_act.at[layer], v_own)
    l_act = copies.start(act, v_act)
    for k in range(2):
        part = jnp.where(k == 0, 1 - core, core)
        at = pl.ds(pl.multiple_of(part * half, 128), half)
        v_left[k, :, :rows] = own_g[:, at].T
        v_left[k, :, rows:] = g[:, at].T
    v_send[half:] = notes[1 - core].astype(bf16)
    v_keep[half:] = notes[core].astype(bf16)
    l_own.wait()
    l_act.wait()
    for k in range(2):
        target = v_send if k == 0 else v_keep

        def body(n):
            at = cols(n)
            out = mm(v_left[k, :, :rows], v_own[:, at]) + mm(v_left[k, :, rows:], v_act[:, at])
            target[:half, at] = out.astype(bf16)

        loop(wide // BLOCK, body)
        copies.send(target, send if k == 0 else keep)
    copies.finish()


def attend_weight_kernel(
    bits, hx, g, own_g, own_na, own_ctx, own_dmixed, gain, shift, qv, qkv_w, out_w,
    send, keep,
    v_qkv, v_out, v_na, v_mixed, v_dctx, v_dmixed, v_ctx, v_left, v_right, v_own, v_own_ctx,
    v_own_dmixed, v_bias, v_send, v_keep, same, sems,
):
    copies = Copies(sems)
    rows, width = g.shape
    layer, core = bits[0], bits[2]
    l_qkv = copies.start(qkv_w.at[layer], v_qkv)
    l_out = copies.start(out_w.at[layer], v_out)
    l_own = copies.start(own_na.at[layer], v_own)
    l_ctx = copies.start(own_ctx.at[layer], v_own_ctx)
    l_dmixed = copies.start(own_dmixed.at[layer], v_own_dmixed)
    pick = lambda ref: jnp.where(layer == 0, ref[0:1, :].astype(f32), ref[1:2, :].astype(f32))
    note = hx[rows:, :].astype(f32)
    bounds = [note[k : k + 1, :rows].astype(jnp.int32) for k in range(2)]
    same[...] = doc_mask(bounds, rows).astype(f32)
    v_bias[...] = pick(qv)
    v_na[...] = norm_forward(hx[:rows, :], pick(gain), pick(shift))
    l_qkv.wait()
    qkv_forward(v_na[...], v_qkv, v_bias, slice(0, 1), v_mixed)
    l_out.wait()

    def back_out(n):
        v_dctx[:, cols(n)] = mm_nt(g[...], v_out[rows_of(n), :]).astype(bf16)

    loop(width // BLOCK, back_out)
    attend_grad(v_mixed, same, v_dctx, v_dmixed, v_ctx)
    part = width // 2
    l_ctx.wait()
    v_left[:, :rows] = v_own_ctx[...].T
    v_left[:, rows:] = v_ctx[...].T
    for k in range(2):
        side = jnp.where(k == 0, 1 - core, core)
        target = v_send if k == 0 else v_keep
        at = pl.ds(pl.multiple_of(side * part, 128), part)
        v_right[:rows, :part] = own_g[:, at]
        v_right[rows:, :part] = g[:, at]
        target[:, :part] = mm(v_left[...], v_right[:, :part]).astype(bf16)
    l_own.wait()
    l_dmixed.wait()
    v_left[:, :rows] = v_own[...].T
    v_left[:, rows:] = v_na[...].T
    for k in range(2):
        side = jnp.where(k == 0, 1 - core, core)
        target = v_send if k == 0 else v_keep

        def body(n):
            at = pl.ds(pl.multiple_of(side * 3 * part + n * part, 128), part)
            v_right[:rows, :part] = v_own_dmixed[:, at]
            v_right[rows:, :part] = v_dmixed[:, at]
            out = mm(v_left[...], v_right[:, :part]).astype(bf16)
            target[:, pl.ds(pl.multiple_of(part + n * part, 128), part)] = out

        loop(3, body)
        copies.send(target, send if k == 0 else keep)
    copies.finish()


def call(kernel, operands, specs, outs, out_specs, scratch, copies, flops, aliases=None):
    moved = sum(2 * x.size for x in operands)
    return pl.pallas_call(
        kernel,
        out_shape=[jax.ShapeDtypeStruct(s, d) for s, d in outs],
        in_specs=specs,
        out_specs=out_specs,
        scratch_shapes=[pltpu.VMEM(s, d) for s, d in scratch] + [pltpu.SemaphoreType.DMA((copies,))],
        input_output_aliases=aliases or {},
        compiler_params=pltpu.CompilerParams(vmem_limit_bytes=LIMIT),
        cost_estimate=pl.CostEstimate(flops=flops, bytes_accessed=moved, transcendentals=0),
    )(*operands)


def swap(x, axis, by):
    size = lax.axis_size(axis)
    return lax.ppermute(x, axis, [(i, i ^ by) for i in range(size)])


def plus(a, b):
    return (a.astype(f32) + b.astype(f32)).astype(bf16)


def ring_sum(near, place_z, nx, nz):
    take = lambda step: lax.dynamic_index_in_dim(near, (place_z - step) % nz, 0, keepdims=False)
    if nz > 4:
        groups = [[z * nx + x for z in range(nz)] for x in range(nx)]
        flat = near.reshape((-1,) + near.shape[2:])
        return lax.psum_scatter(flat, "dp", scatter_dimension=0, axis_index_groups=groups, tiled=True)
    ring = [(d, (d + nx) % (nx * nz)) for d in range(nx * nz)]
    carry = take(1)
    for step in range(2, nz + 1):
        carry = plus(lax.ppermute(carry, "dp", ring), take(step))
    return carry


def in_order(place, mine, theirs, axis=0):
    join = lambda a, b: jnp.concatenate([a, b], axis=axis)
    return jnp.where(place == 0, join(mine, theirs), join(theirs, mine))


def local(
    inputs,
    timesteps,
    lengths,
    cotangent,
    time_table,
    attn_norm_gain,
    attn_norm_bias,
    qkv_weight,
    qv_bias,
    out_weight,
    out_bias,
    mlp_norm_gain,
    mlp_norm_bias,
    up_weight,
    up_bias,
    down_weight,
    down_bias,
):
    place = lax.axis_index("section")
    side, core = place // 2, place % 2
    dp = lax.axis_size("dp")
    nx, nz = 2, dp // 2
    index = lax.axis_index("dp")
    place_z, place_x = index // nx, index % nx
    rows, width = inputs.shape
    wide = up_weight.shape[2]
    docs = lengths.shape[1]
    step_count = time_table.shape[0]
    everyone = dp * lax.axis_size("section")
    bits = jnp.stack([place_x, side, core]).astype(jnp.int32)

    position = jnp.arange(rows, dtype=jnp.int32)[:, None]
    embedded, bound = None, 0
    for k in range(docs):
        row = lax.dynamic_slice_in_dim(time_table, timesteps[0, k], 1, 0).astype(f32)
        embedded = row if k == 0 else jnp.where(position >= bound, row, embedded)
        bound = bound + lengths[0, k]
    h0 = (inputs.astype(f32) + embedded).astype(bf16)

    mat = 2 * rows * width
    tok, tok2 = (rows, width), (LAYERS, rows, width)
    x1, y1, hidden, last, na, mixed, ctx, nm, act, slope = call(
        forward_kernel,
        [bits, lengths, h0, attn_norm_gain, attn_norm_bias, qv_bias, out_bias, mlp_norm_gain,
         mlp_norm_bias, up_bias, down_bias, qkv_weight, out_weight, up_weight, down_weight],
        [SMEM, SMEM] + [VMEM] * 9 + [ANY] * 4,
        [((rows + 16, width), bf16), (tok, bf16), ((2 * LAYERS - 1,) + tok, bf16), (tok, bf16),
         (tok2, bf16), ((LAYERS, rows, 3 * width), bf16), (tok2, bf16), (tok2, bf16),
         ((LAYERS, rows, wide), bf16), ((LAYERS, rows, wide), bf16)],
        [ANY] * 10,
        [(qkv_weight.shape, bf16), (out_weight.shape, bf16), (up_weight.shape, bf16),
         (down_weight.shape, bf16), ((2 * LAYERS + 1,) + tok, bf16), (tok2, bf16),
         ((LAYERS, rows, 3 * width), bf16), (tok2, bf16), (tok2, bf16), ((LAYERS, rows, wide), bf16),
         ((LAYERS, rows, wide), bf16), ((16, width), bf16), ((rows, rows), f32)],
        40,
        2 * mat * (4 * width + 2 * wide),
    )
    peer_hx = swap(x1, "dp", 1)
    peer_hm = swap(y1, "section", 2)

    def backward(layer, g, more):
        outs = [((LAYERS, rows, wide), bf16), ((LAYERS, rows, 3 * width), bf16), (tok, bf16),
                ((1, 12 * width), f32), (tok, bf16), (tok, bf16)]
        last_layer = layer == LAYERS - 1
        if last_layer:
            outs.append((tok, bf16))
            aliases, kept = {}, []
        else:
            outs = [(tok, bf16)] + outs + [((16, width), f32)]
            aliases, kept = {13: 1, 14: 2}, more[:2]
        h_a = h0 if layer == 0 else hidden[2 * layer - 1]
        operands = [bits, lengths, g, attn_norm_gain, mlp_norm_gain, h_a, hidden[2 * layer],
                    mixed, slope, qkv_weight, out_weight, up_weight, down_weight] + kept
        specs = [SMEM, SMEM] + [VMEM] * 3 + [ANY] * (8 + len(kept))
        if not last_layer:
            operands.append(more[2])
            specs.append(ANY)
        out_specs = [ANY] * len(outs)
        out_specs[-1] = out_specs[-1] if last_layer else VMEM
        out_specs[3 if last_layer else 4] = VMEM
        return call(
            functools.partial(backward_kernel, layer),
            operands,
            specs,
            outs,
            out_specs,
            [(qkv_weight.shape[1:], bf16), (out_weight.shape[1:], bf16), (up_weight.shape[1:], bf16),
             (down_weight.shape[1:], bf16), (tok, bf16), (tok, bf16), ((rows, 3 * width), bf16),
             ((rows, wide), bf16), ((rows, wide), bf16), (tok, bf16), ((rows, 3 * width), bf16),
             (tok, f32), (tok, bf16), (tok, bf16), (tok, bf16), ((rows, rows), f32)],
            24,
            mat * (4 * width + 2 * wide),
            aliases,
        )

    dinner, dmixed, g3, vec1, y2, own_gm, g2 = backward(1, cotangent, [])
    peer_gm = swap(y2, "section", 2)
    g0, dinner, dmixed, g1, vec0, x2, own_ga, doc_sums = backward(0, g2, [dinner, dmixed, g3])
    peer_ga = swap(x2, "dp", 1)

    up_send, up_keep, peer_act = call(
        feed_weight_kernel,
        [bits, peer_hm, peer_gm, nm, dinner, mlp_norm_gain, mlp_norm_bias, up_bias, up_weight, down_weight],
        [SMEM, VMEM, VMEM, ANY, ANY, VMEM, VMEM, VMEM, ANY, ANY],
        [((width, wide // 2), bf16), ((width, wide // 2), bf16), ((rows, wide), bf16)],
        [ANY] * 3,
        [((2, width, wide // 2), bf16), ((2, wide // 2, width), bf16), (tok, bf16), (tok, bf16),
         ((width, 2 * rows), bf16), ((2 * rows, BLOCK), bf16), ((2, rows, wide // 2), bf16),
         ((rows, wide), bf16), ((width, wide // 2), bf16), ((width, wide // 2), bf16)],
        12,
        4 * mat * wide,
    )

    vec = jnp.concatenate([vec0, vec1], axis=0)
    group = lambda a, n: vec[:, a : a + n * width].reshape(LAYERS, n, dp, width // dp)
    swing = lambda x: x.transpose(0, 2, 1, 3).reshape(LAYERS, 1, wide)
    qv_part = vec[:, 4 * width : 6 * width].reshape(LAYERS, dp, 2 * width // dp)
    rest = group(6 * width, 2).transpose(0, 2, 1, 3).reshape(LAYERS, dp, 2 * width // dp)
    second = jnp.concatenate([qv_part, rest], axis=2).reshape(LAYERS, 1, wide)
    vec_rows = jnp.concatenate(
        [swing(group(0, 4)), second, vec[:, 8 * width :].reshape(LAYERS, 1, wide)], axis=1
    ).reshape(3 * LAYERS, wide)
    me = index * lax.axis_size("section") + place
    per = wide // width
    sums = jnp.zeros((everyone * docs, width), f32)
    sums = lax.dynamic_update_slice(sums, doc_sums[:docs], (me * docs, 0))
    sums = sums.reshape(-1, per, dp, width // dp).transpose(0, 2, 1, 3).reshape(-1, wide)
    marks = jnp.stack([timesteps[0] // 32, timesteps[0] % 32], axis=1).astype(f32)
    marks = lax.dynamic_update_slice(jnp.zeros((everyone * docs, 2), f32), marks, (me * docs, 0))
    share = wide // dp
    mark_rows = -(-everyone * docs * 2 // share)
    marks = jnp.pad(marks.reshape(-1), (0, mark_rows * share - everyone * docs * 2))
    marks = jnp.broadcast_to(marks.reshape(mark_rows, 1, share), (mark_rows, dp, share))
    notes = jnp.concatenate([vec_rows, sums, marks.reshape(mark_rows, wide)], axis=0)
    sum_rows = sums.shape[0]
    note_rows = -(-notes.shape[0] // 32) * 16
    notes = jnp.pad(notes, ((0, 2 * note_rows - notes.shape[0]), (0, 0))).reshape(2, note_rows, wide)

    half = width // 2
    tall = half + note_rows
    down_send, down_keep = call(
        down_weight_kernel,
        [bits, peer_gm, own_gm, notes, peer_act, act],
        [SMEM, VMEM, VMEM, VMEM, ANY, ANY],
        [((tall, wide), bf16)] * 2,
        [ANY] * 2,
        [((2, half, 2 * rows), bf16), ((rows, wide), bf16), ((rows, wide), bf16),
         ((tall, wide), bf16), ((tall, wide), bf16)],
        4,
        2 * mat * wide,
    )
    at_send, at_keep = call(
        attend_weight_kernel,
        [bits, peer_hx, peer_ga, own_ga, na, ctx, dmixed, attn_norm_gain, attn_norm_bias, qv_bias,
         qkv_weight, out_weight],
        [SMEM, VMEM, VMEM, VMEM, ANY, ANY, ANY, VMEM, VMEM, VMEM, ANY, ANY],
        [((width, 2 * width), bf16)] * 2,
        [ANY] * 2,
        [((width, 3 * width), bf16), ((width, width), bf16), (tok, bf16), ((rows, 3 * width), bf16),
         (tok, bf16), ((rows, 3 * width), bf16), (tok, bf16), ((width, 2 * rows), bf16),
         ((2 * rows, half), bf16), (tok, bf16), (tok, bf16), ((rows, 3 * width), bf16),
         ((1, 2 * width), f32), ((width, 2 * width), bf16), ((width, 2 * width), bf16),
         ((rows, rows), f32)],
        8,
        6 * mat * width,
    )

    pick = lambda x, at, axis: lax.dynamic_index_in_dim(x, at, axis, keepdims=False)

    up = plus(up_keep, swap(up_send, "section", 1)).reshape(nz, nx, width // dp, wide // 2)
    up = plus(pick(up, place_x, 1), swap(pick(up, 1 - place_x, 1), "dp", 1))
    up = ring_sum(up, place_z, nx, nz)
    up = in_order(side, up[None], swap(up, "section", 2)[None])
    grad_up = in_order(core, up, swap(up, "section", 1), 2).astype(f32)

    down = plus(down_keep, swap(down_send, "section", 1)).reshape(tall, nz, nx, share)
    down = plus(pick(down, place_x, 2), swap(pick(down, 1 - place_x, 2), "dp", 1))
    down = ring_sum(down.transpose(1, 0, 2), place_z, nx, nz)
    down = in_order(side, down[None], swap(down, "section", 2)[None])
    down = in_order(core, down[:, None], swap(down, "section", 1)[:, None], 1)
    grad_down = down[:, :, :half].reshape(LAYERS, width, share).transpose(0, 2, 1).astype(f32)
    small = jnp.sum(down[:, :, half:].astype(f32), axis=0).reshape(2 * note_rows, share)
    small_vec = small[: 3 * LAYERS].reshape(LAYERS, 3, share)
    one = width // dp
    a_gain, a_shift, a_out, m_gain = [small_vec[:, 0, k * one : (k + 1) * one] for k in range(4)]
    a_qv, m_shift, m_down = [
        small_vec[:, 1, a * one : b * one] for a, b in ((0, 2), (2, 3), (3, 4))
    ]
    m_up = small_vec[:, 2]
    small_sums = small[3 * LAYERS : 3 * LAYERS + sum_rows].reshape(-1, one)
    small_marks = small[3 * LAYERS + sum_rows : 3 * LAYERS + sum_rows + mark_rows].reshape(-1)
    small_marks = small_marks[: everyone * docs * 2].reshape(-1, 2)
    every_step = (small_marks[:, 0] * 32 + small_marks[:, 1]).astype(jnp.int32)
    onehot = (jnp.arange(step_count, dtype=jnp.int32)[:, None] == every_step[None, :]).astype(f32)
    grad_table = jnp.dot(onehot, small_sums, precision=lax.Precision.HIGHEST)

    at = plus(at_keep, swap(at_send, "section", 1)).reshape(width, 2, width)
    at = plus(pick(at, side, 1), swap(pick(at, 1 - side, 1), "section", 2))
    at = ring_sum(at.reshape(nz, nx * one, width), place_z, nx, nz).reshape(nx, one, width)
    at = in_order(
        place_x, pick(at, place_x, 0)[None], swap(pick(at, 1 - place_x, 0), "dp", 1)[None]
    )
    at = in_order(side, at, swap(at, "section", 2), 2)
    at = in_order(core, at[:, None], swap(at, "section", 1)[:, None], 1)
    grad_out = at[:, :, :, :half].transpose(0, 2, 1, 3).reshape(LAYERS, one, width).astype(f32)
    grad_qkv = at[:, :, :, half:].transpose(0, 2, 1, 3).reshape(LAYERS, one, 3 * width).astype(f32)

    return (
        last,
        g0,
        grad_table,
        a_gain,
        a_shift,
        grad_qkv,
        a_qv,
        grad_out,
        a_out,
        m_gain,
        m_shift,
        grad_up,
        m_up,
        grad_down,
        m_down,
    )


def solution(mesh):
    rows = P(("dp", "section"), None)
    in_specs = (rows,) * 4 + (P(),) * 13
    flat, deep = P(None, "dp"), P(None, "dp", None)
    out_specs = (rows, rows) + (flat, flat, flat, deep, flat, deep, flat, flat, flat, deep, flat, deep, flat)
    return jax.shard_map(local, mesh=mesh, in_specs=in_specs, out_specs=out_specs, check_vma=False)
```

```python
import functools

import jax
import jax.numpy as jnp
from jax import lax
from jax.experimental import pallas as pl
from jax.experimental.pallas import tpu as pltpu
from jax.sharding import PartitionSpec as P

HDIM = 64
PAIR = 2 * HDIM
LAYERS = 2
BLOCK = 768
LIMIT = 60 * 1024 * 1024

epsilon = 1e-05
masked_score = -1000000000.0
scale = HDIM ** (-0.5)
f32 = jnp.float32
bf16 = jnp.bfloat16
ANY = pl.BlockSpec(memory_space=pl.ANY)
VMEM = pl.BlockSpec(memory_space=pltpu.VMEM)
SMEM = pl.BlockSpec(memory_space=pltpu.SMEM)


def mm(a, b):
    return lax.dot_general(a, b, (((1,), (0,)), ((), ())), preferred_element_type=f32)


def mm_nt(a, b):
    return lax.dot_general(a, b, (((1,), (1,)), ((), ())), preferred_element_type=f32)


def cols(n, size=BLOCK):
    return pl.ds(n * size, size)


rows_of = cols


def loop(count, body):
    for n in range(count):
        body(n)


class Copies:
    def __init__(self, sems):
        self.sems, self.used, self.pending = sems, 0, []

    def start(self, source, target):
        copy = pltpu.make_async_copy(source, target, self.sems.at[self.used])
        self.used += 1
        copy.start()
        return copy

    def send(self, source, target):
        self.pending.append(self.start(source, target))

    def finish(self):
        for copy in self.pending:
            copy.wait()


def norm_stats(hidden):
    full = hidden.astype(f32)
    centered = full - jnp.mean(full, axis=-1, keepdims=True)
    rstd = lax.rsqrt(jnp.mean(centered * centered, axis=-1, keepdims=True) + epsilon)
    return centered * rstd, rstd


def norm_forward(hidden, gain, shift):
    xhat, rstd = norm_stats(hidden)
    return (xhat * gain.astype(f32) + shift.astype(f32)).astype(bf16)


def gelu_pair(u):
    c, a = 0.7978845608028654, 0.044715
    square = u * u
    t = jnp.tanh(c * u * (1.0 + a * square))
    half = 0.5 * (1.0 + t)
    slope = half + 0.5 * u * (1.0 - t * t) * (c * (1.0 + 3.0 * a * square))
    return u * half, slope


def doc_mask(bounds, rows):
    one = lax.broadcasted_iota(jnp.int32, (rows, rows), 0)
    other = lax.broadcasted_iota(jnp.int32, (rows, rows), 1)
    left = sum((one >= b).astype(jnp.int32) for b in bounds)
    right = sum((other >= b).astype(jnp.int32) for b in bounds)
    return left == right


def bounds_of(len_ref):
    bounds, total = [], 0
    for k in range(len_ref.shape[1] - 1):
        total = total + len_ref[0, k]
        bounds.append(total)
    return bounds


def halves(x):
    low = lax.broadcasted_iota(jnp.int32, x.shape, 1) < HDIM
    zero = jnp.zeros_like(x)
    return jnp.where(low, x, zero), jnp.where(low, zero, x)


def soft_columns(key, query, same):
    s = jnp.where(same, mm_nt(key, query) * scale, masked_score)
    e = jnp.exp(s - jnp.max(s, axis=0, keepdims=True))
    return e * (1.0 / jnp.sum(e, axis=0, keepdims=True))


def qkv_forward(normed, weight, bias_ref, bias_row, target):
    width = normed.shape[1]
    per = width // BLOCK

    def part(base, bias_base):
        def body(n):
            at = cols(n + base * per)
            out = mm(normed, weight[:, at])
            if bias_base is not None:
                out = out + bias_ref[bias_row, cols(n + bias_base * per)].astype(f32)
            target[:, at] = out.astype(bf16)

        loop(per, body)

    part(0, 0)
    part(1, None)
    part(2, 1)


def attend_context(mixed, same_ref, target):
    width = mixed.shape[1] // 3
    count = width // PAIR

    def body(p):
        q = mixed[:, cols(p, PAIR)]
        k = mixed[:, cols(p + count, PAIR)]
        v = mixed[:, cols(p + 2 * count, PAIR)]
        same = same_ref[...] > 0.5
        total = None
        for key, value in zip(halves(k), halves(v)):
            s = jnp.where(same, mm_nt(q, key) * scale, masked_score)
            e = jnp.exp(s - jnp.max(s, axis=1, keepdims=True))
            piece = mm(e.astype(bf16), value) * (1.0 / jnp.sum(e, axis=1, keepdims=True))
            total = piece if total is None else total + piece
        target[:, cols(p, PAIR)] = total.astype(bf16)

    loop(count, body)


def attend_grad(mixed, same_ref, dcontext, target, context=None):
    width = mixed.shape[1] // 3
    count = width // PAIR

    def body(p):
        q = mixed[:, cols(p, PAIR)]
        k = mixed[:, cols(p + count, PAIR)]
        v = mixed[:, cols(p + 2 * count, PAIR)]
        d = dcontext[:, cols(p, PAIR)]
        same = same_ref[...] > 0.5
        dq = dk = dv = ctx = 0.0
        for key, value, query, dc in zip(halves(k), halves(v), halves(q), halves(d)):
            soft = soft_columns(key, q, same)
            probs = soft.astype(bf16)
            dsoft = mm_nt(value, d)
            inner = jnp.sum(soft * dsoft, axis=0, keepdims=True)
            dscores = (soft * (dsoft - inner)).astype(bf16)
            dv = dv + mm(probs, dc)
            dk = dk + mm(dscores, query)
            dq = dq + mm(key.T, dscores)
            if context is not None:
                ctx = ctx + mm(value.T, probs)
        target[:, cols(p, PAIR)] = (dq * scale).T.astype(bf16)
        target[:, cols(p + count, PAIR)] = (dk * scale).astype(bf16)
        target[:, cols(p + 2 * count, PAIR)] = dv.astype(bf16)
        if context is not None:
            context[:, cols(p, PAIR)] = ctx.T.astype(bf16)

    loop(count, body)


def forward_kernel(
    bits, lengths, timesteps, inputs, a_gain, a_shift, qv, out_b, m_gain, m_shift, up_b, down_b,
    cotangent, table, qkv_w, out_w, up_w, down_w,
    x1, h0, h1, h3, last, na, mixed, ctx, nm, act, slope, dinner, dmixed, g2, g3, vec,
    v_table, v_qkv, v_out, v_up, v_down, v_h, v_na, v_mixed, v_ctx, v_nm, v_act, v_slope, v_x, v_g,
    v_dinner, v_dctx, v_dmixed, v_dn, v_gmid, v_gout, same, sems,
):
    copies = Copies(sems)
    rows, width = inputs.shape
    wide = up_w.shape[2]
    docs = lengths.shape[1]
    l_table = copies.start(table, v_table)
    loads = []
    for l in range(LAYERS):
        loads.append(
            [
                copies.start(w.at[l], v.at[l])
                for w, v in ((qkv_w, v_qkv), (out_w, v_out), (up_w, v_up), (down_w, v_down))
            ]
        )
    l_g = copies.start(cotangent, v_g)
    bounds = bounds_of(lengths)
    same[...] = doc_mask(bounds, rows).astype(f32)
    tail = x1.shape[0] - rows
    which = lax.broadcasted_iota(jnp.int32, (tail, width), 0)
    note = jnp.zeros((tail, width), f32)
    for k, bound in enumerate(bounds):
        note = jnp.where(which == k, bound.astype(f32), note)
    v_x[...] = note.astype(bf16)
    copies.send(v_x, x1.at[pl.ds(rows, tail)])
    steps = table.shape[0]
    doc = lax.broadcasted_iota(jnp.int32, (16, steps), 0)
    wanted = jnp.full((16, steps), -1, jnp.int32)
    for k in range(docs):
        wanted = jnp.where(doc == k, timesteps[0, k], wanted)
    step = lax.broadcasted_iota(jnp.int32, (16, steps), 1)
    onehot = (step == wanted).astype(f32).astype(bf16)
    token = lax.broadcasted_iota(jnp.int32, (rows, 16), 0)
    own = sum((token >= bound).astype(jnp.int32) for bound in bounds)
    chosen = (own == lax.broadcasted_iota(jnp.int32, (rows, 16), 1)).astype(f32).astype(bf16)
    l_table.wait()
    embedded = mm(chosen, mm(onehot, v_table[...]).astype(bf16))
    v_h[0] = (inputs[...].astype(f32) + embedded).astype(bf16)
    for l in range(LAYERS):
        h_in, h_mid = v_h.at[2 * l], v_h.at[2 * l + 1]
        h_out = v_h.at[2 * l + 2]
        v_na[l] = norm_forward(h_in[...], a_gain[l : l + 1, :], a_shift[l : l + 1, :])
        loads[l][0].wait()
        qkv_forward(v_na[l], v_qkv.at[l], qv, slice(l, l + 1), v_mixed.at[l])
        copies.send(v_na.at[l], na.at[l])
        if l == 0:
            copies.send(v_mixed.at[l], mixed)
        attend_context(v_mixed.at[l], same, v_ctx.at[l])
        copies.send(v_ctx.at[l], ctx.at[l])
        loads[l][1].wait()

        def project(n):
            at = cols(n)
            out = h_in[:, at].astype(f32) + mm(v_ctx[l], v_out[l, :, at])
            h_mid[:, at] = (out + out_b[l : l + 1, at].astype(f32)).astype(bf16)

        loop(width // BLOCK, project)
        v_nm[l] = norm_forward(h_mid[...], m_gain[l : l + 1, :], m_shift[l : l + 1, :])
        copies.send(v_nm.at[l], nm.at[l])
        loads[l][2].wait()

        def expand(n):
            at = cols(n)
            inner = mm(v_nm[l], v_up[l, :, at]) + up_b[l : l + 1, at].astype(f32)
            active, s = gelu_pair(inner)
            v_act[l, :, at] = active.astype(bf16)
            v_slope[l, :, at] = s.astype(bf16)

        loop(wide // BLOCK, expand)
        copies.send(v_act.at[l], act.at[l])
        if l == 0:
            copies.send(v_slope.at[l], slope)
        loads[l][3].wait()

        def contract(n):
            at = cols(n)
            out = h_mid[:, at].astype(f32) + mm(v_act[l], v_down[l, :, at])
            h_out[:, at] = (out + down_b[l : l + 1, at].astype(f32)).astype(bf16)

        loop(width // BLOCK, contract)
    for k, h in ((0, h0), (1, h1), (3, h3), (4, last)):
        copies.send(v_h.at[k], h)
    by_x = jnp.where(bits[0] == 0, 2, 0)
    copies.send(v_h.at[by_x], x1.at[pl.ds(0, rows)])
    l_g.wait()
    l = LAYERS - 1
    backward_part(
        l, copies, v_g, a_gain, m_gain, v_h.at[2 * l], v_h.at[2 * l + 1], v_mixed.at[l], v_slope.at[l],
        same, (v_qkv.at[l], v_out.at[l], v_up.at[l], v_down.at[l]), lambda *name: None, vec,
        dinner.at[l], dmixed.at[l], v_dinner, v_dmixed, v_dctx, v_dn, v_gmid, v_gout,
    )
    copies.send(v_gmid, g3)
    copies.send(v_gout, g2)
    copies.finish()


def norm_backward(h, gain, dnormed, upstream, vec, at_gain, at_shift, target):
    width = h.shape[1]
    xhat, rstd = norm_stats(h[...])
    dn = dnormed[...]
    e = dn * gain.astype(f32)
    grad = (
        e - jnp.mean(e, axis=-1, keepdims=True) - xhat * jnp.mean(e * xhat, axis=-1, keepdims=True)
    ) * rstd
    target[...] = (upstream[...].astype(f32) + grad).astype(bf16)
    vec[:, at_gain : at_gain + width] = jnp.sum(dn * xhat, axis=0, keepdims=True)
    vec[:, at_shift : at_shift + width] = jnp.sum(dn, axis=0, keepdims=True)


def colsum(x):
    return jnp.sum(x.astype(f32), axis=0, keepdims=True)


def write_notes(me, timesteps, vectors, doc_sums, notes):
    _, _, shares, ahead, width = notes.shape
    docs = timesteps.shape[1]
    one = width // shares
    per = width // one
    for core, vec in enumerate(vectors):
        count = vec.shape[1] // width
        rows = [vec[:, k * width : (k + 1) * width] for k in range(count)]
        rows.append(jnp.zeros((ahead - count, width), f32))
        value = jnp.concatenate(rows, axis=0).astype(bf16)
        for s in range(shares):
            notes[core, 0, s] = value
    row = lax.broadcasted_iota(jnp.int32, (ahead, width), 0)
    lane = lax.broadcasted_iota(jnp.int32, (ahead, width), 1)
    docs_rows = notes_rows(shares, docs, width)
    marks = jnp.zeros((ahead, width), f32)
    sums = [jnp.zeros((ahead, width), f32) for _ in range(shares)]
    for k in range(docs):
        number = me * docs + k
        r, j = number // per, number % per
        step = timesteps[0, k]
        here = lane == j * docs_rows + r
        marks = jnp.where(here & (row == 0), (step // 32).astype(f32), marks)
        marks = jnp.where(here & (row == 1), (step % 32).astype(f32), marks)
        here = (row == r) & (lane >= j * one) & (lane < (j + 1) * one)
        wide = jnp.broadcast_to(doc_sums[k : k + 1, :], (8, width))
        for s in range(shares):
            turned = pltpu.roll(wide, lax.rem((j - s) * one + width, width), 1)
            turned = jnp.broadcast_to(turned[:1], (ahead, width))
            sums[s] = jnp.where(here, turned, sums[s])
    for s in range(shares):
        notes[0, 1, s] = sums[s].astype(bf16)
        notes[1, 1, s] = marks.astype(bf16)


def notes_rows(shares, docs, width):
    return 4 * shares * docs * (width // shares) // width


def backward_part(
    layer, copies, g, a_gain, m_gain, h_a, h_m, mixed, slope, same, weights, wait, vec, dinner, dmixed,
    v_dinner, v_dmixed, v_dctx, v_dn, v_gmid, v_gout,
):
    v_qkv, v_out, v_up, v_down = weights
    rows, width = g.shape
    wide = v_up.shape[1]
    one_row = slice(layer, layer + 1)
    at_qv, at_mshift, at_downb, at_upb = 4 * width, 6 * width, 7 * width, 8 * width
    vec[:, at_downb : at_downb + width] = colsum(g[...])
    wait("slope")
    for n in range(wide // BLOCK):
        wait("down", n)
        at = cols(n)
        dact = mm_nt(g[...], v_down[at, :])
        di = (dact * slope[:, at].astype(f32)).astype(bf16)
        v_dinner[:, at] = di
        vec[:, at_upb + n * BLOCK : at_upb + (n + 1) * BLOCK] = colsum(di)
    copies.send(v_dinner, dinner)
    wait("up")
    v_dn[...] = mm_nt(v_dinner[...], v_up[...])
    wait("h_m")
    norm_backward(h_m, m_gain[one_row, :], v_dn, g, vec, 3 * width, at_mshift, v_gmid)
    vec[:, 2 * width : 3 * width] = colsum(v_gmid[...])
    wait("out")
    v_dctx[...] = mm_nt(v_gmid[...], v_out[...]).astype(bf16)
    wait("mixed")
    attend_grad(mixed, same, v_dctx, v_dmixed)
    copies.send(v_dmixed, dmixed)
    vec[:, at_qv : at_qv + width] = colsum(v_dmixed[:, :width])
    vec[:, at_qv + width : at_qv + 2 * width] = colsum(v_dmixed[:, 2 * width :])
    wait("qkv")
    v_dn[...] = mm_nt(v_dmixed[...], v_qkv[...])
    wait("h_a")
    norm_backward(h_a, a_gain[one_row, :], v_dn, v_gmid, vec, 0, width, v_gout)


def backward_kernel(
    bits, lengths, timesteps, a_gain, m_gain, vec_upper, g, g_upper, h_a, h_m, mixed, slope,
    qkv_w, out_w, up_w, down_w, _, __,
    dinner, dmixed, g_out, send, own, notes,
    v_qkv, v_out, v_up, v_down, v_g, v_ha, v_hm, v_mixed, v_slope, v_dinner, v_dctx, v_dmixed, v_dn,
    v_gmid, v_gout, v_trade, v_notes, vec, same, sems,
):
    copies = Copies(sems)
    rows, width = h_a.shape
    wide = up_w.shape[2]
    l_g = copies.start(g, v_g)
    loads = {"slope": copies.start(slope, v_slope)}
    for n in range(wide // BLOCK):
        loads["down", n] = copies.start(down_w.at[0, cols(n)], v_down.at[cols(n)])
    for name, source, target in (
        ("up", up_w.at[0], v_up), ("h_m", h_m, v_hm), ("out", out_w.at[0], v_out), ("mixed", mixed, v_mixed),
        ("qkv", qkv_w.at[0], v_qkv), ("h_a", h_a, v_ha), ("g_upper", g_upper, v_trade.at[0]),
    ):
        loads[name] = copies.start(source, target)
    wait = lambda *name: loads[name if len(name) > 1 else name[0]].wait()
    same[...] = doc_mask(bounds_of(lengths), rows).astype(f32)
    l_g.wait()
    backward_part(
        0, copies, v_g, a_gain, m_gain, v_ha, v_hm, v_mixed, v_slope, same, (v_qkv, v_out, v_up, v_down),
        wait, vec, dinner.at[0], dmixed.at[0], v_dinner, v_dmixed, v_dctx, v_dn, v_gmid, v_gout,
    )
    copies.send(v_gout, g_out)
    v_trade[1] = v_gmid[...]
    wait("g_upper")
    copies.send(v_trade.at[bits[0]], send)
    copies.send(v_trade.at[1 - bits[0]], own)
    count = lengths.shape[1]
    doc = lax.broadcasted_iota(jnp.int32, (16, rows), 0)
    token = lax.broadcasted_iota(jnp.int32, (16, rows), 1)
    index = sum((token >= bound).astype(jnp.int32) for bound in bounds_of(lengths))
    onehot = ((index == doc) & (doc < count)).astype(f32).astype(bf16)
    doc_sums = mm(onehot, v_gout[...])
    write_notes(bits[3], timesteps, (vec, vec_upper), doc_sums, v_notes)
    copies.send(v_notes, notes)
    copies.finish()


def pick_layer(ref, layer, at=slice(None)):
    return jnp.where(layer == 0, ref[0:1, at].astype(f32), ref[1:2, at].astype(f32))


def feed_weight_kernel(
    layer, bits, h, g, own_g, own_act, own_nm, own_dinner, gain, shift, up_b, up_w, down_w, *rest
):
    *outs, v_up, v_down, v_nm, v_own, v_g, v_n, v_act, v_dinner, v_send, v_keep, sems = rest
    copies = Copies(sems)
    rows, width = h.shape
    wide = up_w.shape[2]
    quarter = width // 4
    side, core = bits[1], bits[2]
    one_row = slice(layer, layer + 1)
    l_nm = copies.start(own_nm.at[layer], v_own)
    order = [2 * side + 1 - core, 2 * side + core, 2 - 2 * side, 3 - 2 * side]
    size = wide // 4
    loads = []
    for n, block in enumerate(order):
        at = pl.ds(pl.multiple_of(block * size, 128), size)
        load = [copies.start(up_w.at[layer, :, at], v_up.at[n])]
        if n < 2:
            load.append(copies.start(down_w.at[layer, at], v_down.at[n]))
        load.append(copies.start(own_act.at[layer, :, at], v_act.at[n, pl.ds(0, rows)]))
        if n < 2:
            load.append(copies.start(own_dinner.at[layer, :, at], v_dinner.at[n, pl.ds(0, rows)]))
        loads.append(load)
    normed = norm_forward(h[...], gain[one_row, :], shift[one_row, :])
    v_nm[...] = normed
    v_n[:, rows:] = normed.T
    for k in range(2):
        part = 2 * side + (1 - core if k == 0 else core)
        at = pl.ds(pl.multiple_of(part * quarter // 128 * 128, 128), 2 * 128)
        for ref, first in ((own_g, 0), (g, rows)):
            piece = ref[:, at].T
            shifted = jnp.where(part % 2 == 0, piece[:quarter].astype(f32), piece[256 - quarter :].astype(f32))
            v_g[k * quarter : (k + 1) * quarter, first : first + rows] = shifted.astype(bf16)
    l_nm.wait()
    v_n[:, :rows] = v_own[...].T
    flat = len(v_send.shape) == 2
    for n, block in enumerate(order):
        for load in loads[n]:
            load.wait()
        at = pl.ds(pl.multiple_of(block * size, 128), size)
        inner = mm(v_nm[...], v_up[n]) + up_b[one_row, at].astype(f32)
        active, slope = gelu_pair(inner)
        v_act[n, rows:] = active.astype(bf16)
        down = mm(v_g[...], v_act[n]).astype(bf16)
        for k, target in ((0, v_send), (1, v_keep)):
            half = down[k * quarter : (k + 1) * quarter]
            if flat:
                target[:quarter, at] = half
            else:
                shares, _, one, _ = target.shape
                share = wide // shares
                for m in range(size // share):
                    for p in range(quarter // one):
                        piece = half[p * one : (p + 1) * one, m * share : (m + 1) * share]
                        target[block * (size // share) + m, 0, :, p * share : (p + 1) * share] = piece
        if n < 2:
            dact = mm_nt(g[...], v_down[n])
            v_dinner[n, rows:] = (dact * slope).astype(bf16)
            up = mm(v_n[...], v_dinner[n]).astype(bf16)
            target = v_send if n == 0 else v_keep
            if flat:
                target[quarter:, :size] = up
            else:
                shares, _, one, _ = target.shape
                for m in range(shares):
                    target[m, 1] = up[m * one : (m + 1) * one]
    copies.send(v_send, outs[-2])
    copies.send(v_keep, outs[-1])
    copies.finish()


def attend_weight_kernel(
    bits, hx, g, own_g, own_na, own_ctx, own_dmixed, notes, gain, shift, qv, qkv_w, out_w,
    send, keep,
    v_qkv, v_out, v_na, v_mixed, v_dctx, v_dmixed, v_ctx, v_left, v_right, v_own, v_own_ctx,
    v_own_dmixed, v_bias, v_send, v_keep, same, sems,
):
    copies = Copies(sems)
    rows, width = g.shape
    layer, core = bits[0], bits[2]
    l_qkv = copies.start(qkv_w.at[layer], v_qkv)
    l_out = copies.start(out_w.at[layer], v_out)
    l_ctx = copies.start(own_ctx.at[layer], v_own_ctx)
    l_own = copies.start(own_na.at[layer], v_own)
    l_dmixed = copies.start(own_dmixed.at[layer], v_own_dmixed)
    note = hx[rows:, :].astype(f32)
    bounds = [note[k : k + 1, :rows].astype(jnp.int32) for k in range(2)]
    same[...] = doc_mask(bounds, rows).astype(f32)
    v_bias[...] = pick_layer(qv, layer)
    v_na[...] = norm_forward(hx[:rows, :], pick_layer(gain, layer), pick_layer(shift, layer))
    l_qkv.wait()
    qkv_forward(v_na[...], v_qkv, v_bias, slice(0, 1), v_mixed)
    l_out.wait()

    def back_out(n):
        v_dctx[:, cols(n)] = mm_nt(g[...], v_out[rows_of(n), :]).astype(bf16)

    loop(width // BLOCK, back_out)
    attend_grad(v_mixed, same, v_dctx, v_dmixed, v_ctx)
    part = width // 2
    shares, ahead = notes.shape[2], notes.shape[3]
    share = width // shares

    def put(target, k, n, out):
        for s in range(shares):
            piece = out[s * share : (s + 1) * share].astype(bf16)
            target[n // 2, s, ahead:, (n % 2) * part : (n % 2 + 1) * part] = piece

    for k in range(2):
        target = v_send if k == 0 else v_keep
        target[:, :, :ahead] = notes[1 - core if k == 0 else core]
    l_ctx.wait()
    v_left[:, :rows] = v_own_ctx[...].T
    v_left[:, rows:] = v_ctx[...].T
    for k in range(2):
        side = jnp.where(k == 0, 1 - core, core)
        at = pl.ds(pl.multiple_of(side * part, 128), part)
        v_right[k, :rows, :part] = own_g[:, at]
        v_right[k, rows:, :part] = g[:, at]
        put(v_send if k == 0 else v_keep, k, 0, mm(v_left[...], v_right[k, :, :part]))
    l_own.wait()
    l_dmixed.wait()
    v_left[:, :rows] = v_own[...].T
    v_left[:, rows:] = v_na[...].T
    for k in range(2):
        side = jnp.where(k == 0, 1 - core, core)
        target = v_send if k == 0 else v_keep
        at = pl.ds(pl.multiple_of(side * 3 * part, 128), 3 * part)
        v_right[k, :rows] = v_own_dmixed[:, at]
        v_right[k, rows:] = v_dmixed[:, at]
        out = mm(v_left[...], v_right[k])
        for n in range(1, 4):
            put(target, k, n, out[:, (n - 1) * part : n * part])
        copies.send(target, send if k == 0 else keep)
    copies.finish()


def feed_finish_kernel(layer, bits, own, other, beside, *rest):
    up_out, down_out, v_up, v_down, sems = rest[-5:]
    copies = Copies(sems)
    side, core = bits[1], bits[2]
    rows, width = own.shape[1:]
    share, quarter = v_down.shape[0], width // 4
    pieces = width // share
    for ref, chip, half in (
        (own, side, core), (other, 1 - side, core), (beside.at[0], side, 1 - core), (beside.at[1], 1 - side, 1 - core)
    ):
        part = 2 * chip + half
        v_up[:, pl.ds(pl.multiple_of(part * width, 128), width)] = ref[1].astype(f32)
        down = jnp.concatenate(
            [ref[0, :, p * share : (p + 1) * share].astype(f32) for p in range(pieces)], axis=0
        ).T
        for at in range(4):

            @pl.when(part == at)
            def _():
                v_down[:, at * quarter : (at + 1) * quarter] = down

    copies.send(v_up, up_out.at[layer])
    copies.send(v_down, down_out.at[layer])
    copies.finish()


def attend_finish_kernel(
    ahead, docs_rows, bits, own, other, beside,
    table, a_gain, a_shift, qkv, a_qv, out, a_out, m_gain, m_shift, m_up, m_down, notes, sums,
):
    place_x, side, core = bits[0], bits[1], bits[2]
    width = own.shape[2]
    part = width // 2

    def put(ref, first, which):
        for relative in range(2):
            layer = jnp.where(relative == 0, place_x, 1 - place_x)
            value = ref[relative, ahead:, :].astype(f32)
            base = 3 * part * which
            if first:
                out[layer, :, pl.ds(pl.multiple_of(which * part, 128), part)] = value[:, :part]
                qkv[layer, :, pl.ds(pl.multiple_of(base, 128), part)] = value[:, part:]
            else:
                qkv[layer, :, pl.ds(pl.multiple_of(base + part, 128), width)] = value

    def note(ref, which, half):
        notes[which, half] = ref[0, :ahead, :].astype(f32) + ref[1, :ahead, :].astype(f32)

    for half in range(2):
        for here, mine in ((own, 0), (other, 1)):

            @pl.when((side == half) == (mine == 0))
            def _():
                put(here, half == 0, core)
                put(beside.at[mine], half == 0, 1 - core)

                note(here, core, half)
                note(beside.at[mine], 1 - core, half)

    index = bits[4]
    one = a_gain.shape[1]
    for l in range(LAYERS):
        value = notes[l, 0]
        at = 0
        for ref in (a_gain, a_shift, a_out, m_gain, a_qv, m_shift, m_down, m_up):
            size = ref.shape[1]
            count = size // one
            place = index * size
            line = value[at : at + 1]
            for k in range(1, count):
                line = jnp.where(place // width == k, value[at + k : at + k + 1], line)
            line = jnp.broadcast_to(line, (8, width))
            turned = pltpu.roll(line, lax.rem(width - lax.rem(place, width), width), 1)
            ref[l : l + 1, :] = turned[:1, :size]
            at += count
    per, count = width // one, (width // one) * docs_rows
    high, low = notes[1, 1, 0:1, :count], notes[1, 1, 1:2, :count]
    steps = (high * 32.0 + low).astype(jnp.int32)
    for j in range(per):
        sums[j * docs_rows : (j + 1) * docs_rows, :] = notes[0, 1, :docs_rows, j * one : (j + 1) * one]
    step = lax.broadcasted_iota(jnp.int32, (table.shape[1], count), 0)
    onehot = (step == steps).astype(f32).astype(bf16)
    table[...] = mm_nt(sums[...].T.astype(bf16), onehot)


def call(kernel, operands, specs, outs, out_specs, scratch, copies, aliases=None):
    return pl.pallas_call(
        kernel,
        out_shape=[jax.ShapeDtypeStruct(s, d) for s, d in outs],
        in_specs=specs,
        out_specs=out_specs,
        scratch_shapes=[pltpu.VMEM(s, d) for s, d in scratch]
        + [pltpu.SemaphoreType.DMA((copies,))] * (copies > 0),
        input_output_aliases=aliases or {},
        compiler_params=pltpu.CompilerParams(vmem_limit_bytes=LIMIT),
        cost_estimate=pl.CostEstimate(flops=0, bytes_accessed=0, transcendentals=0),
    )(*operands)


def swap(x, axis, by):
    size = lax.axis_size(axis)
    return lax.ppermute(x, axis, [(i, i ^ by) for i in range(size)])


def plus(a, b):
    return (a.astype(f32) + b.astype(f32)).astype(bf16)


def after(x, *others):
    return lax.optimization_barrier((x,) + others)[0] if others else x


class Ring:
    def __init__(self, term, place_z, nx, nz):
        self.term, self.place_z, self.nx, self.nz = term, place_z, nx, nz
        if nz > 4:
            groups = [[z * nx + x for z in range(nz)] for x in range(nx)]
            held = jnp.stack([term(z) for z in range(nz)]).astype(bf16)
            self.carry = lax.psum_scatter(held, "dp", scatter_dimension=0, axis_index_groups=groups)
            self.at = nz
        else:
            self.carry = term((place_z - 1) % nz).astype(bf16)
            self.at = 1

    def step(self, *others):
        if self.at < self.nz:
            self.at += 1
            size = self.nx * self.nz
            got = lax.ppermute(self.carry, "dp", [(d, (d + self.nx) % size) for d in range(size)])
            got = after(got, *others)
            self.carry = (got.astype(f32) + self.term((self.place_z - self.at) % self.nz)).astype(bf16)

    def finish(self, *others):
        while self.at < self.nz:
            self.step(*others)
        return self.carry


def at(x, *index):
    start = tuple(index) + (0,) * (x.ndim - len(index))
    size = (1,) * len(index) + x.shape[len(index) :]
    return lax.dynamic_slice(x, start, size).reshape(x.shape[len(index) :]).astype(f32)


def lead(x, index, axis):
    return lax.dynamic_index_in_dim(x, index, axis, keepdims=False).astype(f32)


def local(
    inputs,
    timesteps,
    lengths,
    cotangent,
    time_table,
    attn_norm_gain,
    attn_norm_bias,
    qkv_weight,
    qv_bias,
    out_weight,
    out_bias,
    mlp_norm_gain,
    mlp_norm_bias,
    up_weight,
    up_bias,
    down_weight,
    down_bias,
):
    place = lax.axis_index("section")
    side, core = place // 2, place % 2
    dp = lax.axis_size("dp")
    nx, nz = 2, dp // 2
    index = lax.axis_index("dp")
    place_z, place_x = index // nx, index % nx
    rows, width = inputs.shape
    wide = up_weight.shape[2]
    docs = lengths.shape[1]
    step_count = time_table.shape[0]
    me = index * lax.axis_size("section") + place
    bits = jnp.stack([place_x, side, core, me, index]).astype(jnp.int32)

    ahead, docs_rows = 16, notes_rows(dp, docs, width)
    tok, tok2 = (rows, width), (LAYERS, rows, width)
    peer_cot = swap(cotangent, "section", 2)
    full, thrice = ((LAYERS, rows, wide), bf16), ((LAYERS, rows, 3 * width), bf16)
    x1, h0, h1, h3, last, na, mixed, ctx, nm, act, slope, dinner, dmixed, g2, g3, vec1 = call(
        forward_kernel,
        [bits, lengths, timesteps, inputs, attn_norm_gain, attn_norm_bias, qv_bias, out_bias,
         mlp_norm_gain, mlp_norm_bias, up_bias, down_bias, cotangent, time_table, qkv_weight, out_weight,
         up_weight, down_weight],
        [SMEM] * 3 + [VMEM] * 9 + [ANY] * 6,
        [((rows + 16, width), bf16)] + [(tok, bf16)] * 4
        + [(tok2, bf16), ((rows, 3 * width), bf16), (tok2, bf16), (tok2, bf16), full,
           ((rows, wide), bf16), full, thrice, (tok, bf16), (tok, bf16), ((1, 12 * width), f32)],
        [ANY] * 15 + [VMEM],
        [(time_table.shape, bf16), (qkv_weight.shape, bf16), (out_weight.shape, bf16),
         (up_weight.shape, bf16), (down_weight.shape, bf16), ((2 * LAYERS + 1,) + tok, bf16),
         (tok2, bf16), thrice, (tok2, bf16), (tok2, bf16), full, full, ((16, width), bf16), (tok, bf16),
         ((rows, wide), bf16), (tok, bf16), ((rows, 3 * width), bf16), (tok, f32), (tok, bf16), (tok, bf16),
         ((rows, rows), f32)],
        40,
    )
    peer_h3 = swap(h3, "section", 2)
    peer_h1 = swap(h1, "section", 2)
    peer_hx = swap(x1, "dp", 1)
    peer_g2 = swap(g2, "section", 2)
    dinner, dmixed, g0, x2, own_ga, notes = call(
        backward_kernel,
        [bits, lengths, timesteps, attn_norm_gain, mlp_norm_gain, vec1, g2, g3, h0, h1, mixed, slope,
         qkv_weight, out_weight, up_weight, down_weight, dinner, dmixed],
        [SMEM] * 3 + [VMEM] * 3 + [ANY] * 12,
        [full, thrice, (tok, bf16), (tok, bf16), (tok, bf16), ((2, 2, dp, ahead, width), bf16)],
        [ANY] * 6,
        [(qkv_weight.shape[1:], bf16), (out_weight.shape[1:], bf16), (up_weight.shape[1:], bf16),
         (down_weight.shape[1:], bf16), (tok, bf16), (tok, bf16), (tok, bf16), ((rows, 3 * width), bf16),
         ((rows, wide), bf16), ((rows, wide), bf16), (tok, bf16), ((rows, 3 * width), bf16), (tok, f32),
         (tok, bf16), (tok, bf16), ((2,) + tok, bf16), ((2, 2, dp, ahead, width), bf16),
         ((1, 12 * width), f32), ((rows, rows), f32)],
        24,
        {16: 0, 17: 1},
    )
    peer_ga = swap(x2, "dp", 1)

    share, one, half, quarter = wide // dp, width // dp, width // 2, width // 4
    flat = share % 128 != 0

    def feed_weight(layer, h, g, own_g):
        shape = (quarter + width, wide) if flat else (dp, 2, one, width)
        send, keep = call(
            functools.partial(feed_weight_kernel, layer),
            [bits, h, g, own_g, act, nm, dinner, mlp_norm_gain, mlp_norm_bias, up_bias, up_weight,
             down_weight],
            [SMEM, VMEM, VMEM, VMEM, ANY, ANY, ANY, VMEM, VMEM, VMEM, ANY, ANY],
            [(shape, bf16)] * 2,
            [ANY] * 2,
            [((4, width, wide // 4), bf16), ((2, wide // 4, width), bf16), (tok, bf16), (tok, bf16),
             ((2 * quarter, 2 * rows), bf16), ((width, 2 * rows), bf16),
             ((4, 2 * rows, wide // 4), bf16), ((2, 2 * rows, wide // 4), bf16),
             (shape, bf16), (shape, bf16)],
            20,
        )
        if flat:

            def sort(x):
                down = x[:quarter].reshape(-1, one, dp, share).transpose(2, 1, 0, 3)
                return jnp.stack([down.reshape(dp, one, width), x[quarter:, :width].reshape(dp, one, width)], axis=1)

            send, keep = sort(send), sort(keep)
        split = lambda x: x.reshape(nz, nx, 2, one, width)
        return split(keep), split(send)

    def trade(keep, send, *others):
        return keep, swap(after(send, *others), "section", 1)

    def own_part(keep, near, axis, index, *others):
        return lead(keep, index, axis) + lead(after(near, *others), index, axis)

    keep1, send1 = feed_weight(1, peer_h3, peer_cot, after(cotangent, g0, peer_hx))
    keep1, near1 = trade(keep1, send1, peer_ga, peer_h1, peer_g2)
    ring1 = Ring(lambda z: own_part(keep1, near1, 0, z), place_z, nx, nz)

    at_send, at_keep = call(
        attend_weight_kernel,
        [bits, after(peer_hx, ring1.carry), peer_ga, own_ga, na, ctx, dmixed, notes, attn_norm_gain, attn_norm_bias,
         qv_bias, qkv_weight, out_weight],
        [SMEM, VMEM, VMEM, VMEM, ANY, ANY, ANY, VMEM, VMEM, VMEM, VMEM, ANY, ANY],
        [((2, dp, ahead + one, width), bf16)] * 2,
        [ANY] * 2,
        [((width, 3 * width), bf16), ((width, width), bf16), (tok, bf16), ((rows, 3 * width), bf16),
         (tok, bf16), ((rows, 3 * width), bf16), (tok, bf16), ((width, 2 * rows), bf16),
         ((2, 2 * rows, 3 * half), bf16), (tok, bf16), (tok, bf16), ((rows, 3 * width), bf16),
         ((1, 2 * width), f32), ((2, dp, ahead + one, width), bf16),
         ((2, dp, ahead + one, width), bf16), ((rows, rows), f32)],
        8,
    )

    ring1.step(at_keep)
    split = lambda x: x.reshape(2, nz, nx, ahead + one, width)
    keep_a, near_a = trade(split(at_keep), split(at_send), ring1.carry)
    away_a = own_part(keep_a, near_a, 0, 1 - side).astype(bf16)
    far_a = swap(away_a, "section", 2)
    keep0, send0 = feed_weight(0, after(peer_h1, away_a, ring1.carry), peer_g2, g2)
    ring1.step(keep0)
    keep0, near0 = trade(keep0, send0, ring1.carry)
    away0 = own_part(keep0, near0, 1, 1 - place_x).astype(bf16)
    far0 = swap(away0, "dp", 1)
    ring1.finish(away0)
    far_a = after(far_a, away0)
    ring_a = Ring(
        lambda z: at(keep_a, side, z) + at(near_a, side, z) + at(far_a, z), place_z, nx, nz
    )
    both = ring1.carry.reshape(nx, 2, one, width)
    far1 = swap(lax.dynamic_index_in_dim(both, 1 - place_x, 0, keepdims=False), "dp", 1)
    ring_a.step(both)
    own1 = (lead(both, place_x, 0) + after(far1, ring_a.carry).astype(f32)).astype(bf16)
    ring0 = Ring(
        lambda z: at(keep0, z, place_x) + at(near0, z, place_x) + at(far0, z), place_z, nx, nz
    )

    def finish(kernel, own, outs, out_specs, scratch, copies=0, more=(), aliases=None):
        other = swap(own, "section", 2)
        beside = swap(jnp.stack([own, other]), "section", 1)
        return call(kernel, [bits, own, other, beside] + list(more),
                    [SMEM] + [VMEM] * 3 + [ANY] * len(more), outs, out_specs, scratch, copies, aliases)

    def feed_finish(layer, own, more=()):
        return finish(
            functools.partial(feed_finish_kernel, layer), own,
            [((LAYERS, one, wide), f32), ((LAYERS, share, width), f32)], [ANY] * 2,
            [((one, wide), f32), ((share, width), f32)], 2, more, {4: 0, 5: 1} if more else None,
        )

    grads = feed_finish(1, own1)
    both = ring_a.finish().reshape(nx, ahead + one, width)
    grad_up, grad_down = feed_finish(0, ring0.finish().reshape(2, one, width), grads)
    own = jnp.stack([lax.dynamic_index_in_dim(both, place_x, 0, keepdims=False),
                     swap(lax.dynamic_index_in_dim(both, 1 - place_x, 0, keepdims=False), "dp", 1)])
    pair = lambda n: ((LAYERS, n), f32)
    (grad_table, a_gain, a_shift, grad_qkv, a_qv, grad_out, a_out, m_gain, m_shift, m_up, m_down) = finish(
        functools.partial(attend_finish_kernel, ahead, docs_rows),
        own,
        [((one, step_count), f32), pair(one), pair(one), ((LAYERS, one, 3 * width), f32), pair(2 * one),
         ((LAYERS, one, width), f32), pair(one), pair(one), pair(one), pair(share), pair(one)],
        [VMEM] * 11,
        [((2, 2, ahead, width), f32), ((width // one * docs_rows, one), f32)],
    )

    return (
        last,
        g0,
        grad_table.T,
        a_gain,
        a_shift,
        grad_qkv,
        a_qv,
        grad_out,
        a_out,
        m_gain,
        m_shift,
        grad_up,
        m_up,
        grad_down,
        m_down,
    )


def solution(mesh):
    rows = P(("dp", "section"), None)
    in_specs = (rows,) * 4 + (P(),) * 13
    flat, deep = P(None, "dp"), P(None, "dp", None)
    out_specs = (rows, rows) + (flat, flat, flat, deep, flat, deep, flat, flat, flat, deep, flat, deep, flat)
    return jax.shard_map(local, mesh=mesh, in_specs=in_specs, out_specs=out_specs, check_vma=False)
```

```python
import functools

import jax
import jax.numpy as jnp
from jax import lax
from jax.experimental import pallas as pl
from jax.experimental.pallas import tpu as pltpu
from jax.sharding import PartitionSpec as P

HDIM = 64
PAIR = 2 * HDIM
LAYERS = 2
BLOCK = 768
LIMIT = 60 * 1024 * 1024
MIDDLE = 40 * 1024 * 1024
SMALL = 16 * 1024 * 1024

epsilon = 1e-05
masked_score = -1000000000.0
scale = HDIM ** (-0.5)
f32 = jnp.float32
bf16 = jnp.bfloat16
ANY = pl.BlockSpec(memory_space=pl.ANY)
VMEM = pl.BlockSpec(memory_space=pltpu.VMEM)
SMEM = pl.BlockSpec(memory_space=pltpu.SMEM)
HBM = pl.BlockSpec(memory_space=pltpu.HBM)


def mm(a, b):
    return lax.dot_general(a, b, (((1,), (0,)), ((), ())), preferred_element_type=f32)


def mm_nt(a, b):
    return lax.dot_general(a, b, (((1,), (1,)), ((), ())), preferred_element_type=f32)


def cols(n, size=BLOCK):
    return pl.ds(n * size, size)


rows_of = cols


def loop(count, body):
    for n in range(count):
        body(n)


class Copies:
    def __init__(self, sems):
        self.sems, self.used, self.pending = sems, 0, []

    def start(self, source, target):
        copy = pltpu.make_async_copy(source, target, self.sems.at[self.used])
        self.used += 1
        copy.start()
        return copy

    def send(self, source, target):
        self.pending.append(self.start(source, target))

    def finish(self):
        for copy in self.pending:
            copy.wait()


def norm_stats(hidden):
    full = hidden.astype(f32)
    centered = full - jnp.mean(full, axis=-1, keepdims=True)
    rstd = lax.rsqrt(jnp.mean(centered * centered, axis=-1, keepdims=True) + epsilon)
    return centered * rstd, rstd


def norm_forward(hidden, gain, shift):
    xhat, rstd = norm_stats(hidden)
    return (xhat * gain.astype(f32) + shift.astype(f32)).astype(bf16)


def gelu_pair(u):
    c, a = 0.7978845608028654, 0.044715
    square = u * u
    t = jnp.tanh(c * u * (1.0 + a * square))
    half = 0.5 * (1.0 + t)
    slope = half + 0.5 * u * (1.0 - t * t) * (c * (1.0 + 3.0 * a * square))
    return u * half, slope


def doc_mask(bounds, rows):
    one = lax.broadcasted_iota(jnp.int32, (rows, rows), 0)
    other = lax.broadcasted_iota(jnp.int32, (rows, rows), 1)
    left = sum((one >= b).astype(jnp.int32) for b in bounds)
    right = sum((other >= b).astype(jnp.int32) for b in bounds)
    return left == right


def bounds_of(len_ref):
    bounds, total = [], 0
    for k in range(len_ref.shape[1] - 1):
        total = total + len_ref[0, k]
        bounds.append(total)
    return bounds


def halves(x):
    low = lax.broadcasted_iota(jnp.int32, x.shape, 1) < HDIM
    zero = jnp.zeros_like(x)
    return jnp.where(low, x, zero), jnp.where(low, zero, x)


def soft_columns(key, query, same):
    s = jnp.where(same, mm_nt(key, query) * scale, masked_score)
    e = jnp.exp(s - jnp.max(s, axis=0, keepdims=True))
    return e * (1.0 / jnp.sum(e, axis=0, keepdims=True))


def qkv_forward(normed, weight, bias_ref, bias_row, target):
    width = normed.shape[1]
    for n in range(3):
        out = mm(normed, weight[:, cols(n, width)])
        if n != 1:
            out = out + bias_ref[bias_row, cols(n // 2, width)].astype(f32)
        target[:, cols(n, width)] = out.astype(bf16)


def attend_probs(mixed, same_ref, probs):
    width = mixed.shape[1] // 3
    count = width // PAIR
    same = same_ref[...] > 0.5
    for p in range(count):
        q = mixed[:, cols(p, PAIR)]
        k = mixed[:, cols(p + count, PAIR)]
        for h, key in enumerate(halves(k)):
            probs[2 * p + h] = soft_columns(key, q, same).astype(bf16)


def attend_context(mixed, probs, target):
    width = mixed.shape[1] // 3
    count = width // PAIR
    for p in range(count):
        v = mixed[:, cols(p + 2 * count, PAIR)]
        total = sum(mm(value.T, probs[2 * p + h]) for h, value in enumerate(halves(v)))
        target[:, cols(p, PAIR)] = total.T.astype(bf16)


def attend_grad(mixed, probs, dcontext, target):
    width = mixed.shape[1] // 3
    count = width // PAIR
    for p in range(count):
        q = mixed[:, cols(p, PAIR)]
        k = mixed[:, cols(p + count, PAIR)]
        v = mixed[:, cols(p + 2 * count, PAIR)]
        d = dcontext[:, cols(p, PAIR)]
        dq = dk = dv = 0.0
        for h, (key, value, query, dc) in enumerate(zip(halves(k), halves(v), halves(q), halves(d))):
            low = probs[2 * p + h]
            soft = low.astype(f32)
            dsoft = mm_nt(value, d)
            inner = jnp.sum(soft * dsoft, axis=0, keepdims=True)
            dscores = (soft * (dsoft - inner)).astype(bf16)
            dv = dv + mm(low, dc)
            dk = dk + mm(dscores, query)
            dq = dq + mm(key.T, dscores)
        target[:, cols(p, PAIR)] = (dq * scale).T.astype(bf16)
        target[:, cols(p + count, PAIR)] = (dk * scale).astype(bf16)
        target[:, cols(p + 2 * count, PAIR)] = dv.astype(bf16)


def forward_kernel(
    bits, lengths, timesteps, inputs, a_gain, a_shift, qv, out_b, m_gain, m_shift, up_b, down_b,
    cotangent, table, qkv_w, out_w, up_w, down_w,
    x1, h0, h1, h3, last, na, mixed, ctx, nm, act, slope, dinner, dmixed, g2, g3, vec,
    v_table, v_qkv, v_out, v_up, v_down, v_h, v_na, v_mixed, v_ctx, v_nm, v_act, v_slope, v_x, v_g,
    v_dinner, v_dctx, v_dmixed, v_dn, v_gmid, v_gout, v_probs, same, sems,
):
    copies = Copies(sems)
    rows, width = inputs.shape
    wide = up_w.shape[2]
    docs = lengths.shape[1]
    l_table = copies.start(table, v_table)
    loads = []
    for l in range(LAYERS):
        loads.append(
            [
                copies.start(w.at[l], v.at[l])
                for w, v in ((qkv_w, v_qkv), (out_w, v_out), (up_w, v_up), (down_w, v_down))
            ]
        )
    l_g = copies.start(cotangent, v_g)
    bounds = bounds_of(lengths)
    same[...] = doc_mask(bounds, rows).astype(f32)
    tail = x1.shape[0] - rows
    which = lax.broadcasted_iota(jnp.int32, (tail, width), 0)
    note = jnp.zeros((tail, width), f32)
    for k, bound in enumerate(bounds):
        note = jnp.where(which == k, bound.astype(f32), note)
    v_x[...] = note.astype(bf16)
    copies.send(v_x, x1.at[pl.ds(rows, tail)])
    steps = table.shape[0]
    doc = lax.broadcasted_iota(jnp.int32, (16, steps), 0)
    wanted = jnp.full((16, steps), -1, jnp.int32)
    for k in range(docs):
        wanted = jnp.where(doc == k, timesteps[0, k], wanted)
    step = lax.broadcasted_iota(jnp.int32, (16, steps), 1)
    onehot = (step == wanted).astype(f32).astype(bf16)
    token = lax.broadcasted_iota(jnp.int32, (rows, 16), 0)
    own = sum((token >= bound).astype(jnp.int32) for bound in bounds)
    chosen = (own == lax.broadcasted_iota(jnp.int32, (rows, 16), 1)).astype(f32).astype(bf16)
    l_table.wait()
    embedded = mm(chosen, mm(onehot, v_table[...]).astype(bf16))
    v_h[0] = (inputs[...].astype(f32) + embedded).astype(bf16)
    for l in range(LAYERS):
        h_in, h_mid = v_h.at[2 * l], v_h.at[2 * l + 1]
        h_out = v_h.at[2 * l + 2]
        v_na[l] = norm_forward(h_in[...], a_gain[l : l + 1, :], a_shift[l : l + 1, :])
        loads[l][0].wait()
        qkv_forward(v_na[l], v_qkv.at[l], qv, slice(l, l + 1), v_mixed.at[l])
        copies.send(v_na.at[l], na.at[l])
        if l == 0:
            copies.send(v_mixed.at[l], mixed)
        attend_probs(v_mixed.at[l], same, v_probs)
        attend_context(v_mixed.at[l], v_probs, v_ctx.at[l])
        copies.send(v_ctx.at[l], ctx.at[l])
        loads[l][1].wait()

        def project(n):
            at = cols(n)
            out = h_in[:, at].astype(f32) + mm(v_ctx[l], v_out[l, :, at])
            h_mid[:, at] = (out + out_b[l : l + 1, at].astype(f32)).astype(bf16)

        loop(width // BLOCK, project)
        v_nm[l] = norm_forward(h_mid[...], m_gain[l : l + 1, :], m_shift[l : l + 1, :])
        copies.send(v_nm.at[l], nm.at[l])
        loads[l][2].wait()

        def expand(n):
            at = cols(n)
            inner = mm(v_nm[l], v_up[l, :, at]) + up_b[l : l + 1, at].astype(f32)
            active, s = gelu_pair(inner)
            v_act[l, :, at] = active.astype(bf16)
            v_slope[l, :, at] = s.astype(bf16)

        loop(wide // BLOCK, expand)
        copies.send(v_act.at[l], act.at[l])
        if l == 0:
            copies.send(v_slope.at[l], slope)
        loads[l][3].wait()

        def contract(n):
            at = cols(n)
            out = h_mid[:, at].astype(f32) + mm(v_act[l], v_down[l, :, at])
            h_out[:, at] = (out + down_b[l : l + 1, at].astype(f32)).astype(bf16)

        loop(width // BLOCK, contract)
    for k, h in ((0, h0), (1, h1), (3, h3), (4, last)):
        copies.send(v_h.at[k], h)
    by_x = jnp.where(bits[0] == 0, 2, 0)
    copies.send(v_h.at[by_x], x1.at[pl.ds(0, rows)])
    l_g.wait()
    l = LAYERS - 1
    backward_part(
        l, copies, v_g, a_gain, m_gain, v_h.at[2 * l], v_h.at[2 * l + 1], v_mixed.at[l], v_slope.at[l],
        v_probs, (v_qkv.at[l], v_out.at[l], v_up.at[l], v_down.at[l]), lambda *name: None, vec,
        dinner.at[l], dmixed.at[l], v_dinner, v_dmixed, v_dctx, v_dn, v_gmid, v_gout,
    )
    copies.send(v_gmid, g3)
    copies.send(v_gout, g2)
    copies.finish()


def norm_backward(h, gain, dnormed, upstream, vec, at_gain, at_shift, target):
    width = h.shape[1]
    xhat, rstd = norm_stats(h[...])
    dn = dnormed[...]
    e = dn * gain.astype(f32)
    grad = (
        e - jnp.mean(e, axis=-1, keepdims=True) - xhat * jnp.mean(e * xhat, axis=-1, keepdims=True)
    ) * rstd
    target[...] = (upstream[...].astype(f32) + grad).astype(bf16)
    vec[:, at_gain : at_gain + width] = jnp.sum(dn * xhat, axis=0, keepdims=True)
    vec[:, at_shift : at_shift + width] = jnp.sum(dn, axis=0, keepdims=True)


def colsum(x):
    return jnp.sum(x.astype(f32), axis=0, keepdims=True)


def write_notes(me, timesteps, vectors, doc_sums, notes):
    _, _, shares, ahead, width = notes.shape
    docs = timesteps.shape[1]
    one = width // shares
    per = width // one
    for core, vec in enumerate(vectors):
        count = vec.shape[1] // width
        rows = [vec[:, k * width : (k + 1) * width] for k in range(count)]
        rows.append(jnp.zeros((ahead - count, width), f32))
        value = jnp.concatenate(rows, axis=0).astype(bf16)
        for s in range(shares):
            notes[core, 0, s] = value
    row = lax.broadcasted_iota(jnp.int32, (ahead, width), 0)
    lane = lax.broadcasted_iota(jnp.int32, (ahead, width), 1)
    docs_rows = notes_rows(shares, docs, width)
    marks = jnp.zeros((ahead, width), f32)
    sums = [jnp.zeros((ahead, width), f32) for _ in range(shares)]
    for k in range(docs):
        number = me * docs + k
        r, j = number // per, number % per
        step = timesteps[0, k]
        here = lane == j * docs_rows + r
        marks = jnp.where(here & (row == 0), (step // 32).astype(f32), marks)
        marks = jnp.where(here & (row == 1), (step % 32).astype(f32), marks)
        here = (row == r) & (lane >= j * one) & (lane < (j + 1) * one)
        wide = jnp.broadcast_to(doc_sums[k : k + 1, :], (8, width))
        for s in range(shares):
            turned = pltpu.roll(wide, lax.rem((j - s) * one + width, width), 1)
            turned = jnp.broadcast_to(turned[:1], (ahead, width))
            sums[s] = jnp.where(here, turned, sums[s])
    for s in range(shares):
        notes[0, 1, s] = sums[s].astype(bf16)
        notes[1, 1, s] = marks.astype(bf16)


def notes_rows(shares, docs, width):
    return 4 * shares * docs * (width // shares) // width


def backward_part(
    layer, copies, g, a_gain, m_gain, h_a, h_m, mixed, slope, probs, weights, wait, vec, dinner, dmixed,
    v_dinner, v_dmixed, v_dctx, v_dn, v_gmid, v_gout,
):
    v_qkv, v_out, v_up, v_down = weights
    rows, width = g.shape
    wide = v_up.shape[1]
    one_row = slice(layer, layer + 1)
    at_qv, at_mshift, at_downb, at_upb = 4 * width, 6 * width, 7 * width, 8 * width
    vec[:, at_downb : at_downb + width] = colsum(g[...])
    for n in range(wide // BLOCK):
        wait("down", n)
    wait("slope")
    for n in range(wide // BLOCK):
        at = cols(n)
        dact = mm_nt(g[...], v_down[at, :])
        di = (dact * slope[:, at].astype(f32)).astype(bf16)
        v_dinner[:, at] = di
        vec[:, at_upb + n * BLOCK : at_upb + (n + 1) * BLOCK] = colsum(di)
    copies.send(v_dinner, dinner)
    wait("up")
    v_dn[...] = mm_nt(v_dinner[...], v_up[...])
    wait("h_m")
    norm_backward(h_m, m_gain[one_row, :], v_dn, g, vec, 3 * width, at_mshift, v_gmid)
    vec[:, 2 * width : 3 * width] = colsum(v_gmid[...])
    wait("out")
    v_dctx[...] = mm_nt(v_gmid[...], v_out[...]).astype(bf16)
    attend_grad(mixed, probs, v_dctx, v_dmixed)
    copies.send(v_dmixed, dmixed)
    vec[:, at_qv : at_qv + width] = colsum(v_dmixed[:, :width])
    vec[:, at_qv + width : at_qv + 2 * width] = colsum(v_dmixed[:, 2 * width :])
    wait("qkv")
    v_dn[...] = mm_nt(v_dmixed[...], v_qkv[...])
    wait("h_a")
    norm_backward(h_a, a_gain[one_row, :], v_dn, v_gmid, vec, 0, width, v_gout)


def backward_kernel(
    bits, lengths, timesteps, a_gain, m_gain, vec_upper, g, g_upper, h_a, h_m, mixed, slope,
    qkv_w, out_w, up_w, down_w, _, __,
    dinner, dmixed, g_out, send, own, notes,
    v_qkv, v_out, v_up, v_down, v_g, v_ha, v_hm, v_mixed, v_slope, v_dinner, v_dctx, v_dmixed, v_dn,
    v_gmid, v_gout, v_trade, v_notes, vec, v_probs, v_touch, same, sems,
):
    copies = Copies(sems)
    rows, width = h_a.shape
    wide = up_w.shape[2]
    loads = {"mixed": copies.start(mixed, v_mixed), "g": copies.start(g, v_g)}
    for n in range(wide // BLOCK):
        loads["down", n] = copies.start(down_w.at[0, cols(n)], v_down.at[cols(n)])
    for name, source, target in (
        ("slope", slope, v_slope), ("up", up_w.at[0], v_up), ("h_m", h_m, v_hm), ("out", out_w.at[0], v_out),
        ("qkv", qkv_w.at[0], v_qkv), ("h_a", h_a, v_ha), ("g_upper", g_upper, v_trade.at[0]),
    ):
        loads[name] = copies.start(source, target)
    wait = lambda *name: loads[name if len(name) > 1 else name[0]].wait()
    v_touch[...] = jnp.zeros_like(v_touch)
    tile = (pl.ds(0, 16), pl.ds(0, 128))
    touched = [
        copies.start(v_touch, ref.at[tile])
        for ref in (g_out, send, own, notes.at[0, 0, 0], dinner.at[0], dmixed.at[0])
    ]
    same[...] = doc_mask(bounds_of(lengths), rows).astype(f32)
    wait("mixed")
    attend_probs(v_mixed, same, v_probs)
    wait("g")
    for copy in touched:
        copy.wait()
    backward_part(
        0, copies, v_g, a_gain, m_gain, v_ha, v_hm, v_mixed, v_slope, v_probs,
        (v_qkv, v_out, v_up, v_down), wait, vec, dinner.at[0], dmixed.at[0], v_dinner, v_dmixed, v_dctx,
        v_dn, v_gmid, v_gout,
    )
    copies.send(v_gout, g_out)
    v_trade[1] = v_gmid[...]
    wait("g_upper")
    copies.send(v_trade.at[bits[0]], send)
    copies.send(v_trade.at[1 - bits[0]], own)
    count = lengths.shape[1]
    doc = lax.broadcasted_iota(jnp.int32, (16, rows), 0)
    token = lax.broadcasted_iota(jnp.int32, (16, rows), 1)
    index = sum((token >= bound).astype(jnp.int32) for bound in bounds_of(lengths))
    onehot = ((index == doc) & (doc < count)).astype(f32).astype(bf16)
    doc_sums = mm(onehot, v_gout[...])
    write_notes(bits[3], timesteps, (vec, vec_upper), doc_sums, v_notes)
    copies.send(v_notes, notes)
    copies.finish()


def relative(bits, shard, places):
    z, x = shard // 2, lax.rem(shard, 2)
    return lax.rem(bits[5] - z + places, places), lax.rem(x + bits[0], 2)


def pick_layer(ref, layer, at=slice(None)):
    return jnp.where(layer == 0, ref[0:1, at].astype(f32), ref[1:2, at].astype(f32))


def feed_weight_kernel(
    layer, bits, h, g, own_g, own_act, own_nm, own_dinner, gain, shift, up_b, up_w, down_w, *rest
):
    *outs, v_up, v_down, v_nm, v_own, v_g, v_n, v_act, v_dinner, v_send, v_keep, sems = rest
    copies = Copies(sems)
    rows, width = h.shape
    wide = up_w.shape[2]
    quarter = width // 4
    side, core = bits[1], bits[2]
    one_row = slice(layer, layer + 1)
    l_nm = copies.start(own_nm.at[layer], v_own)
    order = [2 * side + 1 - core, 2 * side + core, 2 - 2 * side, 3 - 2 * side]
    size = wide // 4
    loads = []
    for n, block in enumerate(order):
        at = pl.ds(pl.multiple_of(block * size, 128), size)
        load = [copies.start(up_w.at[layer, :, at], v_up.at[n])]
        if n < 2:
            load.append(copies.start(down_w.at[layer, at], v_down.at[n]))
        load.append(copies.start(own_act.at[layer, :, at], v_act.at[n, pl.ds(0, rows)]))
        if n < 2:
            load.append(copies.start(own_dinner.at[layer, :, at], v_dinner.at[n, pl.ds(0, rows)]))
        loads.append(load)
    normed = norm_forward(h[...], gain[one_row, :], shift[one_row, :])
    v_nm[...] = normed
    v_n[:, rows:] = normed.T
    for k in range(2):
        part = 2 * side + (1 - core if k == 0 else core)
        at = pl.ds(pl.multiple_of(part * quarter // 128 * 128, 128), 2 * 128)
        for ref, first in ((own_g, 0), (g, rows)):
            piece = ref[:, at].T
            shifted = jnp.where(part % 2 == 0, piece[:quarter].astype(f32), piece[256 - quarter :].astype(f32))
            v_g[k * quarter : (k + 1) * quarter, first : first + rows] = shifted.astype(bf16)
    l_nm.wait()
    v_n[:, :rows] = v_own[...].T
    flat = len(v_send.shape) == 2

    def feed(n, block):
        at = pl.ds(pl.multiple_of(block * size, 128), size)
        inner = mm(v_nm[...], v_up[n]) + up_b[one_row, at].astype(f32)
        active, slope = gelu_pair(inner)
        v_act[n, rows:] = active.astype(bf16)
        down = mm(v_g[...], v_act[n]).astype(bf16)
        for k, target in ((0, v_send), (1, v_keep)):
            half = down[k * quarter : (k + 1) * quarter]
            if flat:
                target[:quarter, at] = half
                continue
            places, _, _, one, _ = target.shape
            share = wide // (2 * places)
            for m in range(size // share):
                back, across = relative(bits, block * (size // share) + m, places)
                for p in range(quarter // one):
                    piece = half[p * one : (p + 1) * one, m * share : (m + 1) * share]
                    target[back, across, 0, :, p * share : (p + 1) * share] = piece
        if n < 2:
            dact = mm_nt(g[...], v_down[n])
            v_dinner[n, rows:] = (dact * slope).astype(bf16)
            up = mm(v_n[...], v_dinner[n]).astype(bf16)
            target = v_send if n == 0 else v_keep
            if flat:
                target[quarter:, :size] = up
                return
            places, _, _, one, _ = target.shape
            for m in range(2 * places):
                back, across = relative(bits, m, places)
                target[back, across, 1] = up[m * one : (m + 1) * one]

    def leave(n, block):
        if flat:
            return
        places = v_send.shape[0]
        count = 2 * places // 4
        for target, out in ((v_send, outs[-2]), (v_keep, outs[-1])):
            for m in range(count):
                back, across = relative(bits, block * count + m, places)
                copies.send(target.at[back, across, 0], out.at[back, across, 0])
        if n < 2:
            target, out = ((v_send, outs[-2]), (v_keep, outs[-1]))[n]
            copies.send(target.at[:, :, 1], out.at[:, :, 1])

    for group in ((0,), (1, 2, 3)):
        for n in group:
            for load in loads[n]:
                load.wait()
        for n in group:
            feed(n, order[n])
        for n in group:
            leave(n, order[n])
    if flat:
        copies.send(v_send, outs[-2])
        copies.send(v_keep, outs[-1])
    copies.finish()


def attend_weight_kernel(
    bits, hx, g, own_g, own_na, own_ctx, own_dmixed, notes, gain, shift, qv, qkv_w, out_w,
    send, keep,
    v_qkv, v_out, v_na, v_mixed, v_dctx, v_dmixed, v_ctx, v_left, v_right, v_own, v_own_ctx,
    v_own_dmixed, v_bias, v_send, v_keep, v_notes, v_probs, same, sems,
):
    copies = Copies(sems)
    rows, width = g.shape
    layer, core = bits[0], bits[2]
    l_out = copies.start(out_w.at[layer], v_out)
    l_qkv = copies.start(qkv_w.at[layer], v_qkv)
    l_ctx = copies.start(own_ctx.at[layer], v_own_ctx)
    l_own = copies.start(own_na.at[layer], v_own)
    l_dmixed = copies.start(own_dmixed.at[layer], v_own_dmixed)
    l_notes = copies.start(notes, v_notes)
    note = hx[rows:, :].astype(f32)
    bounds = [note[k : k + 1, :rows].astype(jnp.int32) for k in range(2)]
    same[...] = doc_mask(bounds, rows).astype(f32)
    v_bias[...] = pick_layer(qv, layer)
    v_na[...] = norm_forward(hx[:rows, :], pick_layer(gain, layer), pick_layer(shift, layer))
    l_out.wait()
    v_dctx[...] = mm_nt(g[...], v_out[...]).astype(bf16)
    l_qkv.wait()
    qkv_forward(v_na[...], v_qkv, v_bias, slice(0, 1), v_mixed)
    attend_probs(v_mixed, same, v_probs)
    attend_context(v_mixed, v_probs, v_ctx)
    attend_grad(v_mixed, v_probs, v_dctx, v_dmixed)
    part = width // 2
    shares, ahead = notes.shape[2], notes.shape[3]
    share = width // shares
    sides = [lax.rem(bits[1] + h, 2) for h in range(2)]
    places = [relative(bits, s, shares // 2) for s in range(shares)]

    def put(target, k, n, out):
        for s, (back, across) in enumerate(places):
            piece = out[s * share : (s + 1) * share].astype(bf16)
            target[sides[n // 2], back, across, ahead:, (n % 2) * part : (n % 2 + 1) * part] = piece

    l_notes.wait()
    for k in range(2):
        target = v_send if k == 0 else v_keep
        for h in range(2):
            for s, (back, across) in enumerate(places):
                target[sides[h], back, across, :ahead] = v_notes[1 - core if k == 0 else core, h, s]
    l_ctx.wait()
    v_left[:, :rows] = v_own_ctx[...].T
    v_left[:, rows:] = v_ctx[...].T
    for k in range(2):
        side = jnp.where(k == 0, 1 - core, core)
        at = pl.ds(pl.multiple_of(side * part, 128), part)
        v_right[k, :rows, :part] = own_g[:, at]
        v_right[k, rows:, :part] = g[:, at]
        put(v_send if k == 0 else v_keep, k, 0, mm(v_left[...], v_right[k, :, :part]))
    l_own.wait()
    l_dmixed.wait()
    v_left[:, :rows] = v_own[...].T
    v_left[:, rows:] = v_na[...].T
    for k in range(2):
        side = jnp.where(k == 0, 1 - core, core)
        target = v_send if k == 0 else v_keep
        at = pl.ds(pl.multiple_of(side * 3 * part, 128), 3 * part)
        v_right[k, :rows] = v_own_dmixed[:, at]
        v_right[k, rows:] = v_dmixed[:, at]
        out = mm(v_left[...], v_right[k])
        for n in range(1, 4):
            put(target, k, n, out[:, (n - 1) * part : n * part])
        copies.send(target, send if k == 0 else keep)
    copies.finish()


def feed_finish_kernel(layer, bits, own, other, beside, *rest):
    up_out, down_out, v_up, v_down, sems = rest[-5:]
    copies = Copies(sems)
    side, core = bits[1], bits[2]
    rows, width = own.shape[1:]
    share, quarter = v_down.shape[0], width // 4
    pieces = width // share
    for ref, chip, half in (
        (own, side, core), (other, 1 - side, core), (beside.at[0], side, 1 - core), (beside.at[1], 1 - side, 1 - core)
    ):
        part = 2 * chip + half
        v_up[:, pl.ds(pl.multiple_of(part * width, 128), width)] = ref[1].astype(f32)
        down = jnp.concatenate(
            [ref[0, :, p * share : (p + 1) * share].astype(f32) for p in range(pieces)], axis=0
        ).T
        for at in range(4):

            @pl.when(part == at)
            def _():
                v_down[:, at * quarter : (at + 1) * quarter] = down

    copies.send(v_up, up_out.at[layer])
    copies.send(v_down, down_out.at[layer])
    copies.finish()


def attend_finish_kernel(
    ahead, docs_rows, bits, own, other, beside,
    table, a_gain, a_shift, qkv, a_qv, out, a_out, m_gain, m_shift, m_up, m_down, notes, sums,
):
    place_x, side, core = bits[0], bits[1], bits[2]
    width = own.shape[2]
    part = width // 2

    def put(ref, first, which):
        for relative in range(2):
            layer = jnp.where(relative == 0, place_x, 1 - place_x)
            value = ref[relative, ahead:, :].astype(f32)
            base = 3 * part * which
            if first:
                out[layer, :, pl.ds(pl.multiple_of(which * part, 128), part)] = value[:, :part]
                qkv[layer, :, pl.ds(pl.multiple_of(base, 128), part)] = value[:, part:]
            else:
                qkv[layer, :, pl.ds(pl.multiple_of(base + part, 128), width)] = value

    def note(ref, which, half):
        notes[which, half] = ref[0, :ahead, :].astype(f32) + ref[1, :ahead, :].astype(f32)

    for half in range(2):
        for here, mine in ((own, 0), (other, 1)):

            @pl.when((side == half) == (mine == 0))
            def _():
                put(here, half == 0, core)
                put(beside.at[mine], half == 0, 1 - core)

                note(here, core, half)
                note(beside.at[mine], 1 - core, half)

    index = bits[4]
    one = a_gain.shape[1]
    for l in range(LAYERS):
        value = notes[l, 0]
        at = 0
        for ref in (a_gain, a_shift, a_out, m_gain, a_qv, m_shift, m_down, m_up):
            size = ref.shape[1]
            count = size // one
            place = index * size
            line = value[at : at + 1]
            for k in range(1, count):
                line = jnp.where(place // width == k, value[at + k : at + k + 1], line)
            line = jnp.broadcast_to(line, (8, width))
            turned = pltpu.roll(line, lax.rem(width - lax.rem(place, width), width), 1)
            ref[l : l + 1, :] = turned[:1, :size]
            at += count
    per, count = width // one, (width // one) * docs_rows
    high, low = notes[1, 1, 0:1, :count], notes[1, 1, 1:2, :count]
    steps = (high * 32.0 + low).astype(jnp.int32)
    for j in range(per):
        sums[j * docs_rows : (j + 1) * docs_rows, :] = notes[0, 1, :docs_rows, j * one : (j + 1) * one]
    step = lax.broadcasted_iota(jnp.int32, (table.shape[1], count), 0)
    onehot = (step == steps).astype(f32).astype(bf16)
    table[...] = mm_nt(sums[...].T.astype(bf16), onehot)


def call(kernel, operands, specs, outs, out_specs, scratch, copies, aliases=None, limit=LIMIT):
    return pl.pallas_call(
        kernel,
        out_shape=[jax.ShapeDtypeStruct(s, d) for s, d in outs],
        in_specs=specs,
        out_specs=out_specs,
        scratch_shapes=[pltpu.VMEM(s, d) for s, d in scratch]
        + [pltpu.SemaphoreType.DMA((copies,))] * (copies > 0),
        input_output_aliases=aliases or {},
        compiler_params=pltpu.CompilerParams(vmem_limit_bytes=limit),
        cost_estimate=pl.CostEstimate(flops=0, bytes_accessed=0, transcendentals=0),
    )(*operands)


def swap(x, axis, by):
    size = lax.axis_size(axis)
    return lax.ppermute(x, axis, [(i, i ^ by) for i in range(size)])


def plus(a, b):
    return (a.astype(f32) + b.astype(f32)).astype(bf16)


def after(x, *others):
    return lax.optimization_barrier((x,) + others)[0] if others else x


class Ring:
    def __init__(self, term, place_z, nx, nz):
        self.term, self.nx, self.nz = term, nx, nz
        if nz > 4:
            groups = [[z * nx + x for z in range(nz)] for x in range(nx)]
            held = jnp.stack([term(s) for s in range(nz)]).astype(bf16)
            held = jnp.take(held, (place_z - jnp.arange(nz)) % nz, axis=0)
            self.carry = lax.psum_scatter(held, "dp", scatter_dimension=0, axis_index_groups=groups)
            self.at = nz
        else:
            self.carry = term(1).astype(bf16)
            self.at = 1

    def step(self, *others):
        if self.at < self.nz:
            self.at += 1
            size = self.nx * self.nz
            got = lax.ppermute(self.carry, "dp", [(d, (d + self.nx) % size) for d in range(size)])
            got = after(got, *others)
            self.carry = (got.astype(f32) + self.term(self.at % self.nz)).astype(bf16)

    def finish(self, *others):
        while self.at < self.nz:
            self.step(*others)
        return self.carry


def plus(*parts):
    return sum(part.astype(f32) for part in parts)


def local(
    inputs,
    timesteps,
    lengths,
    cotangent,
    time_table,
    attn_norm_gain,
    attn_norm_bias,
    qkv_weight,
    qv_bias,
    out_weight,
    out_bias,
    mlp_norm_gain,
    mlp_norm_bias,
    up_weight,
    up_bias,
    down_weight,
    down_bias,
):
    place = lax.axis_index("section")
    side, core = place // 2, place % 2
    dp = lax.axis_size("dp")
    nx, nz = 2, dp // 2
    index = lax.axis_index("dp")
    place_z, place_x = index // nx, index % nx
    rows, width = inputs.shape
    wide = up_weight.shape[2]
    docs = lengths.shape[1]
    step_count = time_table.shape[0]
    me = index * lax.axis_size("section") + place
    bits = jnp.stack([place_x, side, core, me, index, place_z]).astype(jnp.int32)

    ahead, docs_rows = 16, notes_rows(dp, docs, width)
    tok, tok2 = (rows, width), (LAYERS, rows, width)
    peer_cot = swap(cotangent, "section", 2)
    full, thrice = ((LAYERS, rows, wide), bf16), ((LAYERS, rows, 3 * width), bf16)
    x1, h0, h1, h3, last, na, mixed, ctx, nm, act, slope, dinner, dmixed, g2, g3, vec1 = call(
        forward_kernel,
        [bits, lengths, timesteps, inputs, attn_norm_gain, attn_norm_bias, qv_bias, out_bias,
         mlp_norm_gain, mlp_norm_bias, up_bias, down_bias, cotangent, time_table, qkv_weight, out_weight,
         up_weight, down_weight],
        [SMEM] * 3 + [VMEM] * 9 + [ANY] * 6,
        [((rows + 16, width), bf16)] + [(tok, bf16)] * 4
        + [(tok2, bf16), ((rows, 3 * width), bf16), (tok2, bf16), (tok2, bf16), full,
           ((rows, wide), bf16), full, thrice, (tok, bf16), (tok, bf16), ((1, 12 * width), f32)],
        [ANY] * 15 + [VMEM],
        [(time_table.shape, bf16), (qkv_weight.shape, bf16), (out_weight.shape, bf16),
         (up_weight.shape, bf16), (down_weight.shape, bf16), ((2 * LAYERS + 1,) + tok, bf16),
         (tok2, bf16), thrice, (tok2, bf16), (tok2, bf16), full, full, ((16, width), bf16), (tok, bf16),
         ((rows, wide), bf16), (tok, bf16), ((rows, 3 * width), bf16), (tok, f32), (tok, bf16), (tok, bf16),
         ((width // HDIM, rows, rows), bf16), ((rows, rows), f32)],
        40,
    )
    peer_h3 = swap(h3, "section", 2)
    peer_h1 = swap(h1, "section", 2)
    peer_hx = swap(x1, "dp", 1)
    peer_g2 = swap(g2, "section", 2)
    dinner, dmixed, g0, x2, own_ga, notes = call(
        backward_kernel,
        [bits, lengths, timesteps, attn_norm_gain, mlp_norm_gain, vec1, g2, g3, h0, h1, mixed, slope,
         qkv_weight, out_weight, up_weight, down_weight, dinner, dmixed],
        [SMEM] * 3 + [VMEM] * 3 + [ANY] * 12,
        [full, thrice, (tok, bf16), (tok, bf16), (tok, bf16), ((2, 2, dp, ahead, width), bf16)],
        [ANY] * 6,
        [(qkv_weight.shape[1:], bf16), (out_weight.shape[1:], bf16), (up_weight.shape[1:], bf16),
         (down_weight.shape[1:], bf16), (tok, bf16), (tok, bf16), (tok, bf16), ((rows, 3 * width), bf16),
         ((rows, wide), bf16), ((rows, wide), bf16), (tok, bf16), ((rows, 3 * width), bf16), (tok, f32),
         (tok, bf16), (tok, bf16), ((2,) + tok, bf16), ((2, 2, dp, ahead, width), bf16),
         ((1, 12 * width), f32), ((width // HDIM, rows, rows), bf16), ((16, 128), bf16),
         ((rows, rows), f32)],
        32,
        {16: 0, 17: 1},
    )
    peer_ga = swap(x2, "dp", 1)

    share, one, half, quarter = wide // dp, width // dp, width // 2, width // 4
    flat = share % 128 != 0

    def feed_weight(layer, h, g, own_g):
        shape = (quarter + width, wide) if flat else (nz, nx, 2, one, width)
        send, keep = call(
            functools.partial(feed_weight_kernel, layer),
            [bits, h, g, own_g, act, nm, dinner, mlp_norm_gain, mlp_norm_bias, up_bias, up_weight,
             down_weight],
            [SMEM, VMEM, VMEM, VMEM, HBM, HBM, HBM, VMEM, VMEM, VMEM, HBM, HBM],
            [(shape, bf16)] * 2,
            [HBM] * 2,
            [((4, width, wide // 4), bf16), ((2, wide // 4, width), bf16), (tok, bf16), (tok, bf16),
             ((2 * quarter, 2 * rows), bf16), ((width, 2 * rows), bf16),
             ((4, 2 * rows, wide // 4), bf16), ((2, 2 * rows, wide // 4), bf16),
             (shape, bf16), (shape, bf16)],
            40,
            limit=MIDDLE,
        )
        if flat:

            def sort(x):
                down = x[:quarter].reshape(-1, one, dp, share).transpose(2, 1, 0, 3)
                both = jnp.stack([down.reshape(dp, one, width), x[quarter:, :width].reshape(dp, one, width)], axis=1)
                both = jnp.take(both.reshape(nz, nx, 2, one, width), (place_z - jnp.arange(nz)) % nz, axis=0)
                return jnp.where(place_x == 0, both, both[:, ::-1])

            send, keep = sort(send), sort(keep)
        return keep, send

    def trade(keep, send, *others):
        return keep, swap(after(send, *others), "section", 1)

    keep1, send1 = feed_weight(1, peer_h3, peer_cot, after(cotangent, g0, peer_hx))
    keep1, near1 = trade(keep1, send1, peer_ga, peer_h1, peer_g2)
    ring1 = Ring(lambda s: plus(keep1[s], near1[s]), place_z, nx, nz)

    at_send, at_keep = call(
        attend_weight_kernel,
        [bits, after(peer_hx, ring1.carry), peer_ga, own_ga, na, ctx, dmixed, notes, attn_norm_gain, attn_norm_bias,
         qv_bias, qkv_weight, out_weight],
        [SMEM, VMEM, VMEM, VMEM, HBM, HBM, HBM, HBM, VMEM, VMEM, VMEM, HBM, HBM],
        [((2, nz, nx, ahead + one, width), bf16)] * 2,
        [HBM] * 2,
        [((width, 3 * width), bf16), ((width, width), bf16), (tok, bf16), ((rows, 3 * width), bf16),
         (tok, bf16), ((rows, 3 * width), bf16), (tok, bf16), ((width, 2 * rows), bf16),
         ((2, 2 * rows, 3 * half), bf16), (tok, bf16), (tok, bf16), ((rows, 3 * width), bf16),
         ((1, 2 * width), f32), ((2, nz, nx, ahead + one, width), bf16),
         ((2, nz, nx, ahead + one, width), bf16), ((2, 2, dp, ahead, width), bf16),
         ((width // HDIM, rows, rows), bf16), ((rows, rows), f32)],
        8,
        limit=MIDDLE,
    )

    ring1.step(at_keep)
    order = [s % nz for s in range(1, nz + 1)]
    keep_a, near_a = trade(at_keep, at_send, ring1.carry)
    away_a = {s: plus(keep_a[1, s], near_a[1, s]).astype(bf16) for s in order}
    far_a = {s: swap(away_a[s], "section", 2) for s in order}
    keep0, send0 = feed_weight(0, after(peer_h1, ring1.carry, *away_a.values()), peer_g2, g2)
    ring1.step(keep0)
    far_a[1] = after(far_a[1], ring1.carry)
    ring_a = Ring(lambda s: plus(keep_a[0, s], near_a[0, s], far_a[s]), place_z, nx, nz)
    keep0, near0 = trade(keep0, send0, ring_a.carry)
    away0 = {s: plus(keep0[s, 1], near0[s, 1]).astype(bf16) for s in order}
    far0 = {s: swap(away0[s], "dp", 1) for s in order}
    ring0 = Ring(lambda s: plus(keep0[s, 0], near0[s, 0], far0[s]), place_z, nx, nz)
    ring_a.step(*away0.values())
    both = ring1.finish(ring0.carry, ring_a.carry)
    own1 = plus(both[0], swap(both[1], "dp", 1)).astype(bf16)
    ring_a.step(both)
    ring0.step(both)

    def finish(kernel, own, outs, out_specs, scratch, copies=0, more=(), aliases=None, others=()):
        other = after(swap(own, "section", 2), *others)
        beside = swap(jnp.stack([own, other]), "section", 1)
        return call(kernel, [bits, own, other, beside] + list(more),
                    [SMEM] + [VMEM] * 3 + [ANY] * len(more), outs, out_specs, scratch, copies, aliases, SMALL)

    def feed_finish(layer, own, more=(), others=()):
        return finish(
            functools.partial(feed_finish_kernel, layer), own,
            [((LAYERS, one, wide), f32), ((LAYERS, share, width), f32)], [ANY] * 2,
            [((one, wide), f32), ((share, width), f32)], 2, more, {4: 0, 5: 1} if more else None, others,
        )

    grads = feed_finish(1, own1)
    both = ring_a.finish(own1)
    ring0.step(own1)
    own = jnp.stack([both[0], swap(both[1], "dp", 1)])
    grad_up, grad_down = feed_finish(0, ring0.finish(), grads, grads)
    pair = lambda n: ((LAYERS, n), f32)
    (grad_table, a_gain, a_shift, grad_qkv, a_qv, grad_out, a_out, m_gain, m_shift, m_up, m_down) = finish(
        functools.partial(attend_finish_kernel, ahead, docs_rows),
        own,
        [((one, step_count), f32), pair(one), pair(one), ((LAYERS, one, 3 * width), f32), pair(2 * one),
         ((LAYERS, one, width), f32), pair(one), pair(one), pair(one), pair(share), pair(one)],
        [VMEM] * 11,
        [((2, 2, ahead, width), f32), ((width // one * docs_rows, one), f32)],
    )

    return (
        last,
        g0,
        grad_table.T,
        a_gain,
        a_shift,
        grad_qkv,
        a_qv,
        grad_out,
        a_out,
        m_gain,
        m_shift,
        grad_up,
        m_up,
        grad_down,
        m_down,
    )


def solution(mesh):
    rows = P(("dp", "section"), None)
    in_specs = (rows,) * 4 + (P(),) * 13
    flat, deep = P(None, "dp"), P(None, "dp", None)
    out_specs = (rows, rows) + (flat, flat, flat, deep, flat, deep, flat, flat, flat, deep, flat, deep, flat)
    return jax.shard_map(local, mesh=mesh, in_specs=in_specs, out_specs=out_specs, check_vma=False)
```

```python
import functools

import jax
import jax.numpy as jnp
from jax import lax
from jax.experimental import pallas as pl
from jax.experimental.pallas import tpu as pltpu
from jax.sharding import PartitionSpec as P

HDIM = 64
PAIR = 2 * HDIM
LAYERS = 2
BLOCK = 768
LIMIT = 60 * 1024 * 1024
MIDDLE = 40 * 1024 * 1024
SMALL = 16 * 1024 * 1024

epsilon = 1e-05
masked_score = -1000000000.0
scale = HDIM ** (-0.5)
f32 = jnp.float32
bf16 = jnp.bfloat16
ANY = pl.BlockSpec(memory_space=pl.ANY)
VMEM = pl.BlockSpec(memory_space=pltpu.VMEM)
SMEM = pl.BlockSpec(memory_space=pltpu.SMEM)
HBM = pl.BlockSpec(memory_space=pltpu.HBM)


def mm(a, b):
    return lax.dot_general(a, b, (((1,), (0,)), ((), ())), preferred_element_type=f32)


def mm_nt(a, b):
    return lax.dot_general(a, b, (((1,), (1,)), ((), ())), preferred_element_type=f32)


def cols(n, size=BLOCK):
    return pl.ds(n * size, size)


rows_of = cols


def loop(count, body):
    for n in range(count):
        body(n)


class Copies:
    def __init__(self, sems):
        self.sems, self.used, self.pending = sems, 0, []

    def start(self, source, target):
        copy = pltpu.make_async_copy(source, target, self.sems.at[self.used])
        self.used += 1
        copy.start()
        return copy

    def send(self, source, target):
        self.pending.append(self.start(source, target))

    def finish(self):
        for copy in self.pending:
            copy.wait()


def norm_stats(hidden):
    full = hidden.astype(f32)
    centered = full - jnp.mean(full, axis=-1, keepdims=True)
    rstd = lax.rsqrt(jnp.mean(centered * centered, axis=-1, keepdims=True) + epsilon)
    return centered * rstd, rstd


def norm_forward(hidden, gain, shift):
    xhat, rstd = norm_stats(hidden)
    return (xhat * gain.astype(f32) + shift.astype(f32)).astype(bf16)


def gelu_pair(u):
    c, a = 0.7978845608028654, 0.044715
    square = u * u
    t = jnp.tanh(c * u * (1.0 + a * square))
    half = 0.5 * (1.0 + t)
    slope = half + 0.5 * u * (1.0 - t * t) * (c * (1.0 + 3.0 * a * square))
    return u * half, slope


def doc_mask(bounds, rows):
    one = lax.broadcasted_iota(jnp.int32, (rows, rows), 0)
    other = lax.broadcasted_iota(jnp.int32, (rows, rows), 1)
    left = sum((one >= b).astype(jnp.int32) for b in bounds)
    right = sum((other >= b).astype(jnp.int32) for b in bounds)
    return left == right


def bounds_of(len_ref):
    bounds, total = [], 0
    for k in range(len_ref.shape[1] - 1):
        total = total + len_ref[0, k]
        bounds.append(total)
    return bounds


def halves(x):
    low = lax.broadcasted_iota(jnp.int32, x.shape, 1) < HDIM
    zero = jnp.zeros_like(x)
    return jnp.where(low, x, zero), jnp.where(low, zero, x)


def soft_columns(key, query, same):
    s = jnp.where(same, mm_nt(key, query) * scale, masked_score)
    e = jnp.exp(s - jnp.max(s, axis=0, keepdims=True))
    return e * (1.0 / jnp.sum(e, axis=0, keepdims=True))


def qkv_forward(normed, weight, bias_ref, bias_row, target):
    width = normed.shape[1]
    for n in range(3):
        out = mm(normed, weight[:, cols(n, width)])
        if n != 1:
            out = out + bias_ref[bias_row, cols(n // 2, width)].astype(f32)
        target[:, cols(n, width)] = out.astype(bf16)


def attend_probs(mixed, same_ref, probs):
    width = mixed.shape[1] // 3
    count = width // PAIR
    same = same_ref[...] > 0.5
    for p in range(count):
        q = mixed[:, cols(p, PAIR)]
        k = mixed[:, cols(p + count, PAIR)]
        for h, key in enumerate(halves(k)):
            probs[2 * p + h] = soft_columns(key, q, same).astype(bf16)


def attend_context(mixed, probs, target):
    width = mixed.shape[1] // 3
    count = width // PAIR
    for p in range(count):
        v = mixed[:, cols(p + 2 * count, PAIR)]
        total = sum(mm(value.T, probs[2 * p + h]) for h, value in enumerate(halves(v)))
        target[:, cols(p, PAIR)] = total.T.astype(bf16)


def attend_grad(mixed, probs, dcontext, target):
    width = mixed.shape[1] // 3
    count = width // PAIR
    for p in range(count):
        q = mixed[:, cols(p, PAIR)]
        k = mixed[:, cols(p + count, PAIR)]
        v = mixed[:, cols(p + 2 * count, PAIR)]
        d = dcontext[:, cols(p, PAIR)]
        dq = dk = dv = 0.0
        for h, (key, value, query, dc) in enumerate(zip(halves(k), halves(v), halves(q), halves(d))):
            low = probs[2 * p + h]
            soft = low.astype(f32)
            dsoft = mm_nt(value, d)
            inner = jnp.sum(soft * dsoft, axis=0, keepdims=True)
            dscores = (soft * (dsoft - inner)).astype(bf16)
            dv = dv + mm(low, dc)
            dk = dk + mm(dscores, query)
            dq = dq + mm(key.T, dscores)
        target[:, cols(p, PAIR)] = (dq * scale).T.astype(bf16)
        target[:, cols(p + count, PAIR)] = (dk * scale).astype(bf16)
        target[:, cols(p + 2 * count, PAIR)] = dv.astype(bf16)


def forward_kernel(
    bits, lengths, timesteps, inputs, a_gain, a_shift, qv, out_b, m_gain, m_shift, up_b, down_b,
    cotangent, table, qkv_w, out_w, up_w, down_w,
    x1, h0, h1, h3, last, na, mixed, ctx, nm, act, slope, dinner, dmixed, g2, g3, vec,
    v_table, v_qkv, v_out, v_up, v_down, v_h, v_na, v_mixed, v_ctx, v_nm, v_act, v_slope, v_x, v_g,
    v_dinner, v_dctx, v_dmixed, v_dn, v_gmid, v_gout, v_probs, same, sems,
):
    copies = Copies(sems)
    rows, width = inputs.shape
    wide = up_w.shape[2]
    docs = lengths.shape[1]
    l_table = copies.start(table, v_table)
    loads = []
    for l in range(LAYERS):
        loads.append(
            [
                copies.start(w.at[l], v.at[l])
                for w, v in ((qkv_w, v_qkv), (out_w, v_out), (up_w, v_up), (down_w, v_down))
            ]
        )
    l_g = copies.start(cotangent, v_g)
    bounds = bounds_of(lengths)
    same[...] = doc_mask(bounds, rows).astype(f32)
    tail = x1.shape[0] - rows
    which = lax.broadcasted_iota(jnp.int32, (tail, width), 0)
    note = jnp.zeros((tail, width), f32)
    for k, bound in enumerate(bounds):
        note = jnp.where(which == k, bound.astype(f32), note)
    v_x[...] = note.astype(bf16)
    copies.send(v_x, x1.at[pl.ds(rows, tail)])
    steps = table.shape[0]
    doc = lax.broadcasted_iota(jnp.int32, (16, steps), 0)
    wanted = jnp.full((16, steps), -1, jnp.int32)
    for k in range(docs):
        wanted = jnp.where(doc == k, timesteps[0, k], wanted)
    step = lax.broadcasted_iota(jnp.int32, (16, steps), 1)
    onehot = (step == wanted).astype(f32).astype(bf16)
    token = lax.broadcasted_iota(jnp.int32, (rows, 16), 0)
    own = sum((token >= bound).astype(jnp.int32) for bound in bounds)
    chosen = (own == lax.broadcasted_iota(jnp.int32, (rows, 16), 1)).astype(f32).astype(bf16)
    l_table.wait()
    embedded = mm(chosen, mm(onehot, v_table[...]).astype(bf16))
    v_h[0] = (inputs[...].astype(f32) + embedded).astype(bf16)
    for l in range(LAYERS):
        h_in, h_mid = v_h.at[2 * l], v_h.at[2 * l + 1]
        h_out = v_h.at[2 * l + 2]
        v_na[l] = norm_forward(h_in[...], a_gain[l : l + 1, :], a_shift[l : l + 1, :])
        loads[l][0].wait()
        qkv_forward(v_na[l], v_qkv.at[l], qv, slice(l, l + 1), v_mixed.at[l])
        copies.send(v_na.at[l], na.at[l])
        if l == 0:
            copies.send(v_mixed.at[l], mixed)
        attend_probs(v_mixed.at[l], same, v_probs)
        attend_context(v_mixed.at[l], v_probs, v_ctx.at[l])
        copies.send(v_ctx.at[l], ctx.at[l])
        loads[l][1].wait()

        def project(n):
            at = cols(n)
            out = h_in[:, at].astype(f32) + mm(v_ctx[l], v_out[l, :, at])
            h_mid[:, at] = (out + out_b[l : l + 1, at].astype(f32)).astype(bf16)

        loop(width // BLOCK, project)
        v_nm[l] = norm_forward(h_mid[...], m_gain[l : l + 1, :], m_shift[l : l + 1, :])
        copies.send(v_nm.at[l], nm.at[l])
        loads[l][2].wait()

        def expand(n):
            at = cols(n)
            inner = mm(v_nm[l], v_up[l, :, at]) + up_b[l : l + 1, at].astype(f32)
            active, s = gelu_pair(inner)
            v_act[l, :, at] = active.astype(bf16)
            v_slope[l, :, at] = s.astype(bf16)

        loop(wide // BLOCK, expand)
        copies.send(v_act.at[l], act.at[l])
        if l == 0:
            copies.send(v_slope.at[l], slope)
        loads[l][3].wait()

        def contract(n):
            at = cols(n)
            out = h_mid[:, at].astype(f32) + mm(v_act[l], v_down[l, :, at])
            h_out[:, at] = (out + down_b[l : l + 1, at].astype(f32)).astype(bf16)

        loop(width // BLOCK, contract)
    for k, h in ((0, h0), (1, h1), (3, h3), (4, last)):
        copies.send(v_h.at[k], h)
    by_x = jnp.where(bits[0] == 0, 2, 0)
    copies.send(v_h.at[by_x], x1.at[pl.ds(0, rows)])
    l_g.wait()
    l = LAYERS - 1
    backward_part(
        l, copies, v_g, a_gain, m_gain, v_h.at[2 * l], v_h.at[2 * l + 1], v_mixed.at[l], v_slope.at[l],
        v_probs, (v_qkv.at[l], v_out.at[l], v_up.at[l], v_down.at[l]), lambda *name: None, vec,
        dinner.at[l], dmixed.at[l], v_dinner, v_dmixed, v_dctx, v_dn, v_gmid, v_gout,
    )
    copies.send(v_gmid, g3)
    copies.send(v_gout, g2)
    copies.finish()


def norm_backward(h, gain, dnormed, upstream, vec, at_gain, at_shift, target):
    width = h.shape[1]
    xhat, rstd = norm_stats(h[...])
    dn = dnormed[...]
    e = dn * gain.astype(f32)
    grad = (
        e - jnp.mean(e, axis=-1, keepdims=True) - xhat * jnp.mean(e * xhat, axis=-1, keepdims=True)
    ) * rstd
    target[...] = (upstream[...].astype(f32) + grad).astype(bf16)
    vec[:, at_gain : at_gain + width] = jnp.sum(dn * xhat, axis=0, keepdims=True)
    vec[:, at_shift : at_shift + width] = jnp.sum(dn, axis=0, keepdims=True)


def colsum(x):
    return jnp.sum(x.astype(f32), axis=0, keepdims=True)


def write_notes(me, timesteps, vectors, doc_sums, notes):
    _, _, shares, ahead, width = notes.shape
    docs = timesteps.shape[1]
    one = width // shares
    per = width // one
    for core, vec in enumerate(vectors):
        count = vec.shape[1] // width
        rows = [vec[:, k * width : (k + 1) * width] for k in range(count)]
        rows.append(jnp.zeros((ahead - count, width), f32))
        value = jnp.concatenate(rows, axis=0).astype(bf16)
        for s in range(shares):
            notes[core, 0, s] = value
    row = lax.broadcasted_iota(jnp.int32, (ahead, width), 0)
    lane = lax.broadcasted_iota(jnp.int32, (ahead, width), 1)
    docs_rows = notes_rows(shares, docs, width)
    marks = jnp.zeros((ahead, width), f32)
    sums = [jnp.zeros((ahead, width), f32) for _ in range(shares)]
    for k in range(docs):
        number = me * docs + k
        r, j = number // per, number % per
        step = timesteps[0, k]
        here = lane == j * docs_rows + r
        marks = jnp.where(here & (row == 0), (step // 32).astype(f32), marks)
        marks = jnp.where(here & (row == 1), (step % 32).astype(f32), marks)
        here = (row == r) & (lane >= j * one) & (lane < (j + 1) * one)
        wide = jnp.broadcast_to(doc_sums[k : k + 1, :], (8, width))
        for s in range(shares):
            turned = pltpu.roll(wide, lax.rem((j - s) * one + width, width), 1)
            turned = jnp.broadcast_to(turned[:1], (ahead, width))
            sums[s] = jnp.where(here, turned, sums[s])
    for s in range(shares):
        notes[0, 1, s] = sums[s].astype(bf16)
        notes[1, 1, s] = marks.astype(bf16)


def notes_rows(shares, docs, width):
    return 4 * shares * docs * (width // shares) // width


def backward_part(
    layer, copies, g, a_gain, m_gain, h_a, h_m, mixed, slope, probs, weights, wait, vec, dinner, dmixed,
    v_dinner, v_dmixed, v_dctx, v_dn, v_gmid, v_gout,
):
    v_qkv, v_out, v_up, v_down = weights
    rows, width = g.shape
    wide = v_up.shape[1]
    one_row = slice(layer, layer + 1)
    at_qv, at_mshift, at_downb, at_upb = 4 * width, 6 * width, 7 * width, 8 * width
    vec[:, at_downb : at_downb + width] = colsum(g[...])
    for n in range(wide // BLOCK):
        wait("down", n)
    wait("slope")
    for n in range(wide // BLOCK):
        at = cols(n)
        dact = mm_nt(g[...], v_down[at, :])
        di = (dact * slope[:, at].astype(f32)).astype(bf16)
        v_dinner[:, at] = di
        vec[:, at_upb + n * BLOCK : at_upb + (n + 1) * BLOCK] = colsum(di)
    copies.send(v_dinner, dinner)
    wait("up")
    v_dn[...] = mm_nt(v_dinner[...], v_up[...])
    wait("h_m")
    norm_backward(h_m, m_gain[one_row, :], v_dn, g, vec, 3 * width, at_mshift, v_gmid)
    vec[:, 2 * width : 3 * width] = colsum(v_gmid[...])
    wait("out")
    v_dctx[...] = mm_nt(v_gmid[...], v_out[...]).astype(bf16)
    attend_grad(mixed, probs, v_dctx, v_dmixed)
    copies.send(v_dmixed, dmixed)
    vec[:, at_qv : at_qv + width] = colsum(v_dmixed[:, :width])
    vec[:, at_qv + width : at_qv + 2 * width] = colsum(v_dmixed[:, 2 * width :])
    wait("qkv")
    v_dn[...] = mm_nt(v_dmixed[...], v_qkv[...])
    wait("h_a")
    norm_backward(h_a, a_gain[one_row, :], v_dn, v_gmid, vec, 0, width, v_gout)


def backward_kernel(
    bits, lengths, timesteps, a_gain, m_gain, vec_upper, g, g_upper, h_a, h_m, mixed, slope,
    qkv_w, out_w, up_w, down_w, _, __,
    dinner, dmixed, g_out, send, own, notes,
    v_qkv, v_out, v_up, v_down, v_g, v_ha, v_hm, v_mixed, v_slope, v_dinner, v_dctx, v_dmixed, v_dn,
    v_gmid, v_gout, v_trade, v_notes, vec, v_probs, v_touch, same, sems,
):
    copies = Copies(sems)
    rows, width = h_a.shape
    wide = up_w.shape[2]
    loads = {"mixed": copies.start(mixed, v_mixed), "g": copies.start(g, v_g)}
    for n in range(wide // BLOCK):
        loads["down", n] = copies.start(down_w.at[0, cols(n)], v_down.at[cols(n)])
    for name, source, target in (
        ("slope", slope, v_slope), ("up", up_w.at[0], v_up), ("h_m", h_m, v_hm), ("out", out_w.at[0], v_out),
        ("qkv", qkv_w.at[0], v_qkv), ("h_a", h_a, v_ha), ("g_upper", g_upper, v_trade.at[0]),
    ):
        loads[name] = copies.start(source, target)
    wait = lambda *name: loads[name if len(name) > 1 else name[0]].wait()
    v_touch[...] = jnp.zeros_like(v_touch)
    tile = (pl.ds(0, 16), pl.ds(0, 128))
    touched = [
        copies.start(v_touch, ref.at[tile])
        for ref in (g_out, send, own, notes.at[0, 0, 0], dinner.at[0], dmixed.at[0])
    ]
    same[...] = doc_mask(bounds_of(lengths), rows).astype(f32)
    wait("mixed")
    attend_probs(v_mixed, same, v_probs)
    wait("g")
    for copy in touched:
        copy.wait()
    backward_part(
        0, copies, v_g, a_gain, m_gain, v_ha, v_hm, v_mixed, v_slope, v_probs,
        (v_qkv, v_out, v_up, v_down), wait, vec, dinner.at[0], dmixed.at[0], v_dinner, v_dmixed, v_dctx,
        v_dn, v_gmid, v_gout,
    )
    copies.send(v_gout, g_out)
    v_trade[1] = v_gmid[...]
    wait("g_upper")
    copies.send(v_trade.at[bits[0]], send)
    copies.send(v_trade.at[1 - bits[0]], own)
    count = lengths.shape[1]
    doc = lax.broadcasted_iota(jnp.int32, (16, rows), 0)
    token = lax.broadcasted_iota(jnp.int32, (16, rows), 1)
    index = sum((token >= bound).astype(jnp.int32) for bound in bounds_of(lengths))
    onehot = ((index == doc) & (doc < count)).astype(f32).astype(bf16)
    doc_sums = mm(onehot, v_gout[...])
    write_notes(bits[3], timesteps, (vec, vec_upper), doc_sums, v_notes)
    copies.send(v_notes, notes)
    copies.finish()


def relative(bits, shard, places):
    z, x = shard // 2, lax.rem(shard, 2)
    return lax.rem(bits[5] - z + places, places), lax.rem(x + bits[0], 2)


def pick_layer(ref, layer, at=slice(None)):
    return jnp.where(layer == 0, ref[0:1, at].astype(f32), ref[1:2, at].astype(f32))


def feed_weight_kernel(
    layer, bits, h, g, own_g, own_act, own_nm, own_dinner, gain, shift, up_b, up_w, down_w, *rest
):
    *outs, v_up, v_down, v_nm, v_own, v_g, v_n, v_act, v_dinner, v_send, v_keep, sems = rest
    copies = Copies(sems)
    rows, width = h.shape
    wide = up_w.shape[2]
    quarter = width // 4
    side, core = bits[1], bits[2]
    one_row = slice(layer, layer + 1)
    l_nm = copies.start(own_nm.at[layer], v_own)
    order = [2 * side + 1 - core, 2 * side + core, 2 - 2 * side, 3 - 2 * side]
    size = wide // 4
    loads = []
    for n, block in enumerate(order):
        at = pl.ds(pl.multiple_of(block * size, 128), size)
        load = [copies.start(up_w.at[layer, :, at], v_up.at[n])]
        if n < 2:
            load.append(copies.start(down_w.at[layer, at], v_down.at[n]))
        load.append(copies.start(own_act.at[layer, :, at], v_act.at[n, pl.ds(0, rows)]))
        if n < 2:
            load.append(copies.start(own_dinner.at[layer, :, at], v_dinner.at[n, pl.ds(0, rows)]))
        loads.append(load)
    normed = norm_forward(h[...], gain[one_row, :], shift[one_row, :])
    v_nm[...] = normed
    v_n[:, rows:] = normed.T
    for k in range(2):
        part = 2 * side + (1 - core if k == 0 else core)
        at = pl.ds(pl.multiple_of(part * quarter // 128 * 128, 128), 2 * 128)
        for ref, first in ((own_g, 0), (g, rows)):
            piece = ref[:, at].T
            shifted = jnp.where(part % 2 == 0, piece[:quarter].astype(f32), piece[256 - quarter :].astype(f32))
            v_g[k * quarter : (k + 1) * quarter, first : first + rows] = shifted.astype(bf16)
    l_nm.wait()
    v_n[:, :rows] = v_own[...].T
    flat = len(v_send.shape) == 2

    def feed(n, block):
        at = pl.ds(pl.multiple_of(block * size, 128), size)
        inner = mm(v_nm[...], v_up[n]) + up_b[one_row, at].astype(f32)
        active, slope = gelu_pair(inner)
        v_act[n, rows:] = active.astype(bf16)
        down = mm(v_g[...], v_act[n]).astype(bf16)
        for k, target in ((0, v_send), (1, v_keep)):
            half = down[k * quarter : (k + 1) * quarter]
            if flat:
                target[:quarter, at] = half
                continue
            places, _, _, one, _ = target.shape
            share = wide // (2 * places)
            for m in range(size // share):
                back, across = relative(bits, block * (size // share) + m, places)
                for p in range(quarter // one):
                    piece = half[p * one : (p + 1) * one, m * share : (m + 1) * share]
                    target[back, across, 0, :, p * share : (p + 1) * share] = piece
        if n < 2:
            dact = mm_nt(g[...], v_down[n])
            v_dinner[n, rows:] = (dact * slope).astype(bf16)
            up = mm(v_n[...], v_dinner[n]).astype(bf16)
            target = v_send if n == 0 else v_keep
            if flat:
                target[quarter:, :size] = up
                return
            places, _, _, one, _ = target.shape
            for m in range(2 * places):
                back, across = relative(bits, m, places)
                target[back, across, 1] = up[m * one : (m + 1) * one]

    def leave(n, block):
        if flat:
            return
        places = v_send.shape[0]
        count = 2 * places // 4
        for target, out in ((v_send, outs[-2]), (v_keep, outs[-1])):
            for m in range(count):
                back, across = relative(bits, block * count + m, places)
                copies.send(target.at[back, across, 0], out.at[back, across, 0])
        if n < 2:
            target, out = ((v_send, outs[-2]), (v_keep, outs[-1]))[n]
            copies.send(target.at[:, :, 1], out.at[:, :, 1])

    for group in ((0,), (1, 2, 3)):
        for n in group:
            for load in loads[n]:
                load.wait()
        for n in group:
            feed(n, order[n])
        for n in group:
            leave(n, order[n])
    if flat:
        copies.send(v_send, outs[-2])
        copies.send(v_keep, outs[-1])
    copies.finish()


def attend_weight_kernel(
    bits, hx, g, own_g, own_na, own_ctx, own_dmixed, notes, gain, shift, qv, qkv_w, out_w,
    send, keep,
    v_qkv, v_out, v_na, v_mixed, v_dctx, v_dmixed, v_ctx, v_left, v_right, v_own, v_own_ctx,
    v_own_dmixed, v_bias, v_send, v_keep, v_notes, v_probs, same, sems,
):
    copies = Copies(sems)
    rows, width = g.shape
    layer, core = bits[0], bits[2]
    l_out = copies.start(out_w.at[layer], v_out)
    l_qkv = copies.start(qkv_w.at[layer], v_qkv)
    l_ctx = copies.start(own_ctx.at[layer], v_own_ctx)
    l_own = copies.start(own_na.at[layer], v_own)
    l_dmixed = copies.start(own_dmixed.at[layer], v_own_dmixed)
    l_notes = copies.start(notes, v_notes)
    note = hx[rows:, :].astype(f32)
    bounds = [note[k : k + 1, :rows].astype(jnp.int32) for k in range(2)]
    same[...] = doc_mask(bounds, rows).astype(f32)
    v_bias[...] = pick_layer(qv, layer)
    v_na[...] = norm_forward(hx[:rows, :], pick_layer(gain, layer), pick_layer(shift, layer))
    l_out.wait()
    v_dctx[...] = mm_nt(g[...], v_out[...]).astype(bf16)
    l_qkv.wait()
    qkv_forward(v_na[...], v_qkv, v_bias, slice(0, 1), v_mixed)
    attend_probs(v_mixed, same, v_probs)
    attend_context(v_mixed, v_probs, v_ctx)
    attend_grad(v_mixed, v_probs, v_dctx, v_dmixed)
    part = width // 2
    shares, ahead = notes.shape[2], notes.shape[3]
    share = width // shares
    sides = [lax.rem(bits[1] + h, 2) for h in range(2)]
    places = [relative(bits, s, shares // 2) for s in range(shares)]

    def put(target, k, n, out):
        for s, (back, across) in enumerate(places):
            piece = out[s * share : (s + 1) * share].astype(bf16)
            target[sides[n // 2], back, across, ahead:, (n % 2) * part : (n % 2 + 1) * part] = piece

    l_notes.wait()
    for k in range(2):
        target = v_send if k == 0 else v_keep
        for h in range(2):
            for s, (back, across) in enumerate(places):
                target[sides[h], back, across, :ahead] = v_notes[1 - core if k == 0 else core, h, s]
    l_ctx.wait()
    v_left[:, :rows] = v_own_ctx[...].T
    v_left[:, rows:] = v_ctx[...].T
    for k in range(2):
        side = jnp.where(k == 0, 1 - core, core)
        at = pl.ds(pl.multiple_of(side * part, 128), part)
        v_right[k, :rows, :part] = own_g[:, at]
        v_right[k, rows:, :part] = g[:, at]
        put(v_send if k == 0 else v_keep, k, 0, mm(v_left[...], v_right[k, :, :part]))
    l_own.wait()
    l_dmixed.wait()
    v_left[:, :rows] = v_own[...].T
    v_left[:, rows:] = v_na[...].T
    for k in range(2):
        side = jnp.where(k == 0, 1 - core, core)
        target = v_send if k == 0 else v_keep
        at = pl.ds(pl.multiple_of(side * 3 * part, 128), 3 * part)
        v_right[k, :rows] = v_own_dmixed[:, at]
        v_right[k, rows:] = v_dmixed[:, at]
        out = mm(v_left[...], v_right[k])
        for n in range(1, 4):
            put(target, k, n, out[:, (n - 1) * part : n * part])
        copies.send(target, send if k == 0 else keep)
    copies.finish()


def feed_finish_kernel(layer, bits, own, other, beside, *rest):
    up_out, down_out, v_up, v_down, sems = rest[-5:]
    copies = Copies(sems)
    side, core = bits[1], bits[2]
    rows, width = own.shape[1:]
    share, quarter = v_down.shape[0], width // 4
    pieces = width // share
    for ref, chip, half in (
        (own, side, core), (other, 1 - side, core), (beside.at[0], side, 1 - core), (beside.at[1], 1 - side, 1 - core)
    ):
        part = 2 * chip + half
        v_up[:, pl.ds(pl.multiple_of(part * width, 128), width)] = ref[1].astype(f32)
        down = jnp.concatenate(
            [ref[0, :, p * share : (p + 1) * share].astype(f32) for p in range(pieces)], axis=0
        ).T
        for at in range(4):

            @pl.when(part == at)
            def _():
                v_down[:, at * quarter : (at + 1) * quarter] = down

    copies.send(v_up, up_out.at[layer])
    copies.send(v_down, down_out.at[layer])
    copies.finish()


def attend_finish_kernel(
    ahead, docs_rows, bits, own, other, beside,
    table, a_gain, a_shift, qkv, a_qv, out, a_out, m_gain, m_shift, m_up, m_down, notes, sums,
):
    place_x, side, core = bits[0], bits[1], bits[2]
    width = own.shape[2]
    part = width // 2

    def put(ref, first, which):
        for relative in range(2):
            layer = jnp.where(relative == 0, place_x, 1 - place_x)
            value = ref[relative, ahead:, :].astype(f32)
            base = 3 * part * which
            if first:
                out[layer, :, pl.ds(pl.multiple_of(which * part, 128), part)] = value[:, :part]
                qkv[layer, :, pl.ds(pl.multiple_of(base, 128), part)] = value[:, part:]
            else:
                qkv[layer, :, pl.ds(pl.multiple_of(base + part, 128), width)] = value

    def note(ref, which, half):
        notes[which, half] = ref[0, :ahead, :].astype(f32) + ref[1, :ahead, :].astype(f32)

    for half in range(2):
        for here, mine in ((own, 0), (other, 1)):

            @pl.when((side == half) == (mine == 0))
            def _():
                put(here, half == 0, core)
                put(beside.at[mine], half == 0, 1 - core)

                note(here, core, half)
                note(beside.at[mine], 1 - core, half)

    index = bits[4]
    one = a_gain.shape[1]
    for l in range(LAYERS):
        value = notes[l, 0]
        at = 0
        for ref in (a_gain, a_shift, a_out, m_gain, a_qv, m_shift, m_down, m_up):
            size = ref.shape[1]
            count = size // one
            place = index * size
            line = value[at : at + 1]
            for k in range(1, count):
                line = jnp.where(place // width == k, value[at + k : at + k + 1], line)
            line = jnp.broadcast_to(line, (8, width))
            turned = pltpu.roll(line, lax.rem(width - lax.rem(place, width), width), 1)
            ref[l : l + 1, :] = turned[:1, :size]
            at += count
    per, count = width // one, (width // one) * docs_rows
    high, low = notes[1, 1, 0:1, :count], notes[1, 1, 1:2, :count]
    steps = (high * 32.0 + low).astype(jnp.int32)
    for j in range(per):
        sums[j * docs_rows : (j + 1) * docs_rows, :] = notes[0, 1, :docs_rows, j * one : (j + 1) * one]
    step = lax.broadcasted_iota(jnp.int32, (table.shape[1], count), 0)
    onehot = (step == steps).astype(f32).astype(bf16)
    table[...] = mm_nt(sums[...].T.astype(bf16), onehot)


def call(kernel, operands, specs, outs, out_specs, scratch, copies, aliases=None, limit=LIMIT):
    return pl.pallas_call(
        kernel,
        out_shape=[jax.ShapeDtypeStruct(s, d) for s, d in outs],
        in_specs=specs,
        out_specs=out_specs,
        scratch_shapes=[pltpu.VMEM(s, d) for s, d in scratch]
        + [pltpu.SemaphoreType.DMA((copies,))] * (copies > 0),
        input_output_aliases=aliases or {},
        compiler_params=pltpu.CompilerParams(vmem_limit_bytes=limit),
        cost_estimate=pl.CostEstimate(flops=0, bytes_accessed=0, transcendentals=0),
    )(*operands)


def swap(x, axis, by):
    size = lax.axis_size(axis)
    return lax.ppermute(x, axis, [(i, i ^ by) for i in range(size)])


def plus(a, b):
    return (a.astype(f32) + b.astype(f32)).astype(bf16)


def after(x, *others):
    return lax.optimization_barrier((x,) + others)[0] if others else x


class Ring:
    def __init__(self, term, place_z, nx, nz):
        self.term, self.nx, self.nz = term, nx, nz
        if nz > 4:
            groups = [[z * nx + x for z in range(nz)] for x in range(nx)]
            held = jnp.stack([term(s) for s in range(nz)]).astype(bf16)
            held = jnp.take(held, (place_z - jnp.arange(nz)) % nz, axis=0)
            self.carry = lax.psum_scatter(held, "dp", scatter_dimension=0, axis_index_groups=groups)
            self.at = nz
        else:
            self.carry = term(1).astype(bf16)
            self.at = 1

    def step(self, *others):
        if self.at < self.nz:
            self.at += 1
            size = self.nx * self.nz
            got = lax.ppermute(self.carry, "dp", [(d, (d + self.nx) % size) for d in range(size)])
            got = after(got, *others)
            self.carry = (got.astype(f32) + self.term(self.at % self.nz)).astype(bf16)

    def finish(self, *others):
        while self.at < self.nz:
            self.step(*others)
        return self.carry


def plus(*parts):
    return sum(part.astype(f32) for part in parts)


def local(
    inputs,
    timesteps,
    lengths,
    cotangent,
    time_table,
    attn_norm_gain,
    attn_norm_bias,
    qkv_weight,
    qv_bias,
    out_weight,
    out_bias,
    mlp_norm_gain,
    mlp_norm_bias,
    up_weight,
    up_bias,
    down_weight,
    down_bias,
):
    place = lax.axis_index("section")
    side, core = place // 2, place % 2
    dp = lax.axis_size("dp")
    nx, nz = 2, dp // 2
    index = lax.axis_index("dp")
    place_z, place_x = index // nx, index % nx
    rows, width = inputs.shape
    wide = up_weight.shape[2]
    docs = lengths.shape[1]
    step_count = time_table.shape[0]
    me = index * lax.axis_size("section") + place
    bits = jnp.stack([place_x, side, core, me, index, place_z]).astype(jnp.int32)

    ahead, docs_rows = 16, notes_rows(dp, docs, width)
    tok, tok2 = (rows, width), (LAYERS, rows, width)
    peer_cot = swap(cotangent, "section", 2)
    full, thrice = ((LAYERS, rows, wide), bf16), ((LAYERS, rows, 3 * width), bf16)
    x1, h0, h1, h3, last, na, mixed, ctx, nm, act, slope, dinner, dmixed, g2, g3, vec1 = call(
        forward_kernel,
        [bits, lengths, timesteps, inputs, attn_norm_gain, attn_norm_bias, qv_bias, out_bias,
         mlp_norm_gain, mlp_norm_bias, up_bias, down_bias, cotangent, time_table, qkv_weight, out_weight,
         up_weight, down_weight],
        [SMEM] * 3 + [VMEM] * 9 + [ANY] * 6,
        [((rows + 16, width), bf16)] + [(tok, bf16)] * 4
        + [(tok2, bf16), ((rows, 3 * width), bf16), (tok2, bf16), (tok2, bf16), full,
           ((rows, wide), bf16), full, thrice, (tok, bf16), (tok, bf16), ((1, 12 * width), f32)],
        [ANY] * 15 + [VMEM],
        [(time_table.shape, bf16), (qkv_weight.shape, bf16), (out_weight.shape, bf16),
         (up_weight.shape, bf16), (down_weight.shape, bf16), ((2 * LAYERS + 1,) + tok, bf16),
         (tok2, bf16), thrice, (tok2, bf16), (tok2, bf16), full, full, ((16, width), bf16), (tok, bf16),
         ((rows, wide), bf16), (tok, bf16), ((rows, 3 * width), bf16), (tok, f32), (tok, bf16), (tok, bf16),
         ((width // HDIM, rows, rows), bf16), ((rows, rows), f32)],
        40,
    )
    peer_h3 = swap(h3, "section", 2)
    peer_h1 = swap(h1, "section", 2)
    peer_hx = swap(x1, "dp", 1)
    peer_g2 = swap(g2, "section", 2)
    dinner, dmixed, g0, x2, own_ga, notes = call(
        backward_kernel,
        [bits, lengths, timesteps, attn_norm_gain, mlp_norm_gain, vec1, g2, g3, h0, h1, mixed, slope,
         qkv_weight, out_weight, up_weight, down_weight, dinner, dmixed],
        [SMEM] * 3 + [VMEM] * 3 + [ANY] * 12,
        [full, thrice, (tok, bf16), (tok, bf16), (tok, bf16), ((2, 2, dp, ahead, width), bf16)],
        [ANY] * 6,
        [(qkv_weight.shape[1:], bf16), (out_weight.shape[1:], bf16), (up_weight.shape[1:], bf16),
         (down_weight.shape[1:], bf16), (tok, bf16), (tok, bf16), (tok, bf16), ((rows, 3 * width), bf16),
         ((rows, wide), bf16), ((rows, wide), bf16), (tok, bf16), ((rows, 3 * width), bf16), (tok, f32),
         (tok, bf16), (tok, bf16), ((2,) + tok, bf16), ((2, 2, dp, ahead, width), bf16),
         ((1, 12 * width), f32), ((width // HDIM, rows, rows), bf16), ((16, 128), bf16),
         ((rows, rows), f32)],
        32,
        {16: 0, 17: 1},
    )
    peer_ga = swap(x2, "dp", 1)

    share, one, half, quarter = wide // dp, width // dp, width // 2, width // 4
    flat = share % 128 != 0

    def feed_weight(layer, h, g, own_g):
        shape = (quarter + width, wide) if flat else (nz, nx, 2, one, width)
        send, keep = call(
            functools.partial(feed_weight_kernel, layer),
            [bits, h, g, own_g, act, nm, dinner, mlp_norm_gain, mlp_norm_bias, up_bias, up_weight,
             down_weight],
            [SMEM, VMEM, VMEM, VMEM, HBM, HBM, HBM, VMEM, VMEM, VMEM, HBM, HBM],
            [(shape, bf16)] * 2,
            [HBM] * 2,
            [((4, width, wide // 4), bf16), ((2, wide // 4, width), bf16), (tok, bf16), (tok, bf16),
             ((2 * quarter, 2 * rows), bf16), ((width, 2 * rows), bf16),
             ((4, 2 * rows, wide // 4), bf16), ((2, 2 * rows, wide // 4), bf16),
             (shape, bf16), (shape, bf16)],
            40,
            limit=MIDDLE,
        )
        if flat:

            def sort(x):
                down = x[:quarter].reshape(-1, one, dp, share).transpose(2, 1, 0, 3)
                both = jnp.stack([down.reshape(dp, one, width), x[quarter:, :width].reshape(dp, one, width)], axis=1)
                both = jnp.take(both.reshape(nz, nx, 2, one, width), (place_z - jnp.arange(nz)) % nz, axis=0)
                return jnp.where(place_x == 0, both, both[:, ::-1])

            send, keep = sort(send), sort(keep)
        return keep, send

    def trade(keep, send, *others):
        return keep, swap(after(send, *others), "section", 1)

    keep1, send1 = feed_weight(1, peer_h3, peer_cot, after(cotangent, g0, peer_hx))
    keep1, near1 = trade(keep1, send1, peer_ga, peer_h1, peer_g2)
    ring1 = Ring(lambda s: plus(keep1[s], near1[s]), place_z, nx, nz)

    at_send, at_keep = call(
        attend_weight_kernel,
        [bits, after(peer_hx, ring1.carry), peer_ga, own_ga, na, ctx, dmixed, notes, attn_norm_gain, attn_norm_bias,
         qv_bias, qkv_weight, out_weight],
        [SMEM, VMEM, VMEM, VMEM, HBM, HBM, HBM, HBM, VMEM, VMEM, VMEM, HBM, HBM],
        [((2, nz, nx, ahead + one, width), bf16)] * 2,
        [HBM] * 2,
        [((width, 3 * width), bf16), ((width, width), bf16), (tok, bf16), ((rows, 3 * width), bf16),
         (tok, bf16), ((rows, 3 * width), bf16), (tok, bf16), ((width, 2 * rows), bf16),
         ((2, 2 * rows, 3 * half), bf16), (tok, bf16), (tok, bf16), ((rows, 3 * width), bf16),
         ((1, 2 * width), f32), ((2, nz, nx, ahead + one, width), bf16),
         ((2, nz, nx, ahead + one, width), bf16), ((2, 2, dp, ahead, width), bf16),
         ((width // HDIM, rows, rows), bf16), ((rows, rows), f32)],
        8,
        limit=MIDDLE,
    )

    ring1.step(at_keep)
    order = [s % nz for s in range(1, nz + 1)]
    keep_a, near_a = trade(at_keep, at_send, ring1.carry)
    away_a = {s: plus(keep_a[1, s], near_a[1, s]).astype(bf16) for s in order}
    far_a = {s: swap(away_a[s], "section", 2) for s in order}
    keep0, send0 = feed_weight(0, after(peer_h1, ring1.carry, *away_a.values()), peer_g2, g2)
    ring1.step(keep0)
    far_a[1] = after(far_a[1], ring1.carry)
    ring_a = Ring(lambda s: plus(keep_a[0, s], near_a[0, s], far_a[s]), place_z, nx, nz)
    keep0, near0 = trade(keep0, send0, ring_a.carry)
    away0 = {s: plus(keep0[s, 1], near0[s, 1]).astype(bf16) for s in order}
    far0 = {s: swap(away0[s], "dp", 1) for s in order}
    ring0 = Ring(lambda s: plus(keep0[s, 0], near0[s, 0], far0[s]), place_z, nx, nz)
    ring_a.step(*away0.values())
    both = ring1.finish(ring0.carry, ring_a.carry)
    own1 = plus(both[0], swap(both[1], "dp", 1)).astype(bf16)
    ring_a.step(both)
    ring0.step(both)

    def finish(kernel, own, outs, out_specs, scratch, copies=0, more=(), aliases=None, others=()):
        other = after(swap(own, "section", 2), *others)
        beside = swap(jnp.stack([own, other]), "section", 1)
        return call(kernel, [bits, own, other, beside] + list(more),
                    [SMEM] + [VMEM] * 3 + [ANY] * len(more), outs, out_specs, scratch, copies, aliases, SMALL)

    def feed_finish(layer, own, more=(), others=()):
        return finish(
            functools.partial(feed_finish_kernel, layer), own,
            [((LAYERS, one, wide), f32), ((LAYERS, share, width), f32)], [ANY] * 2,
            [((one, wide), f32), ((share, width), f32)], 2, more, {4: 0, 5: 1} if more else None, others,
        )

    grads = feed_finish(1, own1)
    both = ring_a.finish(own1)
    ring0.step(own1)
    own = jnp.stack([both[0], swap(both[1], "dp", 1)])
    grad_up, grad_down = feed_finish(0, ring0.finish(*grads), grads)
    pair = lambda n: ((LAYERS, n), f32)
    (grad_table, a_gain, a_shift, grad_qkv, a_qv, grad_out, a_out, m_gain, m_shift, m_up, m_down) = finish(
        functools.partial(attend_finish_kernel, ahead, docs_rows),
        own,
        [((one, step_count), f32), pair(one), pair(one), ((LAYERS, one, 3 * width), f32), pair(2 * one),
         ((LAYERS, one, width), f32), pair(one), pair(one), pair(one), pair(share), pair(one)],
        [VMEM] * 11,
        [((2, 2, ahead, width), f32), ((width // one * docs_rows, one), f32)],
    )

    return (
        last,
        g0,
        grad_table.T,
        a_gain,
        a_shift,
        grad_qkv,
        a_qv,
        grad_out,
        a_out,
        m_gain,
        m_shift,
        grad_up,
        m_up,
        grad_down,
        m_down,
    )


def solution(mesh):
    rows = P(("dp", "section"), None)
    in_specs = (rows,) * 4 + (P(),) * 13
    flat, deep = P(None, "dp"), P(None, "dp", None)
    out_specs = (rows, rows) + (flat, flat, flat, deep, flat, deep, flat, flat, flat, deep, flat, deep, flat)
    return jax.shard_map(local, mesh=mesh, in_specs=in_specs, out_specs=out_specs, check_vma=False)
```

```python
import functools

import jax
import jax.numpy as jnp
from jax import lax
from jax.experimental import pallas as pl
from jax.experimental.pallas import tpu as pltpu
from jax.sharding import PartitionSpec as P

HDIM = 64
PAIR = 2 * HDIM
LAYERS = 2
BLOCK = 768
LIMIT = 60 * 1024 * 1024
MIDDLE = 40 * 1024 * 1024
SMALL = 16 * 1024 * 1024

epsilon = 1e-05
masked_score = -1000000000.0
scale = HDIM ** (-0.5)
f32 = jnp.float32
bf16 = jnp.bfloat16
ANY = pl.BlockSpec(memory_space=pl.ANY)
VMEM = pl.BlockSpec(memory_space=pltpu.VMEM)
SMEM = pl.BlockSpec(memory_space=pltpu.SMEM)
HBM = pl.BlockSpec(memory_space=pltpu.HBM)


def mm(a, b):
    return lax.dot_general(a, b, (((1,), (0,)), ((), ())), preferred_element_type=f32)


def mm_nt(a, b):
    return lax.dot_general(a, b, (((1,), (1,)), ((), ())), preferred_element_type=f32)


def cols(n, size=BLOCK):
    return pl.ds(n * size, size)


rows_of = cols


def loop(count, body):
    for n in range(count):
        body(n)


class Copies:
    def __init__(self, sems):
        self.sems, self.used, self.pending = sems, 0, []

    def start(self, source, target):
        copy = pltpu.make_async_copy(source, target, self.sems.at[self.used])
        self.used += 1
        copy.start()
        return copy

    def send(self, source, target):
        self.pending.append(self.start(source, target))

    def finish(self):
        for copy in self.pending:
            copy.wait()


def norm_stats(hidden):
    full = hidden.astype(f32)
    centered = full - jnp.mean(full, axis=-1, keepdims=True)
    rstd = lax.rsqrt(jnp.mean(centered * centered, axis=-1, keepdims=True) + epsilon)
    return centered * rstd, rstd


def norm_forward(hidden, gain, shift):
    xhat, rstd = norm_stats(hidden)
    return (xhat * gain.astype(f32) + shift.astype(f32)).astype(bf16)


def gelu_pair(u):
    c, a = 0.7978845608028654, 0.044715
    square = u * u
    t = jnp.tanh(c * u * (1.0 + a * square))
    half = 0.5 * (1.0 + t)
    slope = half + 0.5 * u * (1.0 - t * t) * (c * (1.0 + 3.0 * a * square))
    return u * half, slope


def doc_mask(bounds, rows):
    one = lax.broadcasted_iota(jnp.int32, (rows, rows), 0)
    other = lax.broadcasted_iota(jnp.int32, (rows, rows), 1)
    left = sum((one >= b).astype(jnp.int32) for b in bounds)
    right = sum((other >= b).astype(jnp.int32) for b in bounds)
    return left == right


def bounds_of(len_ref):
    bounds, total = [], 0
    for k in range(len_ref.shape[1] - 1):
        total = total + len_ref[0, k]
        bounds.append(total)
    return bounds


def halves(x):
    low = lax.broadcasted_iota(jnp.int32, x.shape, 1) < HDIM
    zero = jnp.zeros_like(x)
    return jnp.where(low, x, zero), jnp.where(low, zero, x)


def soft_columns(key, query, same):
    s = jnp.where(same, mm_nt(key, query) * scale, masked_score)
    e = jnp.exp(s - jnp.max(s, axis=0, keepdims=True))
    return e * (1.0 / jnp.sum(e, axis=0, keepdims=True))


def qkv_forward(normed, weight, bias_ref, bias_row, target):
    width = normed.shape[1]
    for n in range(3):
        out = mm(normed, weight[:, cols(n, width)])
        if n != 1:
            out = out + bias_ref[bias_row, cols(n // 2, width)].astype(f32)
        target[:, cols(n, width)] = out.astype(bf16)


def attend_probs(mixed, same_ref, probs):
    width = mixed.shape[1] // 3
    count = width // PAIR
    same = same_ref[...] > 0.5
    for p in range(count):
        q = mixed[:, cols(p, PAIR)]
        k = mixed[:, cols(p + count, PAIR)]
        for h, key in enumerate(halves(k)):
            probs[2 * p + h] = soft_columns(key, q, same).astype(bf16)


def attend_context(mixed, probs, target):
    width = mixed.shape[1] // 3
    count = width // PAIR
    for p in range(count):
        v = mixed[:, cols(p + 2 * count, PAIR)]
        total = sum(mm(value.T, probs[2 * p + h]) for h, value in enumerate(halves(v)))
        target[:, cols(p, PAIR)] = total.T.astype(bf16)


def attend_grad(mixed, probs, dcontext, target):
    width = mixed.shape[1] // 3
    count = width // PAIR
    for p in range(count):
        q = mixed[:, cols(p, PAIR)]
        k = mixed[:, cols(p + count, PAIR)]
        v = mixed[:, cols(p + 2 * count, PAIR)]
        d = dcontext[:, cols(p, PAIR)]
        dq = dk = dv = 0.0
        for h, (key, value, query, dc) in enumerate(zip(halves(k), halves(v), halves(q), halves(d))):
            low = probs[2 * p + h]
            soft = low.astype(f32)
            dsoft = mm_nt(value, d)
            inner = jnp.sum(soft * dsoft, axis=0, keepdims=True)
            dscores = (soft * (dsoft - inner)).astype(bf16)
            dv = dv + mm(low, dc)
            dk = dk + mm(dscores, query)
            dq = dq + mm(key.T, dscores)
        target[:, cols(p, PAIR)] = (dq * scale).T.astype(bf16)
        target[:, cols(p + count, PAIR)] = (dk * scale).astype(bf16)
        target[:, cols(p + 2 * count, PAIR)] = dv.astype(bf16)


def forward_kernel(
    bits, lengths, timesteps, inputs, a_gain, a_shift, qv, out_b, m_gain, m_shift, up_b, down_b,
    cotangent, table, qkv_w, out_w, up_w, down_w,
    x1, h0, h1, h3, last, na, mixed, ctx, nm0, nm1, act0, act1, slope, dinner, dmixed, g2, g3, vec,
    v_table, v_qkv, v_out, v_up, v_down, v_h, v_na, v_mixed, v_ctx, v_nm, v_act, v_slope, v_x, v_g,
    v_dinner, v_dctx, v_dmixed, v_dn, v_gmid, v_gout, v_probs, same, sems,
):
    copies = Copies(sems)
    rows, width = inputs.shape
    wide = up_w.shape[2]
    docs = lengths.shape[1]
    l_table = copies.start(table, v_table)
    loads = []
    for l in range(LAYERS):
        loads.append(
            [
                copies.start(w.at[l], v.at[l])
                for w, v in ((qkv_w, v_qkv), (out_w, v_out), (up_w, v_up), (down_w, v_down))
            ]
        )
    l_g = copies.start(cotangent, v_g)
    bounds = bounds_of(lengths)
    same[...] = doc_mask(bounds, rows).astype(f32)
    tail = x1.shape[0] - rows
    which = lax.broadcasted_iota(jnp.int32, (tail, width), 0)
    note = jnp.zeros((tail, width), f32)
    for k, bound in enumerate(bounds):
        note = jnp.where(which == k, bound.astype(f32), note)
    v_x[...] = note.astype(bf16)
    copies.send(v_x, x1.at[pl.ds(rows, tail)])
    steps = table.shape[0]
    doc = lax.broadcasted_iota(jnp.int32, (16, steps), 0)
    wanted = jnp.full((16, steps), -1, jnp.int32)
    for k in range(docs):
        wanted = jnp.where(doc == k, timesteps[0, k], wanted)
    step = lax.broadcasted_iota(jnp.int32, (16, steps), 1)
    onehot = (step == wanted).astype(f32).astype(bf16)
    token = lax.broadcasted_iota(jnp.int32, (rows, 16), 0)
    own = sum((token >= bound).astype(jnp.int32) for bound in bounds)
    chosen = (own == lax.broadcasted_iota(jnp.int32, (rows, 16), 1)).astype(f32).astype(bf16)
    l_table.wait()
    embedded = mm(chosen, mm(onehot, v_table[...]).astype(bf16))
    v_h[0] = (inputs[...].astype(f32) + embedded).astype(bf16)
    for l in range(LAYERS):
        h_in, h_mid = v_h.at[2 * l], v_h.at[2 * l + 1]
        h_out = v_h.at[2 * l + 2]
        v_na[l] = norm_forward(h_in[...], a_gain[l : l + 1, :], a_shift[l : l + 1, :])
        loads[l][0].wait()
        qkv_forward(v_na[l], v_qkv.at[l], qv, slice(l, l + 1), v_mixed.at[l])
        copies.send(v_na.at[l], na.at[l])
        if l == 0:
            copies.send(v_mixed.at[l], mixed)
        attend_probs(v_mixed.at[l], same, v_probs)
        attend_context(v_mixed.at[l], v_probs, v_ctx.at[l])
        copies.send(v_ctx.at[l], ctx.at[l])
        loads[l][1].wait()

        def project(n):
            at = cols(n)
            out = h_in[:, at].astype(f32) + mm(v_ctx[l], v_out[l, :, at])
            h_mid[:, at] = (out + out_b[l : l + 1, at].astype(f32)).astype(bf16)

        loop(width // BLOCK, project)
        v_nm[l] = norm_forward(h_mid[...], m_gain[l : l + 1, :], m_shift[l : l + 1, :])
        copies.send(v_nm.at[l], (nm0, nm1)[l])
        loads[l][2].wait()

        def expand(n):
            at = cols(n)
            inner = mm(v_nm[l], v_up[l, :, at]) + up_b[l : l + 1, at].astype(f32)
            active, s = gelu_pair(inner)
            v_act[l, :, at] = active.astype(bf16)
            v_slope[l, :, at] = s.astype(bf16)

        loop(wide // BLOCK, expand)
        copies.send(v_act.at[l], (act0, act1)[l])
        if l == 0:
            copies.send(v_slope.at[l], slope)
        loads[l][3].wait()

        def contract(n):
            at = cols(n)
            out = h_mid[:, at].astype(f32) + mm(v_act[l], v_down[l, :, at])
            h_out[:, at] = (out + down_b[l : l + 1, at].astype(f32)).astype(bf16)

        loop(width // BLOCK, contract)
    for k, h in ((0, h0), (1, h1), (3, h3), (4, last)):
        copies.send(v_h.at[k], h)
    by_x = jnp.where(bits[0] == 0, 2, 0)
    copies.send(v_h.at[by_x], x1.at[pl.ds(0, rows)])
    l_g.wait()
    l = LAYERS - 1
    backward_part(
        l, copies, v_g, a_gain, m_gain, v_h.at[2 * l], v_h.at[2 * l + 1], v_mixed.at[l], v_slope.at[l],
        v_probs, (v_qkv.at[l], v_out.at[l], v_up.at[l], v_down.at[l]), lambda *name: None, vec,
        dinner, dmixed.at[l], v_dinner, v_dmixed, v_dctx, v_dn, v_gmid, v_gout,
    )
    copies.send(v_gmid, g3)
    copies.send(v_gout, g2)
    copies.finish()


def norm_backward(h, gain, dnormed, upstream, vec, at_gain, at_shift, target):
    width = h.shape[1]
    xhat, rstd = norm_stats(h[...])
    dn = dnormed[...]
    e = dn * gain.astype(f32)
    grad = (
        e - jnp.mean(e, axis=-1, keepdims=True) - xhat * jnp.mean(e * xhat, axis=-1, keepdims=True)
    ) * rstd
    target[...] = (upstream[...].astype(f32) + grad).astype(bf16)
    vec[:, at_gain : at_gain + width] = jnp.sum(dn * xhat, axis=0, keepdims=True)
    vec[:, at_shift : at_shift + width] = jnp.sum(dn, axis=0, keepdims=True)


def colsum(x):
    return jnp.sum(x.astype(f32), axis=0, keepdims=True)


def write_notes(me, timesteps, vectors, doc_sums, notes):
    _, _, shares, ahead, width = notes.shape
    docs = timesteps.shape[1]
    one = width // shares
    per = width // one
    for core, vec in enumerate(vectors):
        count = vec.shape[1] // width
        rows = [vec[:, k * width : (k + 1) * width] for k in range(count)]
        rows.append(jnp.zeros((ahead - count, width), f32))
        value = jnp.concatenate(rows, axis=0).astype(bf16)
        for s in range(shares):
            notes[core, 0, s] = value
    row = lax.broadcasted_iota(jnp.int32, (ahead, width), 0)
    lane = lax.broadcasted_iota(jnp.int32, (ahead, width), 1)
    docs_rows = notes_rows(shares, docs, width)
    marks = jnp.zeros((ahead, width), f32)
    sums = [jnp.zeros((ahead, width), f32) for _ in range(shares)]
    for k in range(docs):
        number = me * docs + k
        r, j = number // per, number % per
        step = timesteps[0, k]
        here = lane == j * docs_rows + r
        marks = jnp.where(here & (row == 0), (step // 32).astype(f32), marks)
        marks = jnp.where(here & (row == 1), (step % 32).astype(f32), marks)
        here = (row == r) & (lane >= j * one) & (lane < (j + 1) * one)
        wide = jnp.broadcast_to(doc_sums[k : k + 1, :], (8, width))
        for s in range(shares):
            turned = pltpu.roll(wide, lax.rem((j - s) * one + width, width), 1)
            turned = jnp.broadcast_to(turned[:1], (ahead, width))
            sums[s] = jnp.where(here, turned, sums[s])
    for s in range(shares):
        notes[0, 1, s] = sums[s].astype(bf16)
        notes[1, 1, s] = marks.astype(bf16)


def notes_rows(shares, docs, width):
    return 4 * shares * docs * (width // shares) // width


def backward_part(
    layer, copies, g, a_gain, m_gain, h_a, h_m, mixed, slope, probs, weights, wait, vec, dinner, dmixed,
    v_dinner, v_dmixed, v_dctx, v_dn, v_gmid, v_gout,
):
    v_qkv, v_out, v_up, v_down = weights
    rows, width = g.shape
    wide = v_up.shape[1]
    one_row = slice(layer, layer + 1)
    at_qv, at_mshift, at_downb, at_upb = 4 * width, 6 * width, 7 * width, 8 * width
    vec[:, at_downb : at_downb + width] = colsum(g[...])
    for n in range(wide // BLOCK):
        wait("down", n)
    wait("slope")
    for n in range(wide // BLOCK):
        at = cols(n)
        dact = mm_nt(g[...], v_down[at, :])
        di = (dact * slope[:, at].astype(f32)).astype(bf16)
        v_dinner[:, at] = di
        vec[:, at_upb + n * BLOCK : at_upb + (n + 1) * BLOCK] = colsum(di)
    copies.send(v_dinner, dinner)
    wait("up")
    v_dn[...] = mm_nt(v_dinner[...], v_up[...])
    wait("h_m")
    norm_backward(h_m, m_gain[one_row, :], v_dn, g, vec, 3 * width, at_mshift, v_gmid)
    vec[:, 2 * width : 3 * width] = colsum(v_gmid[...])
    wait("out")
    v_dctx[...] = mm_nt(v_gmid[...], v_out[...]).astype(bf16)
    attend_grad(mixed, probs, v_dctx, v_dmixed)
    copies.send(v_dmixed, dmixed)
    vec[:, at_qv : at_qv + width] = colsum(v_dmixed[:, :width])
    vec[:, at_qv + width : at_qv + 2 * width] = colsum(v_dmixed[:, 2 * width :])
    wait("qkv")
    v_dn[...] = mm_nt(v_dmixed[...], v_qkv[...])
    wait("h_a")
    norm_backward(h_a, a_gain[one_row, :], v_dn, v_gmid, vec, 0, width, v_gout)


def backward_kernel(
    bits, lengths, timesteps, a_gain, m_gain, vec_upper, g, g_upper, h_a, h_m, mixed, slope,
    qkv_w, out_w, up_w, down_w, _,
    dinner, dmixed, g_out, send, own, notes,
    v_qkv, v_out, v_up, v_down, v_g, v_ha, v_hm, v_mixed, v_slope, v_dinner, v_dctx, v_dmixed, v_dn,
    v_gmid, v_gout, v_trade, v_notes, vec, v_probs, v_touch, same, sems,
):
    copies = Copies(sems)
    rows, width = h_a.shape
    wide = up_w.shape[2]
    loads = {"mixed": copies.start(mixed, v_mixed), "g": copies.start(g, v_g)}
    for n in range(wide // BLOCK):
        loads["down", n] = copies.start(down_w.at[0, cols(n)], v_down.at[cols(n)])
    for name, source, target in (
        ("slope", slope, v_slope), ("up", up_w.at[0], v_up), ("h_m", h_m, v_hm), ("out", out_w.at[0], v_out),
        ("qkv", qkv_w.at[0], v_qkv), ("h_a", h_a, v_ha), ("g_upper", g_upper, v_trade.at[0]),
    ):
        loads[name] = copies.start(source, target)
    wait = lambda *name: loads[name if len(name) > 1 else name[0]].wait()
    v_touch[...] = jnp.zeros_like(v_touch)
    tile = (pl.ds(0, 16), pl.ds(0, 128))
    touched = [
        copies.start(v_touch, ref.at[tile])
        for ref in (g_out, send, own, notes.at[0, 0, 0], dinner, dmixed.at[0])
    ]
    same[...] = doc_mask(bounds_of(lengths), rows).astype(f32)
    wait("mixed")
    attend_probs(v_mixed, same, v_probs)
    wait("g")
    for copy in touched:
        copy.wait()
    backward_part(
        0, copies, v_g, a_gain, m_gain, v_ha, v_hm, v_mixed, v_slope, v_probs,
        (v_qkv, v_out, v_up, v_down), wait, vec, dinner, dmixed.at[0], v_dinner, v_dmixed, v_dctx,
        v_dn, v_gmid, v_gout,
    )
    copies.send(v_gout, g_out)
    v_trade[1] = v_gmid[...]
    wait("g_upper")
    copies.send(v_trade.at[bits[0]], send)
    copies.send(v_trade.at[1 - bits[0]], own)
    count = lengths.shape[1]
    doc = lax.broadcasted_iota(jnp.int32, (16, rows), 0)
    token = lax.broadcasted_iota(jnp.int32, (16, rows), 1)
    index = sum((token >= bound).astype(jnp.int32) for bound in bounds_of(lengths))
    onehot = ((index == doc) & (doc < count)).astype(f32).astype(bf16)
    doc_sums = mm(onehot, v_gout[...])
    write_notes(bits[3], timesteps, (vec, vec_upper), doc_sums, v_notes)
    copies.send(v_notes, notes)
    copies.finish()


def relative(bits, shard, places):
    z, x = shard // 2, lax.rem(shard, 2)
    return lax.rem(bits[5] - z + places, places), lax.rem(x + bits[0], 2)


def pick_layer(ref, layer, at=slice(None)):
    return jnp.where(layer == 0, ref[0:1, at].astype(f32), ref[1:2, at].astype(f32))


def feed_weight_kernel(
    layer, bits, h, g, own_g, own_act, own_nm, own_dinner, gain, shift, up_b, up_w, down_w, *rest
):
    *outs, v_up, v_down, v_nm, v_own, v_g, v_n, v_act, v_dinner, v_send, v_keep, sems = rest
    copies = Copies(sems)
    rows, width = h.shape
    wide = up_w.shape[2]
    quarter = width // 4
    side, core = bits[1], bits[2]
    one_row = slice(layer, layer + 1)
    l_nm = copies.start(own_nm, v_own)
    order = [2 * side + 1 - core, 2 * side + core, 2 - 2 * side, 3 - 2 * side]
    size = wide // 4
    loads = []
    for n, block in enumerate(order):
        at = pl.ds(pl.multiple_of(block * size, 128), size)
        load = [copies.start(up_w.at[layer, :, at], v_up.at[n])]
        if n < 2:
            load.append(copies.start(down_w.at[layer, at], v_down.at[n]))
        load.append(copies.start(own_act.at[:, at], v_act.at[n, pl.ds(0, rows)]))
        if n < 2:
            load.append(copies.start(own_dinner.at[:, at], v_dinner.at[n, pl.ds(0, rows)]))
        loads.append(load)
    normed = norm_forward(h[...], gain[one_row, :], shift[one_row, :])
    v_nm[...] = normed
    v_n[:, rows:] = normed.T
    for k in range(2):
        part = 2 * side + (1 - core if k == 0 else core)
        at = pl.ds(pl.multiple_of(part * quarter // 128 * 128, 128), 2 * 128)
        for ref, first in ((own_g, 0), (g, rows)):
            piece = ref[:, at].T
            shifted = jnp.where(part % 2 == 0, piece[:quarter].astype(f32), piece[256 - quarter :].astype(f32))
            v_g[k * quarter : (k + 1) * quarter, first : first + rows] = shifted.astype(bf16)
    l_nm.wait()
    v_n[:, :rows] = v_own[...].T
    flat = len(v_send.shape) == 2

    def feed(n, block):
        at = pl.ds(pl.multiple_of(block * size, 128), size)
        inner = mm(v_nm[...], v_up[n]) + up_b[one_row, at].astype(f32)
        active, slope = gelu_pair(inner)
        v_act[n, rows:] = active.astype(bf16)
        down = mm(v_g[...], v_act[n]).astype(bf16)
        for k, target in ((0, v_send), (1, v_keep)):
            half = down[k * quarter : (k + 1) * quarter]
            if flat:
                target[:quarter, at] = half
                continue
            places, _, _, one, _ = target.shape
            share = wide // (2 * places)
            for m in range(size // share):
                back, across = relative(bits, block * (size // share) + m, places)
                for p in range(quarter // one):
                    piece = half[p * one : (p + 1) * one, m * share : (m + 1) * share]
                    target[back, across, 0, :, p * share : (p + 1) * share] = piece
        if n < 2:
            dact = mm_nt(g[...], v_down[n])
            v_dinner[n, rows:] = (dact * slope).astype(bf16)
            up = mm(v_n[...], v_dinner[n]).astype(bf16)
            target = v_send if n == 0 else v_keep
            if flat:
                target[quarter:, :size] = up
                return
            places, _, _, one, _ = target.shape
            for m in range(2 * places):
                back, across = relative(bits, m, places)
                target[back, across, 1] = up[m * one : (m + 1) * one]

    def leave(n, block):
        if flat:
            return
        places = v_send.shape[0]
        count = 2 * places // 4
        for target, out in ((v_send, outs[-2]), (v_keep, outs[-1])):
            for m in range(count):
                back, across = relative(bits, block * count + m, places)
                copies.send(target.at[back, across, 0], out.at[back, across, 0])
        if n < 2:
            target, out = ((v_send, outs[-2]), (v_keep, outs[-1]))[n]
            copies.send(target.at[:, :, 1], out.at[:, :, 1])

    for group in ((0,), (1, 2, 3)):
        for n in group:
            for load in loads[n]:
                load.wait()
        for n in group:
            feed(n, order[n])
        for n in group:
            leave(n, order[n])
    if flat:
        copies.send(v_send, outs[-2])
        copies.send(v_keep, outs[-1])
    copies.finish()


def attend_weight_kernel(
    bits, hx, g, own_g, own_na, own_ctx, own_dmixed, notes, gain, shift, qv, qkv_w, out_w,
    send, keep,
    v_qkv, v_out, v_na, v_mixed, v_dctx, v_dmixed, v_ctx, v_left, v_right, v_own, v_own_ctx,
    v_own_dmixed, v_bias, v_send, v_keep, v_notes, v_probs, same, sems,
):
    copies = Copies(sems)
    rows, width = g.shape
    layer, core = bits[0], bits[2]
    l_out = copies.start(out_w.at[layer], v_out)
    l_qkv = copies.start(qkv_w.at[layer], v_qkv)
    l_ctx = copies.start(own_ctx.at[layer], v_own_ctx)
    l_own = copies.start(own_na.at[layer], v_own)
    l_dmixed = copies.start(own_dmixed.at[layer], v_own_dmixed)
    l_notes = copies.start(notes, v_notes)
    note = hx[rows:, :].astype(f32)
    bounds = [note[k : k + 1, :rows].astype(jnp.int32) for k in range(2)]
    same[...] = doc_mask(bounds, rows).astype(f32)
    v_bias[...] = pick_layer(qv, layer)
    v_na[...] = norm_forward(hx[:rows, :], pick_layer(gain, layer), pick_layer(shift, layer))
    l_out.wait()
    v_dctx[...] = mm_nt(g[...], v_out[...]).astype(bf16)
    l_qkv.wait()
    qkv_forward(v_na[...], v_qkv, v_bias, slice(0, 1), v_mixed)
    attend_probs(v_mixed, same, v_probs)
    attend_context(v_mixed, v_probs, v_ctx)
    attend_grad(v_mixed, v_probs, v_dctx, v_dmixed)
    part = width // 2
    shares, ahead = notes.shape[2], notes.shape[3]
    share = width // shares
    sides = [lax.rem(bits[1] + h, 2) for h in range(2)]
    places = [relative(bits, s, shares // 2) for s in range(shares)]

    def put(target, k, n, out):
        for s, (back, across) in enumerate(places):
            piece = out[s * share : (s + 1) * share].astype(bf16)
            target[sides[n // 2], back, across, ahead:, (n % 2) * part : (n % 2 + 1) * part] = piece

    l_notes.wait()
    for k in range(2):
        target = v_send if k == 0 else v_keep
        for h in range(2):
            for s, (back, across) in enumerate(places):
                target[sides[h], back, across, :ahead] = v_notes[1 - core if k == 0 else core, h, s]
    l_ctx.wait()
    v_left[:, :rows] = v_own_ctx[...].T
    v_left[:, rows:] = v_ctx[...].T
    for k in range(2):
        side = jnp.where(k == 0, 1 - core, core)
        at = pl.ds(pl.multiple_of(side * part, 128), part)
        v_right[k, :rows, :part] = own_g[:, at]
        v_right[k, rows:, :part] = g[:, at]
        put(v_send if k == 0 else v_keep, k, 0, mm(v_left[...], v_right[k, :, :part]))
    l_own.wait()
    l_dmixed.wait()
    v_left[:, :rows] = v_own[...].T
    v_left[:, rows:] = v_na[...].T
    for k in range(2):
        side = jnp.where(k == 0, 1 - core, core)
        target = v_send if k == 0 else v_keep
        at = pl.ds(pl.multiple_of(side * 3 * part, 128), 3 * part)
        v_right[k, :rows] = v_own_dmixed[:, at]
        v_right[k, rows:] = v_dmixed[:, at]
        out = mm(v_left[...], v_right[k])
        for n in range(1, 4):
            put(target, k, n, out[:, (n - 1) * part : n * part])
        copies.send(target, send if k == 0 else keep)
    copies.finish()


def feed_finish_kernel(layer, bits, own, other, beside, *rest):
    up_out, down_out, v_up, v_down, sems = rest[-5:]
    copies = Copies(sems)
    side, core = bits[1], bits[2]
    rows, width = own.shape[1:]
    share, quarter = v_down.shape[0], width // 4
    pieces = width // share
    for ref, chip, half in (
        (own, side, core), (other, 1 - side, core), (beside.at[0], side, 1 - core), (beside.at[1], 1 - side, 1 - core)
    ):
        part = 2 * chip + half
        v_up[:, pl.ds(pl.multiple_of(part * width, 128), width)] = ref[1].astype(f32)
        down = jnp.concatenate(
            [ref[0, :, p * share : (p + 1) * share].astype(f32) for p in range(pieces)], axis=0
        ).T
        for at in range(4):

            @pl.when(part == at)
            def _():
                v_down[:, at * quarter : (at + 1) * quarter] = down

    copies.send(v_up, up_out.at[layer])
    copies.send(v_down, down_out.at[layer])
    copies.finish()


def attend_finish_kernel(
    ahead, docs_rows, bits, own, other, beside,
    table, a_gain, a_shift, qkv, a_qv, out, a_out, m_gain, m_shift, m_up, m_down, notes, sums,
):
    place_x, side, core = bits[0], bits[1], bits[2]
    width = own.shape[2]
    part = width // 2

    def put(ref, first, which):
        for relative in range(2):
            layer = jnp.where(relative == 0, place_x, 1 - place_x)
            value = ref[relative, ahead:, :].astype(f32)
            base = 3 * part * which
            if first:
                out[layer, :, pl.ds(pl.multiple_of(which * part, 128), part)] = value[:, :part]
                qkv[layer, :, pl.ds(pl.multiple_of(base, 128), part)] = value[:, part:]
            else:
                qkv[layer, :, pl.ds(pl.multiple_of(base + part, 128), width)] = value

    def note(ref, which, half):
        notes[which, half] = ref[0, :ahead, :].astype(f32) + ref[1, :ahead, :].astype(f32)

    for half in range(2):
        for here, mine in ((own, 0), (other, 1)):

            @pl.when((side == half) == (mine == 0))
            def _():
                put(here, half == 0, core)
                put(beside.at[mine], half == 0, 1 - core)

                note(here, core, half)
                note(beside.at[mine], 1 - core, half)

    index = bits[4]
    one = a_gain.shape[1]
    for l in range(LAYERS):
        value = notes[l, 0]
        at = 0
        for ref in (a_gain, a_shift, a_out, m_gain, a_qv, m_shift, m_down, m_up):
            size = ref.shape[1]
            count = size // one
            place = index * size
            line = value[at : at + 1]
            for k in range(1, count):
                line = jnp.where(place // width == k, value[at + k : at + k + 1], line)
            line = jnp.broadcast_to(line, (8, width))
            turned = pltpu.roll(line, lax.rem(width - lax.rem(place, width), width), 1)
            ref[l : l + 1, :] = turned[:1, :size]
            at += count
    per, count = width // one, (width // one) * docs_rows
    high, low = notes[1, 1, 0:1, :count], notes[1, 1, 1:2, :count]
    steps = (high * 32.0 + low).astype(jnp.int32)
    for j in range(per):
        sums[j * docs_rows : (j + 1) * docs_rows, :] = notes[0, 1, :docs_rows, j * one : (j + 1) * one]
    step = lax.broadcasted_iota(jnp.int32, (table.shape[1], count), 0)
    onehot = (step == steps).astype(f32).astype(bf16)
    table[...] = mm_nt(sums[...].T.astype(bf16), onehot)


def call(kernel, operands, specs, outs, out_specs, scratch, copies, aliases=None, limit=LIMIT):
    return pl.pallas_call(
        kernel,
        out_shape=[jax.ShapeDtypeStruct(s, d) for s, d in outs],
        in_specs=specs,
        out_specs=out_specs,
        scratch_shapes=[pltpu.VMEM(s, d) for s, d in scratch]
        + [pltpu.SemaphoreType.DMA((copies,))] * (copies > 0),
        input_output_aliases=aliases or {},
        compiler_params=pltpu.CompilerParams(vmem_limit_bytes=limit),
        cost_estimate=pl.CostEstimate(flops=0, bytes_accessed=0, transcendentals=0),
    )(*operands)


def swap(x, axis, by):
    size = lax.axis_size(axis)
    return lax.ppermute(x, axis, [(i, i ^ by) for i in range(size)])


def plus(a, b):
    return (a.astype(f32) + b.astype(f32)).astype(bf16)


def after(x, *others):
    return lax.optimization_barrier((x,) + others)[0] if others else x


class Ring:
    def __init__(self, term, place_z, nx, nz):
        self.term, self.nx, self.nz = term, nx, nz
        if nz > 4:
            groups = [[z * nx + x for z in range(nz)] for x in range(nx)]
            held = jnp.stack([term(s) for s in range(nz)]).astype(bf16)
            held = jnp.take(held, (place_z - jnp.arange(nz)) % nz, axis=0)
            self.carry = lax.psum_scatter(held, "dp", scatter_dimension=0, axis_index_groups=groups)
            self.at = nz
        else:
            self.carry = term(1).astype(bf16)
            self.at = 1

    def step(self, *others):
        if self.at < self.nz:
            self.at += 1
            size = self.nx * self.nz
            got = lax.ppermute(self.carry, "dp", [(d, (d + self.nx) % size) for d in range(size)])
            got = after(got, *others)
            self.carry = (got.astype(f32) + self.term(self.at % self.nz)).astype(bf16)

    def finish(self, *others):
        while self.at < self.nz:
            self.step(*others)
        return self.carry


def plus(*parts):
    return sum(part.astype(f32) for part in parts)


def local(
    inputs,
    timesteps,
    lengths,
    cotangent,
    time_table,
    attn_norm_gain,
    attn_norm_bias,
    qkv_weight,
    qv_bias,
    out_weight,
    out_bias,
    mlp_norm_gain,
    mlp_norm_bias,
    up_weight,
    up_bias,
    down_weight,
    down_bias,
):
    place = lax.axis_index("section")
    side, core = place // 2, place % 2
    dp = lax.axis_size("dp")
    nx, nz = 2, dp // 2
    index = lax.axis_index("dp")
    place_z, place_x = index // nx, index % nx
    rows, width = inputs.shape
    wide = up_weight.shape[2]
    docs = lengths.shape[1]
    step_count = time_table.shape[0]
    me = index * lax.axis_size("section") + place
    bits = jnp.stack([place_x, side, core, me, index, place_z]).astype(jnp.int32)

    ahead, docs_rows = 16, notes_rows(dp, docs, width)
    tok, tok2 = (rows, width), (LAYERS, rows, width)
    peer_cot = swap(cotangent, "section", 2)
    one_wide = ((rows, wide), bf16)
    full, thrice = ((LAYERS, rows, wide), bf16), ((LAYERS, rows, 3 * width), bf16)
    x1, h0, h1, h3, last, na, mixed, ctx, nm0, nm1, act0, act1, slope, dinner1, dmixed, g2, g3, vec1 = call(
        forward_kernel,
        [bits, lengths, timesteps, inputs, attn_norm_gain, attn_norm_bias, qv_bias, out_bias,
         mlp_norm_gain, mlp_norm_bias, up_bias, down_bias, cotangent, time_table, qkv_weight, out_weight,
         up_weight, down_weight],
        [SMEM] * 3 + [VMEM] * 9 + [ANY] * 6,
        [((rows + 16, width), bf16)] + [(tok, bf16)] * 4
        + [(tok2, bf16), ((rows, 3 * width), bf16), (tok2, bf16), (tok, bf16), (tok, bf16), one_wide,
           one_wide, one_wide, one_wide, thrice, (tok, bf16), (tok, bf16), ((1, 12 * width), f32)],
        [ANY] * 17 + [VMEM],
        [(time_table.shape, bf16), (qkv_weight.shape, bf16), (out_weight.shape, bf16),
         (up_weight.shape, bf16), (down_weight.shape, bf16), ((2 * LAYERS + 1,) + tok, bf16),
         (tok2, bf16), thrice, (tok2, bf16), (tok2, bf16), full, full, ((16, width), bf16), (tok, bf16),
         ((rows, wide), bf16), (tok, bf16), ((rows, 3 * width), bf16), (tok, f32), (tok, bf16), (tok, bf16),
         ((width // HDIM, rows, rows), bf16), ((rows, rows), f32)],
        40,
    )
    peer_h3 = swap(h3, "section", 2)
    peer_h1 = swap(h1, "section", 2)
    peer_hx = swap(x1, "dp", 1)
    peer_g2 = swap(g2, "section", 2)
    dinner0, dmixed, g0, x2, own_ga, notes = call(
        backward_kernel,
        [bits, lengths, timesteps, attn_norm_gain, mlp_norm_gain, vec1, g2, g3, h0, h1, mixed, slope,
         qkv_weight, out_weight, up_weight, down_weight, dmixed],
        [SMEM] * 3 + [VMEM] * 3 + [ANY] * 11,
        [one_wide, thrice, (tok, bf16), (tok, bf16), (tok, bf16), ((2, 2, dp, ahead, width), bf16)],
        [ANY] * 6,
        [(qkv_weight.shape[1:], bf16), (out_weight.shape[1:], bf16), (up_weight.shape[1:], bf16),
         (down_weight.shape[1:], bf16), (tok, bf16), (tok, bf16), (tok, bf16), ((rows, 3 * width), bf16),
         ((rows, wide), bf16), ((rows, wide), bf16), (tok, bf16), ((rows, 3 * width), bf16), (tok, f32),
         (tok, bf16), (tok, bf16), ((2,) + tok, bf16), ((2, 2, dp, ahead, width), bf16),
         ((1, 12 * width), f32), ((width // HDIM, rows, rows), bf16), ((16, 128), bf16),
         ((rows, rows), f32)],
        32,
        {16: 1},
    )
    peer_ga = swap(x2, "dp", 1)

    share, one, half, quarter = wide // dp, width // dp, width // 2, width // 4
    flat = share % 128 != 0

    def feed_weight(layer, h, g, own_g):
        shape = (quarter + width, wide) if flat else (nz, nx, 2, one, width)
        send, keep = call(
            functools.partial(feed_weight_kernel, layer),
            [bits, h, g, own_g, (act0, act1)[layer], (nm0, nm1)[layer], (dinner0, dinner1)[layer], mlp_norm_gain, mlp_norm_bias, up_bias, up_weight,
             down_weight],
            [SMEM, VMEM, VMEM, VMEM, HBM, HBM, HBM, VMEM, VMEM, VMEM, HBM, HBM],
            [(shape, bf16)] * 2,
            [HBM] * 2,
            [((4, width, wide // 4), bf16), ((2, wide // 4, width), bf16), (tok, bf16), (tok, bf16),
             ((2 * quarter, 2 * rows), bf16), ((width, 2 * rows), bf16),
             ((4, 2 * rows, wide // 4), bf16), ((2, 2 * rows, wide // 4), bf16),
             (shape, bf16), (shape, bf16)],
            40,
            limit=MIDDLE,
        )
        if flat:

            def sort(x):
                down = x[:quarter].reshape(-1, one, dp, share).transpose(2, 1, 0, 3)
                both = jnp.stack([down.reshape(dp, one, width), x[quarter:, :width].reshape(dp, one, width)], axis=1)
                both = jnp.take(both.reshape(nz, nx, 2, one, width), (place_z - jnp.arange(nz)) % nz, axis=0)
                return jnp.where(place_x == 0, both, both[:, ::-1])

            send, keep = sort(send), sort(keep)
        return keep, send

    def trade(keep, send, *others):
        return keep, swap(after(send, *others), "section", 1)

    keep1, send1 = feed_weight(1, peer_h3, peer_cot, after(cotangent, g0, peer_hx))
    keep1, near1 = trade(keep1, send1, peer_ga, peer_h1, peer_g2)
    ring1 = Ring(lambda s: plus(keep1[s], near1[s]), place_z, nx, nz)

    at_send, at_keep = call(
        attend_weight_kernel,
        [bits, after(peer_hx, ring1.carry), peer_ga, own_ga, na, ctx, dmixed, notes, attn_norm_gain, attn_norm_bias,
         qv_bias, qkv_weight, out_weight],
        [SMEM, VMEM, VMEM, VMEM, HBM, HBM, HBM, HBM, VMEM, VMEM, VMEM, HBM, HBM],
        [((2, nz, nx, ahead + one, width), bf16)] * 2,
        [HBM] * 2,
        [((width, 3 * width), bf16), ((width, width), bf16), (tok, bf16), ((rows, 3 * width), bf16),
         (tok, bf16), ((rows, 3 * width), bf16), (tok, bf16), ((width, 2 * rows), bf16),
         ((2, 2 * rows, 3 * half), bf16), (tok, bf16), (tok, bf16), ((rows, 3 * width), bf16),
         ((1, 2 * width), f32), ((2, nz, nx, ahead + one, width), bf16),
         ((2, nz, nx, ahead + one, width), bf16), ((2, 2, dp, ahead, width), bf16),
         ((width // HDIM, rows, rows), bf16), ((rows, rows), f32)],
        8,
        limit=MIDDLE,
    )

    ring1.step(at_keep)
    order = [s % nz for s in range(1, nz + 1)]
    keep_a, near_a = trade(at_keep, at_send, ring1.carry)
    away_a = {s: plus(keep_a[1, s], near_a[1, s]).astype(bf16) for s in order}
    far_a = {s: swap(away_a[s], "section", 2) for s in order}
    keep0, send0 = feed_weight(0, after(peer_h1, ring1.carry, *away_a.values()), peer_g2, g2)
    ring1.step(keep0)
    far_a[1] = after(far_a[1], ring1.carry)
    ring_a = Ring(lambda s: plus(keep_a[0, s], near_a[0, s], far_a[s]), place_z, nx, nz)
    keep0, near0 = trade(keep0, send0, ring_a.carry)
    away0 = {s: plus(keep0[s, 1], near0[s, 1]).astype(bf16) for s in order}
    far0 = {s: swap(away0[s], "dp", 1) for s in order}
    ring0 = Ring(lambda s: plus(keep0[s, 0], near0[s, 0], far0[s]), place_z, nx, nz)
    ring_a.step(*away0.values())
    both = ring1.finish(ring0.carry, ring_a.carry)
    own1 = plus(both[0], swap(both[1], "dp", 1)).astype(bf16)
    ring_a.step(both)
    ring0.step(both)

    def finish(kernel, own, outs, out_specs, scratch, copies=0, more=(), aliases=None, others=()):
        other = after(swap(own, "section", 2), *others)
        beside = swap(jnp.stack([own, other]), "section", 1)
        return call(kernel, [bits, own, other, beside] + list(more),
                    [SMEM] + [VMEM] * 3 + [ANY] * len(more), outs, out_specs, scratch, copies, aliases, SMALL)

    def feed_finish(layer, own, more=(), others=()):
        return finish(
            functools.partial(feed_finish_kernel, layer), own,
            [((LAYERS, one, wide), f32), ((LAYERS, share, width), f32)], [ANY] * 2,
            [((one, wide), f32), ((share, width), f32)], 2, more, {4: 0, 5: 1} if more else None, others,
        )

    grads = feed_finish(1, own1)
    both = ring_a.finish(own1)
    ring0.step(own1)
    own = jnp.stack([both[0], swap(both[1], "dp", 1)])
    grad_up, grad_down = feed_finish(0, ring0.finish(*grads), grads)
    pair = lambda n: ((LAYERS, n), f32)
    (grad_table, a_gain, a_shift, grad_qkv, a_qv, grad_out, a_out, m_gain, m_shift, m_up, m_down) = finish(
        functools.partial(attend_finish_kernel, ahead, docs_rows),
        own,
        [((one, step_count), f32), pair(one), pair(one), ((LAYERS, one, 3 * width), f32), pair(2 * one),
         ((LAYERS, one, width), f32), pair(one), pair(one), pair(one), pair(share), pair(one)],
        [VMEM] * 11,
        [((2, 2, ahead, width), f32), ((width // one * docs_rows, one), f32)],
    )

    return (
        last,
        g0,
        grad_table.T,
        a_gain,
        a_shift,
        grad_qkv,
        a_qv,
        grad_out,
        a_out,
        m_gain,
        m_shift,
        grad_up,
        m_up,
        grad_down,
        m_down,
    )


def solution(mesh):
    rows = P(("dp", "section"), None)
    in_specs = (rows,) * 4 + (P(),) * 13
    flat, deep = P(None, "dp"), P(None, "dp", None)
    out_specs = (rows, rows) + (flat, flat, flat, deep, flat, deep, flat, flat, flat, deep, flat, deep, flat)
    return jax.shard_map(local, mesh=mesh, in_specs=in_specs, out_specs=out_specs, check_vma=False)
```
